32 devices in a mesh: img: 4 (over y, core), cell: 8 (over z, x).
Axes of the slice: x: 2, y: 2, z: 4, core: 2. Of those that a mesh axis runs over, the one named last changes fastest.
Arguments:
- attributes: float32 [59, 262144], P(None, ('img', 'cell')), may hold values from -5 to 2, as said below
- camera: float32 [3, 3], replicated, may hold values from -6 to 5, as said below
- target: float32 [3, 128, 2048], P(None, 'img', 'cell'), may hold values from 0 to 1
- visible_index: int32 [32, 2048], P(('img', 'cell')), may hold values from 0 to 8191
- tile_lists: int32 [8, 128, 128], P('img', 'cell'), may hold values from 0 to 2047
- tile_len: int32 [8, 128], P('img', 'cell'), may hold values from 16 to 128
Outputs:
- gradient: float32 [59, 262144], P(None, ('img', 'cell'))
The draws below stay inside these ranges and needn't reach their ends.
Inputs may be any that keep to these rules, and one draw needn't show every extreme that they name: `attributes`: rows 0 to 2 (positions) lie within [-1, 1]. `camera`: row 2, the eye, lies 4 or more from the anchor.
All inputs are finite; a program needn't handle non-finite values.
Results may differ from the reference program's by a relative error of at most 0.0003.
Values sent between devices are 32-bit elements; how exact they have to be, the bound alone decides.
No kernel may reach another device: no remote copies, remote signals or barrier semaphores. Data moves between devices by JAX's collectives and lax.ppermute only.
A program may use at most 64 MiB of HBM per device.

```python
import math
import jax
import jax.numpy as jnp
from jax import lax

TILE = 16
LIST = 128
PH = 32
PW = 256
G_DEV = 8192
CAP = 64
H = 128
W = 2048
TY = 8
TX = 128
GAUSS = 262144
VIS = 2048
N_CELL = 8
DEVICES = 32


def draw_attributes(key, part):
    subkeys = jax.random.split(jax.random.fold_in(key, 11), 5)
    positions = jax.random.uniform(subkeys[0], (3, GAUSS), jnp.float32, -1.0, 1.0)
    rotations = jax.random.uniform(subkeys[2], (4, GAUSS), jnp.float32, -2.0, 2.0)
    opacity = jax.random.uniform(subkeys[3], (1, GAUSS), jnp.float32, -4.5, -1.5)
    log_scale = jax.random.uniform(subkeys[1], (3, GAUSS), jnp.float32, -1.2, 0.2)
    harmonics = jax.random.uniform(subkeys[4], (48, GAUSS), jnp.float32, -0.6, 0.6)
    return jnp.concatenate([positions, log_scale, rotations, opacity, harmonics])


def draw_camera(key, part):
    subkeys = jax.random.split(jax.random.fold_in(key, 23), 2)
    projection = jax.random.uniform(subkeys[0], (2, 3), jnp.float32, -5.0, 5.0)
    viewer = jnp.array([0.0, 0.0, -5.0], jnp.float32) + jax.random.uniform(subkeys[1], (3,), jnp.float32, -1.0, 1.0)
    return jnp.concatenate([projection, viewer[None, :]])


def set_ends(values, rng, low, high):
    place = [jax.random.randint(jax.random.fold_in(rng, axis), (), 0, length) for axis, length in enumerate(values.shape)]
    main_axis = values.shape.index(max(values.shape))
    neighbour = place[:main_axis] + [(place[main_axis] + 1) % values.shape[main_axis]] + place[main_axis + 1:]
    return values.at[tuple(place)].set(low).at[tuple(neighbour)].set(high)


def block_levels(stream_key, shape, shards, least, top_value):
    loudness, own = 1.0, jax.random.fold_in(stream_key, 6)
    for dim, parts in shards:
        draws = jnp.exp(jax.random.uniform(jax.random.fold_in(own, dim), (parts,), jnp.float32, least / len(shards), top_value / len(shards)))
        loudness = loudness * jnp.repeat(draws, shape[dim] // parts).reshape([-1 if axis == dim else 1 for axis in range(len(shape))])
    return loudness


def setup_inputs(seed: int = 0) -> dict:
    splits = jax.random.split(jax.random.key(seed), 7)
    attributes = draw_attributes(jax.random.fold_in(splits[6], 71), 0)
    camera = draw_camera(jax.random.fold_in(splits[6], 71), 0)
    target = jnp.clip(1.0 * jax.random.uniform(splits[2], (3, H, W), jnp.float32) ** block_levels(splits[2], (3, H, W), ((1, 4), (2, 8)), -0.2, 0.2), 0.0, 1.0)
    visible_index = set_ends(jax.random.randint(splits[3], (DEVICES, VIS), 0, G_DEV), jax.random.fold_in(splits[3], 1), 0, G_DEV - 1).astype(jnp.int32)
    tile_lists = set_ends(jax.random.randint(splits[4], (TY, TX, LIST), 0, VIS), jax.random.fold_in(splits[4], 1), 0, VIS - 1).astype(jnp.int32)
    tile_len = set_ends(jax.random.randint(splits[5], (TY, TX), LIST // 8, LIST + 1), jax.random.fold_in(splits[5], 1), LIST // 8, LIST).astype(jnp.int32)
    return {"attributes": attributes, "camera": camera, "target": target, "visible_index": visible_index, "tile_lists": tile_lists, "tile_len": tile_len}


WEIGHT_SSIM = 0.2
SMOOTHING = 0.01
STAB_ONE = 0.0001
STAB_TWO = 0.0009
BLUR_SIGMA = 1.5
SH_ZERO = 0.28209479177387814
SH_ONE = 0.4886025119029199
SH_TWO = (1.0925484305920792, -1.0925484305920792, 0.31539156525252005, -1.0925484305920792, 0.5462742152960396)
SH_THREE = (-0.5900435899266435, 2.890611442640554, -0.4570457994644658, 0.3731763325901154, -0.4570457994644658, 1.445305721320277, -0.5900435899266435)

def harmonic_basis(unit_x, unit_y, unit_z):
    unit_xx = unit_x * unit_x
    unit_yy = unit_y * unit_y
    unit_zz = unit_z * unit_z
    return [SH_ZERO + 0.0 * unit_x, -SH_ONE * unit_y, SH_ONE * unit_z, -SH_ONE * unit_x, SH_TWO[0] * unit_x * unit_y, SH_TWO[1] * unit_y * unit_z, SH_TWO[2] * (2.0 * unit_zz - unit_xx - unit_yy), SH_TWO[3] * unit_x * unit_z, SH_TWO[4] * (unit_xx - unit_yy), SH_THREE[0] * unit_y * (3.0 * unit_xx - unit_yy), SH_THREE[1] * unit_x * unit_y * unit_z, SH_THREE[2] * unit_y * (4.0 * unit_zz - unit_xx - unit_yy), SH_THREE[3] * unit_z * (2.0 * unit_zz - 3.0 * unit_xx - 3.0 * unit_yy), SH_THREE[4] * unit_x * (4.0 * unit_zz - unit_xx - unit_yy), SH_THREE[5] * unit_z * (unit_xx - unit_yy), SH_THREE[6] * unit_x * (unit_xx - 3.0 * unit_yy)]

def project_rows(attr_rows, camera):
    positions = [attr_rows[number] for number in range(3)]
    scales = [jnp.exp(attr_rows[3 + number]) for number in range(3)]
    quat_w = 1.5 + jnp.tanh(attr_rows[6])
    quat_x = attr_rows[7]
    quat_y = attr_rows[8]
    quat_z = attr_rows[9]
    length = jnp.sqrt(quat_w * quat_w + quat_x * quat_x + quat_y * quat_y + quat_z * quat_z)
    quat_w, quat_x, quat_y, quat_z = (quat_w / length, quat_x / length, quat_y / length, quat_z / length)
    rotation = [[1.0 - 2.0 * (quat_y * quat_y + quat_z * quat_z), 2.0 * (quat_x * quat_y - quat_w * quat_z), 2.0 * (quat_x * quat_z + quat_w * quat_y)], [2.0 * (quat_x * quat_y + quat_w * quat_z), 1.0 - 2.0 * (quat_x * quat_x + quat_z * quat_z), 2.0 * (quat_y * quat_z - quat_w * quat_x)], [2.0 * (quat_x * quat_z - quat_w * quat_y), 2.0 * (quat_y * quat_z + quat_w * quat_x), 1.0 - 2.0 * (quat_x * quat_x + quat_y * quat_y)]]
    screen_axes = [[sum((camera[screen_axis, world_axis] * rotation[world_axis][scale_axis] for world_axis in range(3))) * scales[scale_axis] for scale_axis in range(3)] for screen_axis in range(2)]
    cov_first = sum((screen_axes[0][scale_axis] * screen_axes[0][scale_axis] for scale_axis in range(3))) + 0.3
    cov_mixed = sum((screen_axes[0][scale_axis] * screen_axes[1][scale_axis] for scale_axis in range(3)))
    cov_second = sum((screen_axes[1][scale_axis] * screen_axes[1][scale_axis] for scale_axis in range(3))) + 0.3
    determinant = cov_first * cov_second - cov_mixed * cov_mixed
    centers = [8.0 + 7.0 * jnp.sin(sum((camera[screen_axis, world_axis] * positions[world_axis] for world_axis in range(3))) / 3.0) for screen_axis in range(2)]
    offsets = [positions[world_axis] - camera[2, world_axis] for world_axis in range(3)]
    distance = jnp.sqrt(offsets[0] * offsets[0] + offsets[1] * offsets[1] + offsets[2] * offsets[2])
    basis = harmonic_basis(offsets[0] / distance, offsets[1] / distance, offsets[2] / distance)
    harmonics = attr_rows[11:].reshape((3, 16) + attr_rows.shape[1:])
    colours = [0.5 + sum((basis[term] * harmonics[channel, term] for term in range(16))) for channel in range(3)]
    opacity = jax.nn.sigmoid(attr_rows[10])
    return jnp.stack(centers + [cov_second / determinant, -cov_mixed / determinant, cov_first / determinant, opacity] + colours)

def render_block(tile_feats, live_mask):
    pixels = jnp.arange(TILE * TILE, dtype=jnp.int32)
    pixel_x = (pixels % TILE).astype(jnp.float32) + 0.5
    pixel_y = (pixels // TILE).astype(jnp.float32) + 0.5
    delta_x = pixel_x[None, None, :] - tile_feats[0][:, :, None]
    delta_y = pixel_y[None, None, :] - tile_feats[1][:, :, None]
    exponent = -0.5 * (tile_feats[2][:, :, None] * delta_x * delta_x + 2.0 * tile_feats[3][:, :, None] * delta_x * delta_y + tile_feats[4][:, :, None] * delta_y * delta_y)
    opacity_map = (live_mask * tile_feats[5])[:, :, None] * jnp.exp(exponent)
    log_keep = jnp.log1p(-opacity_map)
    before = jnp.cumsum(log_keep, axis=1) - log_keep
    weight = jnp.exp(before) * opacity_map
    return jnp.einsum('cbk,bkp->cbp', tile_feats[6:9], weight, precision=lax.Precision.HIGHEST)

def render_pair(block_pair):
    return render_block(block_pair[0], block_pair[1])

def blur_taps():
    offsets = jnp.arange(11, dtype=jnp.float32) - 5.0
    taps = jnp.exp(-offsets * offsets / (2.0 * BLUR_SIGMA * BLUR_SIGMA))
    return taps / jnp.sum(taps)

def blur_image(image):
    taps = blur_taps()
    height = image.shape[1]
    breadth = image.shape[2]
    padded = jnp.pad(image, ((0, 0), (5, 5), (5, 5)))
    rows_done = sum((taps[offset] * padded[:, offset:offset + height, :] for offset in range(11)))
    return sum((taps[offset] * rows_done[:, :, offset:offset + breadth] for offset in range(11)))

def ssim_value(mean_render, mean_target, square_render, square_target, cross_term):
    spread_render = square_render - mean_render * mean_render
    spread_target = square_target - mean_target * mean_target
    covariance = cross_term - mean_render * mean_target
    upper = (2.0 * mean_render * mean_target + STAB_ONE) * (2.0 * covariance + STAB_TWO)
    lower = (mean_render * mean_render + mean_target * mean_target + STAB_ONE) * (spread_render + spread_target + STAB_TWO)
    return upper / lower

def image_loss(image, target):
    filtered = blur_image(jnp.concatenate([image, target, image * image, target * target, image * target]))
    mean_render, mean_target, square_render, square_target, cross_term = jnp.split(filtered, 5)
    similarity = ssim_value(mean_render, mean_target, square_render, square_target, cross_term)
    difference = image - target
    return jnp.sum((1.0 - WEIGHT_SSIM) * jnp.sqrt(difference * difference + SMOOTHING * SMOOTHING) + WEIGHT_SSIM * (1.0 - similarity))

def reference(attributes, camera, target, visible_index, tile_lists, tile_len):
    owner_of = jnp.arange(VIS, dtype=jnp.int32) // CAP
    global_ids = (owner_of[None, :] * G_DEV + visible_index).reshape(-1).astype(jnp.int32)
    tiles_down = PH // TILE
    tiles_across = PW // TILE
    tile_group = ((jnp.arange(TY, dtype=jnp.int32) // tiles_down)[:, None] * N_CELL + (jnp.arange(TX, dtype=jnp.int32) // tiles_across)[None, :]).astype(jnp.int32)
    entry_ids = (tile_group[:, :, None] * VIS + tile_lists).reshape(TY * TX, LIST).astype(jnp.int32)
    live_mask = (jnp.arange(LIST, dtype=jnp.int32)[None, None, :] < tile_len[:, :, None]).astype(jnp.float32).reshape(TY * TX, LIST)
    tile_count = TY * TX
    block_size = math.gcd(tile_count, 64)
    block_total = tile_count // block_size

    def total_loss(attr_all):
        visible_rows = jnp.take(attr_all, global_ids, axis=1)
        features = project_rows(visible_rows, camera)
        tile_feats = jnp.take(features, entry_ids, axis=1)
        grouped = tile_feats.reshape(9, block_total, block_size, LIST).transpose(1, 0, 2, 3)
        masks = live_mask.reshape(block_total, block_size, LIST)
        rendered = lax.map(jax.checkpoint(render_pair), (grouped, masks))
        image = rendered.transpose(1, 0, 2, 3).reshape(3, TY, TX, TILE, TILE).transpose(0, 1, 3, 2, 4).reshape(3, H, W)
        return image_loss(image, target)
    return jax.grad(total_loss)(attributes)
```

```python
import functools
import math

import jax
import jax.numpy as jnp
import numpy as np
from jax import lax
from jax.experimental import pallas as pl
from jax.experimental.pallas import tpu as pltpu
from jax.sharding import PartitionSpec as P

TILE = 16
LANES = 128
SUBS = 8
GROUP = 8
RIM = 5
HALO = 16
WEIGHT_SSIM = 0.2
SMOOTHING = 0.01
STAB_ONE = 0.0001
STAB_TWO = 0.0009
BLUR_SIGMA = 1.5
LOG2E = 1.4426950408889634
SH_ZERO = 0.28209479177387814
SH_ONE = 0.4886025119029199
SH_TWO = (
    1.0925484305920792,
    -1.0925484305920792,
    0.31539156525252005,
    -1.0925484305920792,
    0.5462742152960396,
)
SH_THREE = (
    -0.5900435899266435,
    2.890611442640554,
    -0.4570457994644658,
    0.3731763325901154,
    -0.4570457994644658,
    1.445305721320277,
    -0.5900435899266435,
)
F32 = jnp.float32
BF16 = jnp.bfloat16
JAC_ROWS = 51
VMEM_BYTES = 56 * 1024 * 1024


def harmonic_basis(unit_x, unit_y, unit_z):
    unit_xx = unit_x * unit_x
    unit_yy = unit_y * unit_y
    unit_zz = unit_z * unit_z
    return [
        -SH_ONE * unit_y,
        SH_ONE * unit_z,
        -SH_ONE * unit_x,
        SH_TWO[0] * unit_x * unit_y,
        SH_TWO[1] * unit_y * unit_z,
        SH_TWO[2] * (2.0 * unit_zz - unit_xx - unit_yy),
        SH_TWO[3] * unit_x * unit_z,
        SH_TWO[4] * (unit_xx - unit_yy),
        SH_THREE[0] * unit_y * (3.0 * unit_xx - unit_yy),
        SH_THREE[1] * unit_x * unit_y * unit_z,
        SH_THREE[2] * unit_y * (4.0 * unit_zz - unit_xx - unit_yy),
        SH_THREE[3] * unit_z * (2.0 * unit_zz - 3.0 * unit_xx - 3.0 * unit_yy),
        SH_THREE[4] * unit_x * (4.0 * unit_zz - unit_xx - unit_yy),
        SH_THREE[5] * unit_z * (unit_xx - unit_yy),
        SH_THREE[6] * unit_x * (unit_xx - 3.0 * unit_yy),
    ]


def three_pieces(value):
    first = value.astype(BF16)
    rest = value - first.astype(F32)
    second = rest.astype(BF16)
    third = (rest - second.astype(F32)).astype(BF16)
    return first, second, third


def two_pieces(value):
    first = value.astype(BF16)
    return first, (value - first.astype(F32)).astype(BF16)


def dot(left, right):
    return jnp.dot(left, right, preferred_element_type=F32)


def dot_nt(left, right):
    return lax.dot_general(left, right, (((1,), (1,)), ((), ())), preferred_element_type=F32)


def dot_full(left, right):
    return jnp.dot(left, right, preferred_element_type=F32, precision=lax.Precision.HIGHEST)


def iota(shape, dim):
    return lax.broadcasted_iota(jnp.int32, shape, dim)


def block_transpose(block):
    turn = (iota(block.shape, 0) - iota(block.shape, 1) // TILE) & (SUBS - 1)
    out = block
    for step in range(1, SUBS):
        moved = pltpu.roll(block, LANES - TILE * step, 1)
        moved = pltpu.roll(moved, step, 0)
        out = jnp.where(turn == step, moved, out)
    return out


def covariance(scale_rows, quat_rows, cam):
    scales = [jnp.exp(row) for row in scale_rows]
    quat_w = 1.5 + jnp.tanh(quat_rows[0])
    quat_x, quat_y, quat_z = quat_rows[1:]
    inverse = lax.rsqrt(quat_w * quat_w + quat_x * quat_x + quat_y * quat_y + quat_z * quat_z)
    quat_w, quat_x, quat_y, quat_z = (
        quat_w * inverse,
        quat_x * inverse,
        quat_y * inverse,
        quat_z * inverse,
    )
    rotation = [
        [
            1.0 - 2.0 * (quat_y * quat_y + quat_z * quat_z),
            2.0 * (quat_x * quat_y - quat_w * quat_z),
            2.0 * (quat_x * quat_z + quat_w * quat_y),
        ],
        [
            2.0 * (quat_x * quat_y + quat_w * quat_z),
            1.0 - 2.0 * (quat_x * quat_x + quat_z * quat_z),
            2.0 * (quat_y * quat_z - quat_w * quat_x),
        ],
        [
            2.0 * (quat_x * quat_z - quat_w * quat_y),
            2.0 * (quat_y * quat_z + quat_w * quat_x),
            1.0 - 2.0 * (quat_x * quat_x + quat_y * quat_y),
        ],
    ]
    axes = [
        [
            (
                cam[screen][0] * rotation[0][axis]
                + cam[screen][1] * rotation[1][axis]
                + cam[screen][2] * rotation[2][axis]
            )
            * scales[axis]
            for axis in range(3)
        ]
        for screen in range(2)
    ]
    first = axes[0][0] * axes[0][0] + axes[0][1] * axes[0][1] + axes[0][2] * axes[0][2] + 0.3
    mixed = axes[0][0] * axes[1][0] + axes[0][1] * axes[1][1] + axes[0][2] * axes[1][2]
    second = axes[1][0] * axes[1][0] + axes[1][1] * axes[1][1] + axes[1][2] * axes[1][2] + 0.3
    return first, mixed, second


def owner_kernel(attr_ref, cam_ref, table_ref, jac_ref, pack_ref, feat_ref):
    count, own = attr_ref.shape
    high = own // LANES
    cam = [[cam_ref[row, col] for col in range(3)] for row in range(3)]
    for first in range(0, count, SUBS):
        number = min(SUBS, count - first)
        for place in range(high):
            pack_ref[pl.ds(first * high + place, number, stride=high), :] = attr_ref[
                first : first + number, place * LANES : (place + 1) * LANES
            ]

    def block(index, carry):
        start = pl.multiple_of(index * SUBS, SUBS)

        def row(number):
            return pack_ref[pl.ds(number * high + start, SUBS), :]

        positions = [row(number) for number in range(3)]
        shape_rows = [row(3 + number) for number in range(7)]
        jac = []
        (cov_first, cov_mixed, cov_second), pull = jax.vjp(
            lambda *rows: covariance(rows[:3], rows[3:], cam), *shape_rows
        )
        one = jnp.ones_like(cov_first)
        zero = jnp.zeros_like(cov_first)
        jac += pull((one, zero, zero))
        jac += pull((zero, one, zero))
        jac += pull((zero, zero, one))
        inverse = 1.0 / (cov_first * cov_second - cov_mixed * cov_mixed)
        conic = [cov_second * inverse, -cov_mixed * inverse, cov_first * inverse]
        centers = []
        slopes = []
        for screen in range(2):
            angle = (
                cam[screen][0] * positions[0]
                + cam[screen][1] * positions[1]
                + cam[screen][2] * positions[2]
            ) / 3.0
            centers.append(7.0 * jnp.sin(angle))
            slopes.append((7.0 / 3.0) * jnp.cos(angle))
        raw = row(10)
        decay = jnp.exp(-raw)
        log_opacity = -jnp.log(1.0 + decay)
        harmonics = [[row(11 + 16 * channel + term) for term in range(16)] for channel in range(3)]

        def colours_of(pos_x, pos_y, pos_z):
            off_x = pos_x - cam[2][0]
            off_y = pos_y - cam[2][1]
            off_z = pos_z - cam[2][2]
            scale = lax.rsqrt(off_x * off_x + off_y * off_y + off_z * off_z)
            basis = harmonic_basis(off_x * scale, off_y * scale, off_z * scale)
            colours = []
            for channel in range(3):
                total = 0.5 + SH_ZERO * harmonics[channel][0]
                for term in range(1, 16):
                    total = total + basis[term - 1] * harmonics[channel][term]
                colours.append(total)
            return tuple(colours), basis

        colours, pull_colours, basis = jax.vjp(colours_of, *positions, has_aux=True)
        jac += pull_colours((one, zero, zero))
        jac += pull_colours((zero, one, zero))
        jac += pull_colours((zero, zero, one))
        jac += slopes
        jac.append(decay / (1.0 + decay))
        jac += basis
        jac += conic
        for number, value in enumerate(jac):
            jac_ref[pl.ds(number * high + start, SUBS), :] = value
        features = centers + conic + [log_opacity] + list(colours)
        for number in range(SUBS):
            feat_ref[pl.ds(start * SUBS + number, SUBS, stride=SUBS), :] = features[number]
        feat_ref[pl.ds(high * SUBS + start, SUBS), :] = features[SUBS]
        return carry

    lax.fori_loop(0, high // SUBS, block, 0)
    for number, piece in enumerate(three_pieces(feat_ref[...])):
        table_ref[:, number * LANES : (number + 1) * LANES] = piece


def fill_numbers(got_ref, row_ref):
    lane_low = iota((1, LANES), 1) < LANES // 2
    for pair in range(got_ref.shape[0] // 2):
        row_ref[:, pair * LANES : (pair + 1) * LANES] = jnp.where(
            lane_low, got_ref[2 * pair : 2 * pair + 1, :], got_ref[2 * pair + 1 : 2 * pair + 2, :]
        )


def reply_kernel(table_ref, got_ref, out_ref, row_ref, wide_ref):
    devices = got_ref.shape[0]
    high = table_ref.shape[0] // (SUBS + 1)
    chunk = 2 * LANES
    half = LANES // 2
    fill_numbers(got_ref, row_ref)

    def step(index, carry):
        numbers = row_ref[:, pl.ds(pl.multiple_of(index * chunk, chunk), chunk)]
        low = numbers & (LANES - 1)
        top = numbers >> 7
        hot = jnp.where(iota((LANES, chunk), 0) == low, 1.0, 0.0).astype(BF16)
        wide_ref[...] = dot(
            table_ref[:, : 2 * LANES], jnp.concatenate([hot, hot], axis=0)
        ) + dot(table_ref[:, 2 * LANES :], hot)
        spread = jnp.broadcast_to(top, (SUBS, chunk))
        picked = jnp.zeros((SUBS, chunk), F32)
        for place in range(high):
            picked = jnp.where(spread == place, wide_ref[place * SUBS : (place + 1) * SUBS, :], picked)
        last = jnp.sum(
            jnp.where(iota((high, chunk), 0) == top, wide_ref[high * SUBS :, :], 0.0),
            axis=0,
            keepdims=True,
        )
        lane_low = iota((SUBS, LANES), 1) < half
        for part in range(chunk // LANES):
            eight = picked[:, part * LANES : (part + 1) * LANES]
            ninth = jnp.broadcast_to(last[:, part * LANES : (part + 1) * LANES], (SUBS, LANES))
            peer = index * 4 + part * 2
            out_ref[peer] = jnp.where(lane_low, eight, pltpu.roll(ninth, half, 1))
            out_ref[peer + 1] = jnp.where(lane_low, pltpu.roll(eight, half, 1), ninth)
        return carry

    lax.fori_loop(0, devices // 4, step, 0)


def render_kernel(
    place_ref, arrived_ref, entry_ref, bias_ref, target_ref, mono_ref,
    image_ref, feat_ref, column_ref, alpha_ref, weight_ref, send_a_ref, send_b_ref,
    wide_ref, coef_ref,
):
    peers = arrived_ref.shape[0]
    entries = entry_ref.shape[1]
    rows = image_ref.shape[1]
    across = image_ref.shape[2] // LANES
    groups = (rows // TILE) * across
    length = entries // (groups * GROUP)
    half = LANES // 2
    chunk = 512

    table = arrived_ref[...].reshape(peers * SUBS, LANES)
    ninth = arrived_ref[:, 0, :]
    low = iota((peers * SUBS, LANES), 1) < half
    low9 = iota((peers, LANES), 1) < half
    one, two, three = [piece.astype(F32) for piece in three_pieces(table)]
    one9, two9, three9 = [piece.astype(F32) for piece in three_pieces(ninth)]
    left = jnp.concatenate(
        [
            jnp.where(low, one, pltpu.roll(two, half, 1)),
            jnp.where(low9, pltpu.roll(two9, half, 1), one9),
        ],
        axis=0,
    ).astype(BF16)
    left_rest = jnp.concatenate(
        [jnp.where(low, three, 0.0), jnp.where(low9, 0.0, three9)], axis=0
    ).astype(BF16)
    feat_ref[...] = jnp.zeros(feat_ref.shape, F32)
    coef_ref[...] = jnp.zeros(coef_ref.shape, F32)

    def gather(index, carry):
        start = pl.multiple_of(index * chunk, chunk)
        slot = entry_ref[:, pl.ds(start, chunk)]
        within = slot & (half - 1)
        owner = slot >> 6
        hot = jnp.where((iota((LANES, chunk), 0) & (half - 1)) == within, 1.0, 0.0).astype(BF16)
        wide_ref[...] = dot(left, hot) + dot(left_rest, hot)
        spread = jnp.broadcast_to(owner, (SUBS, chunk))
        picked = jnp.zeros((SUBS, chunk), F32)
        for place in range(peers):
            picked = jnp.where(spread == place, wide_ref[place * SUBS : (place + 1) * SUBS, :], picked)
        last = jnp.sum(
            jnp.where(iota((peers, chunk), 0) == owner, wide_ref[peers * SUBS :, :], 0.0),
            axis=0,
            keepdims=True,
        )
        feat_ref[0:SUBS, pl.ds(start, chunk)] = picked
        feat_ref[SUBS : SUBS + 1, pl.ds(start, chunk)] = last
        center_x = picked[0:1]
        center_y = picked[1:2]
        conic_xx = picked[2:3]
        conic_xy = picked[3:4]
        conic_yy = picked[4:5]
        lin_x = conic_xx * center_x + conic_xy * center_y
        lin_y = conic_xy * center_x + conic_yy * center_y
        constant = picked[5:6] - 0.5 * (center_x * lin_x + center_y * lin_y)
        coef_ref[0:1] = (-0.5 * LOG2E) * conic_xx
        coef_ref[1:2] = -LOG2E * conic_xy
        coef_ref[2:3] = (-0.5 * LOG2E) * conic_yy
        coef_ref[3:4] = LOG2E * lin_x
        coef_ref[4:5] = LOG2E * lin_y
        coef_ref[5:6] = LOG2E * constant + bias_ref[:, pl.ds(start, chunk)]
        for number, piece in enumerate(three_pieces(coef_ref[0:SUBS])):
            coef_ref[number * SUBS : (number + 1) * SUBS] = piece.astype(F32)
        coef_ref[24:25] = picked[6:7]
        coef_ref[25:26] = picked[7:8]
        coef_ref[26:27] = last
        columns = jnp.transpose(coef_ref[...])
        coef_ref[0:SUBS] = jnp.zeros((SUBS, chunk), F32)
        column_ref[pl.ds(start, chunk), :] = columns
        alpha_ref[pl.ds(start, chunk), :] = jnp.exp2(dot(columns.astype(BF16), mono_ref[...]))
        return carry

    lax.fori_loop(0, entries // chunk, gather, 0)

    pixels = TILE * TILE
    step_rows = length * GROUP

    def scan(number, carry):
        keeps, sums = carry
        new_keeps = []
        new_sums = []
        for group in range(groups):
            at = pl.ds(pl.multiple_of(group * step_rows + number * GROUP, GROUP), GROUP)
            weight = keeps[group] * alpha_ref[at, :]
            weight_ref[at, :] = weight
            new_keeps.append(keeps[group] - weight)
            columns = column_ref[at, :]
            new_sums.append(
                tuple(
                    sums[group][channel] + weight * columns[:, 24 + channel : 25 + channel]
                    for channel in range(3)
                )
            )
        return tuple(new_keeps), tuple(new_sums)

    zero = jnp.zeros((GROUP, pixels), F32)
    start_keeps = tuple(jnp.ones((GROUP, pixels), F32) for _ in range(groups))
    start_sums = tuple((zero, zero, zero) for _ in range(groups))
    _, sums = lax.fori_loop(0, length, scan, (start_keeps, start_sums), unroll=4)
    for group in range(groups):
        row = (group // across) * TILE
        col = (group % across) * LANES
        for channel in range(3):
            for part in range(2):
                image_ref[
                    channel, row + part * SUBS : row + (part + 1) * SUBS, col : col + LANES
                ] = block_transpose(sums[group][channel][:, part * LANES : (part + 1) * LANES])

    blocks = rows // SUBS
    lane_block = iota((SUBS, LANES), 1) // TILE
    even = place_ref[1] % 2 == 0
    for vector in range(6 * blocks // SUBS):
        at_left = jnp.zeros((SUBS, LANES), F32)
        at_right = jnp.zeros((SUBS, LANES), F32)
        for place in range(SUBS):
            number = vector * SUBS + place
            source = image_ref if number // blocks < 3 else target_ref
            channel = (number // blocks) % 3
            top = (number % blocks) * SUBS
            first = source[channel, top : top + SUBS, 0:LANES]
            final = source[channel, top : top + SUBS, (across - 1) * LANES :]
            if place:
                first = pltpu.roll(first, TILE * place, 1)
            if place != SUBS - 1:
                final = pltpu.roll(final, TILE * (place + 1), 1)
            at_left = jnp.where(lane_block == place, first, at_left)
            at_right = jnp.where(lane_block == place, final, at_right)
        send_a_ref[vector * SUBS : (vector + 1) * SUBS, :] = jnp.where(even, at_right, at_left)
        send_b_ref[vector * SUBS : (vector + 1) * SUBS, :] = jnp.where(even, at_left, at_right)


def strip_kernel(place_ref, got_a_ref, got_b_ref, image_ref, target_ref, side_ref, send_a_ref, send_b_ref):
    rows = image_ref.shape[1]
    cols = image_ref.shape[2]
    blocks = rows // SUBS
    lane_block = iota((SUBS, LANES), 1) // TILE
    even = place_ref[1] % 2 == 0
    for vector in range(6 * blocks // SUBS):
        got_a = got_a_ref[vector * SUBS : (vector + 1) * SUBS, :]
        got_b = got_b_ref[vector * SUBS : (vector + 1) * SUBS, :]
        from_right = jnp.where(even, got_a, got_b)
        from_left = jnp.where(even, got_b, got_a)
        for place in range(SUBS):
            number = vector * SUBS + place
            right = pltpu.roll(from_right, LANES - TILE * place, 1) if place else from_right
            left = from_left
            if place != SUBS - 1:
                left = pltpu.roll(from_left, LANES - TILE * (place + 1), 1)
            top = (number % blocks) * SUBS
            side_ref[number // blocks, top : top + SUBS, :] = jnp.where(
                lane_block == 0, right, jnp.where(lane_block == SUBS - 1, left, 0.0)
            )
    even_row = place_ref[0] % 2 == 0
    for number in range(6):
        source = image_ref if number < 3 else target_ref
        channel = number % 3
        top = source[channel, 0:HALO, :]
        bottom = source[channel, rows - HALO :, :]
        send_a_ref[number, :, 0:cols] = jnp.where(even_row, bottom, top)
        send_b_ref[number, :, 0:cols] = jnp.where(even_row, top, bottom)
        top = side_ref[number, 0:HALO, :]
        bottom = side_ref[number, rows - HALO :, :]
        send_a_ref[number, :, cols:] = jnp.where(even_row, bottom, top)
        send_b_ref[number, :, cols:] = jnp.where(even_row, top, bottom)


def back_kernel(
    place_ref, got_a_ref, got_b_ref, image_ref, target_ref, side_ref, entry_ref, feat_ref,
    column_ref, alpha_ref, weight_ref, down_ref, down_back_ref, across_ref, mono_ref,
    out_ref,
    raw_ref, vert_ref, blur_ref, coef_ref, grad_ref, pair_ref, right_ref, slope_ref, mask_ref, sum_ref,
):
    rows = image_ref.shape[1]
    cols = image_ref.shape[2]
    wide = cols + LANES
    entries = entry_ref.shape[1]
    across = cols // LANES
    groups = (rows // TILE) * across
    length = entries // (groups * GROUP)
    tall = rows + 2 * HALO
    mid = rows + 2 * SUBS
    peers = out_ref.shape[0]
    half = LANES // 2

    even_row = place_ref[0] % 2 == 0
    for number in range(6):
        source = image_ref if number < 3 else target_ref
        raw_ref[number, 0:rows, 0:cols] = source[number % 3]
        raw_ref[number, 0:rows, cols:] = side_ref[number]
        got_a = got_a_ref[number]
        got_b = got_b_ref[number]
        raw_ref[number, rows : rows + HALO, :] = jnp.where(even_row, got_a, got_b)
        raw_ref[number, rows + HALO :, :] = jnp.where(even_row, got_b, got_a)
    down = down_ref[...]
    for channel in range(3):
        shown = raw_ref[channel]
        wanted = raw_ref[3 + channel]
        for number, value in enumerate(
            [shown, wanted, shown * shown, wanted * wanted, shown * wanted]
        ):
            at = (channel * 5 + number) * mid
            vert_ref[at : at + mid, :] = dot_full(down, value)
    for part in range(3):
        at = part * 5 * mid
        blur_ref[at : at + 5 * mid, :] = dot_full(vert_ref[at : at + 5 * mid, :], across_ref[...])
    line = iota((mid, wide), 0) - SUBS + place_ref[0] * rows
    spot = iota((mid, wide), 1)
    spot = jnp.where(spot < cols + half, spot, spot - wide) + place_ref[1] * cols
    inside = (
        (line >= 0) & (line < place_ref[2] * rows) & (spot >= 0) & (spot < place_ref[3] * cols)
    )
    down_back = down_back_ref[...]
    for channel in range(3):
        at = channel * 5 * mid
        mean_r, mean_t, square_r, square_t, cross = [
            blur_ref[at + number * mid : at + (number + 1) * mid, :] for number in range(5)
        ]
        upper_one = 2.0 * mean_r * mean_t + STAB_ONE
        upper_two = 2.0 * (cross - mean_r * mean_t) + STAB_TWO
        lower_one = mean_r * mean_r + mean_t * mean_t + STAB_ONE
        lower_two = (square_r - mean_r * mean_r) + (square_t - mean_t * mean_t) + STAB_TWO
        inv_one = 1.0 / lower_one
        inv_two = 1.0 / lower_two
        inverse = inv_one * inv_two
        value = upper_one * upper_two * inverse
        on_mean = (
            2.0 * mean_t * (upper_two - upper_one) * inverse
            + 2.0 * mean_r * value * (inv_two - inv_one)
        )
        on_square = -value * inv_two
        on_cross = 2.0 * upper_one * inverse
        for number, part in enumerate([on_mean, on_square, on_cross]):
            part = jnp.where(inside, -WEIGHT_SSIM * part, 0.0)
            spot_at = (channel * 3 + number) * rows
            coef_ref[spot_at : spot_at + rows, :] = dot_full(down_back, part)
    for channel in range(3):
        at = channel * 3 * rows
        back = dot_full(coef_ref[at : at + 3 * rows, :], across_ref[:, 0:cols])
        shown = image_ref[channel]
        wanted = target_ref[channel]
        gap = shown - wanted
        grad_ref[channel] = (
            (1.0 - WEIGHT_SSIM) * gap * lax.rsqrt(gap * gap + SMOOTHING * SMOOTHING)
            + back[0:rows]
            + 2.0 * shown * back[rows : 2 * rows]
            + wanted * back[2 * rows :]
        )

    pixels = TILE * TILE
    step_rows = length * GROUP
    mono8 = mono_ref[0:SUBS, :].astype(F32)
    right_ref[...] = jnp.zeros(right_ref.shape, F32)
    right_ref[0:SUBS, 0:pixels] = mono8
    right_ref[0:SUBS, pixels : 2 * pixels] = mono8
    same = iota((SUBS, step_rows), 0) == (iota((SUBS, step_rows), 1) & (GROUP - 1))
    slope_ref[...] = jnp.zeros(slope_ref.shape, F32)

    for group in range(groups):
        row = (group // across) * TILE
        col = (group % across) * LANES
        slopes = []
        for channel in range(3):
            slope = jnp.concatenate(
                [
                    block_transpose(
                        grad_ref[channel, row + part * SUBS : row + (part + 1) * SUBS, col : col + LANES]
                    )
                    for part in range(2)
                ],
                axis=1,
            )
            slopes.append(slope)
            for number, piece in enumerate(two_pieces(slope)):
                at = 16 + 24 * number + SUBS * channel
                right_ref[at : at + SUBS, 2 * pixels : 3 * pixels] = piece.astype(F32)
                right_ref[at : at + SUBS, 3 * pixels :] = piece.astype(F32)

        def step(number, behind):
            at = (length // 2 - 1 - number) * 2 * GROUP
            source = pl.ds(pl.multiple_of(group * step_rows + at, 2 * GROUP), 2 * GROUP)
            alpha = alpha_ref[source, :]
            weight = weight_ref[source, :]
            columns = column_ref[source, :]
            parts = []
            for low in (GROUP, 0):
                ahead = (
                    columns[low : low + GROUP, 24:25] * slopes[0]
                    + columns[low : low + GROUP, 25:26] * slopes[1]
                    + columns[low : low + GROUP, 26:27] * slopes[2]
                )
                change = ahead - behind
                parts.append(weight[low : low + GROUP] * change)
                behind = behind + alpha[low : low + GROUP] * change
            target_at = pl.ds(pl.multiple_of(at, 2 * GROUP), 2 * GROUP)
            high, rest = two_pieces(jnp.concatenate([parts[1], parts[0]], axis=0))
            pair_ref[target_at, 0:pixels] = high
            pair_ref[target_at, pixels : 2 * pixels] = rest
            high, rest = two_pieces(weight)
            pair_ref[target_at, 2 * pixels : 3 * pixels] = high
            pair_ref[target_at, 3 * pixels :] = rest
            return behind

        lax.fori_loop(0, length // 2, step, jnp.zeros((GROUP, pixels), F32), unroll=4)
        moments = jnp.transpose(dot_nt(pair_ref[...], right_ref[...].astype(BF16)))
        here = slice(group * step_rows, (group + 1) * step_rows)
        on_xx = moments[0:1]
        on_xy = moments[1:2]
        on_yy = moments[2:3]
        on_x = moments[3:4]
        on_y = moments[4:5]
        on_one = moments[5:6]
        center_x = feat_ref[0:1, here]
        center_y = feat_ref[1:2, here]
        conic_xx = feat_ref[2:3, here]
        conic_xy = feat_ref[3:4, here]
        conic_yy = feat_ref[4:5, here]
        near_x = on_x - center_x * on_one
        near_y = on_y - center_y * on_one
        slope_ref[0:1, here] = conic_xx * near_x + conic_xy * near_y
        slope_ref[1:2, here] = conic_xy * near_x + conic_yy * near_y
        slope_ref[2:3, here] = -0.5 * (on_xx - center_x * (on_x + near_x))
        slope_ref[3:4, here] = -(on_xy - center_y * on_x - center_x * near_y)
        slope_ref[4:5, here] = -0.5 * (on_yy - center_y * (on_y + near_y))
        slope_ref[5:6, here] = on_one
        for channel in range(3):
            at = 16 + SUBS * channel
            both = moments[at : at + SUBS] + moments[at + 24 : at + 24 + SUBS]
            slope_ref[6 + channel : 7 + channel, here] = jnp.sum(
                jnp.where(same, both, 0.0), axis=0, keepdims=True
            )

    chunk = 512
    tops = peers * SUBS
    sum_ref[...] = jnp.zeros(sum_ref.shape, F32)
    pair_step = iota((2 * SUBS, chunk), 0) // SUBS

    def collect(index, carry):
        start = pl.multiple_of(index * chunk, chunk)
        slot = entry_ref[:, pl.ds(start, chunk)]
        within = slot & (half - 1)
        owner = slot >> 6
        hot = jnp.where((iota((LANES, chunk), 0) & (half - 1)) == within, 1.0, 0.0).astype(BF16)
        values = [
            piece.astype(F32) for piece in two_pieces(slope_ref[0:SUBS, pl.ds(start, chunk)])
        ]
        values = [jnp.concatenate([value, value], axis=0) for value in values]
        offset = jnp.broadcast_to(owner, (2 * SUBS, chunk)) - pair_step
        for place in range(peers // 2):
            hit = offset == 2 * place
            for number in range(2):
                at = number * (tops + peers) + place * 2 * SUBS
                mask_ref[at : at + 2 * SUBS, :] = jnp.where(hit, values[number], 0.0).astype(BF16)
        hit = iota((peers, chunk), 0) == owner
        for number, piece in enumerate(
            two_pieces(slope_ref[SUBS : SUBS + 1, pl.ds(start, chunk)])
        ):
            at = number * (tops + peers) + tops
            mask_ref[at : at + peers, :] = jnp.where(hit, piece.astype(F32), 0.0).astype(BF16)
        sum_ref[...] += dot_nt(mask_ref[...], hot)
        return carry

    lax.fori_loop(0, entries // chunk, collect, 0)
    lane_low = iota((SUBS, LANES), 1) < half
    for place in range(peers):
        at = place * SUBS
        eight = sum_ref[at : at + SUBS, :] + sum_ref[tops + peers + at : tops + peers + at + SUBS, :]
        at = tops + place
        ninth = sum_ref[at : at + 1, :] + sum_ref[tops + peers + at : tops + peers + at + 1, :]
        out_ref[place] = jnp.where(lane_low, eight, jnp.broadcast_to(ninth, (SUBS, LANES)))


def return_kernel(returned_ref, got_ref, jac_ref, cam_ref, grad_ref, row_ref, mask_ref, sum_ref, pack_ref):
    devices = got_ref.shape[0]
    count, own = grad_ref.shape
    high = own // LANES
    half = LANES // 2
    tops = high * SUBS
    part_rows = tops + high
    chunk = 4 * LANES
    cam = [[cam_ref[row, col] for col in range(3)] for row in range(3)]
    fill_numbers(got_ref, row_ref)
    sum_ref[...] = jnp.zeros(sum_ref.shape, F32)
    lane_low = iota((SUBS, LANES), 1) < half
    pair_step = iota((2 * SUBS, chunk), 0) // SUBS

    def collect(index, carry):
        numbers = row_ref[:, pl.ds(pl.multiple_of(index * chunk, chunk), chunk)]
        low = numbers & (LANES - 1)
        top = numbers >> 7
        hot = jnp.where(iota((LANES, chunk), 0) == low, 1.0, 0.0).astype(BF16)
        eights = []
        ninths = []
        for part in range(chunk // LANES):
            first = returned_ref[index * 8 + 2 * part]
            second = returned_ref[index * 8 + 2 * part + 1]
            eights.append(jnp.where(lane_low, first, pltpu.roll(second, half, 1)))
            ninths.append(jnp.where(lane_low, pltpu.roll(first, half, 1), second)[0:1])
        values = [piece.astype(F32) for piece in two_pieces(jnp.concatenate(eights, axis=1))]
        values = [jnp.concatenate([value, value], axis=0) for value in values]
        offset = jnp.broadcast_to(top, (2 * SUBS, chunk)) - pair_step
        for place in range(high // 2):
            hit = offset == 2 * place
            for number in range(2):
                at = number * part_rows + place * 2 * SUBS
                mask_ref[at : at + 2 * SUBS, :] = jnp.where(hit, values[number], 0.0).astype(BF16)
        hit = iota((high, chunk), 0) == top
        for number, piece in enumerate(two_pieces(jnp.concatenate(ninths, axis=1))):
            at = number * part_rows + tops
            mask_ref[at : at + high, :] = jnp.where(hit, piece.astype(F32), 0.0).astype(BF16)
        sum_ref[...] += dot_nt(mask_ref[...], hot)
        return carry

    lax.fori_loop(0, devices * half // chunk, collect, 0)

    def block(index, carry):
        start = pl.multiple_of(index * SUBS, SUBS)

        def jac(number):
            return jac_ref[pl.ds(number * high + start, SUBS), :]

        slopes = []
        for number in range(SUBS):
            at = start * SUBS + number
            slopes.append(
                sum_ref[pl.ds(at, SUBS, stride=SUBS), :]
                + sum_ref[pl.ds(part_rows + at, SUBS, stride=SUBS), :]
            )
        at = tops + start
        slopes.append(sum_ref[pl.ds(at, SUBS), :] + sum_ref[pl.ds(part_rows + at, SUBS), :])
        on_center = [slopes[0] * jac(30), slopes[1] * jac(31)]
        conic_xx = jac(48)
        conic_xy = jac(49)
        conic_yy = jac(50)
        on_xx, on_xy, on_yy = slopes[2:5]
        first_x = conic_xx * on_xx + conic_xy * on_xy
        first_y = conic_xy * on_xy + conic_yy * on_yy
        on_first = -(conic_xx * first_x + conic_xy * conic_xy * on_yy)
        on_second = -(conic_xy * conic_xy * on_xx + conic_yy * first_y)
        on_mixed = -(
            2.0 * conic_xx * conic_xy * on_xx
            + (conic_xx * conic_yy + conic_xy * conic_xy) * on_xy
            + 2.0 * conic_xy * conic_yy * on_yy
        )
        out = []
        for axis in range(3):
            out.append(
                cam[0][axis] * on_center[0]
                + cam[1][axis] * on_center[1]
                + slopes[6] * jac(21 + axis)
                + slopes[7] * jac(24 + axis)
                + slopes[8] * jac(27 + axis)
            )
        for number in range(7):
            out.append(
                on_first * jac(number) + on_mixed * jac(7 + number) + on_second * jac(14 + number)
            )
        out.append(slopes[5] * jac(32))
        for channel in range(3):
            out.append(SH_ZERO * slopes[6 + channel])
            for term in range(1, 16):
                out.append(slopes[6 + channel] * jac(32 + term))
        for number, value in enumerate(out):
            pack_ref[pl.ds(number * high + start, SUBS), :] = value
        return carry

    lax.fori_loop(0, high // SUBS, block, 0)
    for first in range(0, count, SUBS):
        number = min(SUBS, count - first)
        for place in range(high):
            grad_ref[first : first + number, place * LANES : (place + 1) * LANES] = pack_ref[
                pl.ds(first * high + place, number, stride=high), :
            ]


def band(outs, ins):
    taps = np.exp(-((np.arange(11) - 5.0) ** 2) / (2.0 * BLUR_SIGMA * BLUR_SIGMA))
    offset = np.asarray(ins)[None, :] - np.asarray(outs)[:, None]
    values = np.exp(-(offset**2) / (2.0 * BLUR_SIGMA * BLUR_SIGMA)) / taps.sum()
    return np.where(np.abs(offset) <= RIM, values, 0.0).astype(np.float32)


def monomials():
    pixel = np.arange(TILE * TILE)
    x = (pixel % TILE) - 7.5
    y = (pixel // TILE) - 7.5
    eight = np.stack([x * x, x * y, y * y, x, y, x * 0 + 1, x * 0, x * 0])
    return np.concatenate([eight, eight, eight, eight * 0]).astype(np.float32)


def call(body, out_shape, scratch, scalar_at, args, flops):
    in_specs = [
        pl.BlockSpec(memory_space=pltpu.SMEM if number in scalar_at else pltpu.VMEM)
        for number in range(len(args))
    ]
    return pl.pallas_call(
        body,
        out_shape=out_shape,
        in_specs=in_specs,
        out_specs=jax.tree.map(lambda _: pl.BlockSpec(memory_space=pltpu.VMEM), out_shape),
        scratch_shapes=scratch,
        compiler_params=pltpu.CompilerParams(vmem_limit_bytes=VMEM_BYTES),
        cost_estimate=pl.CostEstimate(flops=flops, bytes_accessed=1 << 20, transcendentals=0),
    )(*args)


def swap_pairs(count, first):
    pairs = []
    for low in range(first, count - 1, 2):
        pairs += [(low, low + 1), (low + 1, low)]
    return pairs


def swap(value_a, value_b, axis):
    count = lax.axis_size(axis)
    return (
        lax.ppermute(value_a, axis, swap_pairs(count, 0)),
        lax.ppermute(value_b, axis, swap_pairs(count, 1)),
    )


def exchange(payload):
    return lax.all_to_all(payload, ("img", "cell"), split_axis=0, concat_axis=0, tiled=True)


def shards(attributes, camera, target, visible_index, tile_lists, tile_len):
    img_count = lax.axis_size("img")
    cell_count = lax.axis_size("cell")
    devices = img_count * cell_count
    slots = visible_index.shape[1]
    per_owner = slots // devices
    count, own = attributes.shape
    high = own // LANES
    _, rows, cols = target.shape
    tiles_down, tiles_across, length = tile_lists.shape
    entries = tiles_down * tiles_across * length
    wide = cols + LANES
    mid = rows + 2 * SUBS
    tall = rows + 2 * HALO
    place = jnp.stack(
        [
            lax.axis_index("img"),
            lax.axis_index("cell"),
            jnp.int32(img_count),
            jnp.int32(cell_count),
        ]
    ).astype(jnp.int32)

    asked = visible_index.reshape(devices, per_owner)
    got = exchange(jnp.concatenate([asked, asked], axis=1))

    table, jac = call(
        owner_kernel,
        (
            jax.ShapeDtypeStruct((high * (SUBS + 1), 3 * LANES), BF16),
            jax.ShapeDtypeStruct((JAC_ROWS * high, LANES), F32),
        ),
        [pltpu.VMEM((count * high, LANES), F32), pltpu.VMEM((high * (SUBS + 1), LANES), F32)],
        (1,),
        (attributes, camera),
        1 << 24,
    )
    reply = call(
        reply_kernel,
        jax.ShapeDtypeStruct((devices, SUBS, LANES), F32),
        [pltpu.VMEM((1, slots), jnp.int32), pltpu.VMEM((high * (SUBS + 1), 2 * LANES), F32)],
        (),
        (table, got),
        1 << 24,
    )
    arrived = exchange(reply)

    order = (tiles_down, tiles_across // GROUP, GROUP, length)
    entry = tile_lists.reshape(order).transpose(0, 1, 3, 2).reshape(1, entries)
    live = jnp.arange(length, dtype=jnp.int32)[None, None, :, None] < tile_len.reshape(
        tiles_down, tiles_across // GROUP, 1, GROUP
    )
    bias = jnp.where(live, 0.0, -1e30).astype(F32).reshape(1, entries)
    mono = jnp.asarray(monomials()).astype(BF16)
    packed = 6 * rows // SUBS
    big = jax.ShapeDtypeStruct((entries, TILE * TILE), F32)
    strip = jax.ShapeDtypeStruct((packed, LANES), F32)
    image, feat, column, alpha, weight, send_a, send_b = call(
        render_kernel,
        (
            jax.ShapeDtypeStruct((3, rows, cols), F32),
            jax.ShapeDtypeStruct((2 * SUBS, entries), F32),
            jax.ShapeDtypeStruct((entries, 32), F32),
            big,
            big,
            strip,
            strip,
        ),
        [pltpu.VMEM((devices * (SUBS + 1), 512), F32), pltpu.VMEM((32, 512), F32)],
        (0,),
        (place, arrived, entry, bias, target, mono),
        1 << 26,
    )
    got_a, got_b = swap(send_a, send_b, "cell")
    edge = jax.ShapeDtypeStruct((6, HALO, wide), F32)
    side, send_a, send_b = call(
        strip_kernel,
        (jax.ShapeDtypeStruct((6, rows, LANES), F32), edge, edge),
        [],
        (0,),
        (place, got_a, got_b, image, target),
        1 << 20,
    )
    got_a, got_b = swap(send_a, send_b, "img")

    tall_at = np.arange(tall)
    tall_at = np.where(tall_at < rows + HALO, tall_at, tall_at - tall)
    mid_at = np.arange(mid) - SUBS
    wide_at = np.arange(wide)
    wide_at = np.where(wide_at < cols + LANES // 2, wide_at, wide_at - wide)
    down = jnp.asarray(band(mid_at, tall_at))
    down_back = jnp.asarray(band(np.arange(rows), mid_at))
    across = jnp.asarray(band(wide_at, wide_at))
    pixels = TILE * TILE
    group_rows = length * GROUP
    slot_grads = call(
        back_kernel,
        jax.ShapeDtypeStruct((devices, SUBS, LANES), F32),
        [
            pltpu.VMEM((6, tall, wide), F32),
            pltpu.VMEM((15 * mid, wide), F32),
            pltpu.VMEM((15 * mid, wide), F32),
            pltpu.VMEM((9 * rows, wide), F32),
            pltpu.VMEM((3, rows, cols), F32),
            pltpu.VMEM((group_rows, 4 * pixels), BF16),
            pltpu.VMEM((64, 4 * pixels), F32),
            pltpu.VMEM((2 * SUBS, entries), F32),
            pltpu.VMEM((2 * devices * (SUBS + 1), 512), BF16),
            pltpu.VMEM((2 * devices * (SUBS + 1), LANES), F32),
        ],
        (0,),
        (
            place, got_a, got_b, image, target, side, entry, feat, column, alpha, weight,
            down, down_back, across, mono,
        ),
        1 << 27,
    )
    returned = exchange(slot_grads)
    return call(
        return_kernel,
        jax.ShapeDtypeStruct((count, own), F32),
        [
            pltpu.VMEM((1, slots), jnp.int32),
            pltpu.VMEM((2 * high * (SUBS + 1), 4 * LANES), BF16),
            pltpu.VMEM((2 * high * (SUBS + 1), LANES), F32),
            pltpu.VMEM((count * high, LANES), F32),
        ],
        (3,),
        (returned, got, jac, camera),
        1 << 26,
    )


def solution(mesh):
    return jax.shard_map(
        shards,
        mesh=mesh,
        in_specs=(
            P(None, ("img", "cell")),
            P(),
            P(None, "img", "cell"),
            P(("img", "cell"), None),
            P("img", "cell", None),
            P("img", "cell"),
        ),
        out_specs=P(None, ("img", "cell")),
        check_vma=False,
    )
```

```python
import functools
import math

import jax
import jax.numpy as jnp
import numpy as np
from jax import lax
from jax.experimental import pallas as pl
from jax.experimental.pallas import tpu as pltpu
from jax.sharding import PartitionSpec as P

TILE = 16
LANES = 128
SUBS = 8
GROUP = 8
RIM = 5
HALO = 16
WEIGHT_SSIM = 0.2
SMOOTHING = 0.01
STAB_ONE = 0.0001
STAB_TWO = 0.0009
BLUR_SIGMA = 1.5
LOG2E = 1.4426950408889634
SH_ZERO = 0.28209479177387814
SH_ONE = 0.4886025119029199
SH_TWO = (
    1.0925484305920792,
    -1.0925484305920792,
    0.31539156525252005,
    -1.0925484305920792,
    0.5462742152960396,
)
SH_THREE = (
    -0.5900435899266435,
    2.890611442640554,
    -0.4570457994644658,
    0.3731763325901154,
    -0.4570457994644658,
    1.445305721320277,
    -0.5900435899266435,
)
F32 = jnp.float32
BF16 = jnp.bfloat16
JAC_ROWS = 51
VMEM_BYTES = 56 * 1024 * 1024


def harmonic_basis(unit_x, unit_y, unit_z):
    unit_xx = unit_x * unit_x
    unit_yy = unit_y * unit_y
    unit_zz = unit_z * unit_z
    return [
        -SH_ONE * unit_y,
        SH_ONE * unit_z,
        -SH_ONE * unit_x,
        SH_TWO[0] * unit_x * unit_y,
        SH_TWO[1] * unit_y * unit_z,
        SH_TWO[2] * (2.0 * unit_zz - unit_xx - unit_yy),
        SH_TWO[3] * unit_x * unit_z,
        SH_TWO[4] * (unit_xx - unit_yy),
        SH_THREE[0] * unit_y * (3.0 * unit_xx - unit_yy),
        SH_THREE[1] * unit_x * unit_y * unit_z,
        SH_THREE[2] * unit_y * (4.0 * unit_zz - unit_xx - unit_yy),
        SH_THREE[3] * unit_z * (2.0 * unit_zz - 3.0 * unit_xx - 3.0 * unit_yy),
        SH_THREE[4] * unit_x * (4.0 * unit_zz - unit_xx - unit_yy),
        SH_THREE[5] * unit_z * (unit_xx - unit_yy),
        SH_THREE[6] * unit_x * (unit_xx - 3.0 * unit_yy),
    ]


def three_pieces(value):
    first = value.astype(BF16)
    rest = value - first.astype(F32)
    second = rest.astype(BF16)
    third = (rest - second.astype(F32)).astype(BF16)
    return first, second, third


def two_pieces(value):
    first = value.astype(BF16)
    return first, (value - first.astype(F32)).astype(BF16)


def dot(left, right):
    return jnp.dot(left, right, preferred_element_type=F32)


def dot_nt(left, right):
    return lax.dot_general(left, right, (((1,), (1,)), ((), ())), preferred_element_type=F32)


def dot_full(left, right):
    return jnp.dot(left, right, preferred_element_type=F32, precision=lax.Precision.HIGHEST)


def iota(shape, dim):
    return lax.broadcasted_iota(jnp.int32, shape, dim)


def block_transpose(block):
    turn = (iota(block.shape, 0) - iota(block.shape, 1) // TILE) & (SUBS - 1)
    out = block
    for step in range(1, SUBS):
        moved = pltpu.roll(block, LANES - TILE * step, 1)
        moved = pltpu.roll(moved, step, 0)
        out = jnp.where(turn == step, moved, out)
    return out


def covariance(scale_rows, quat_rows, cam):
    scales = [jnp.exp(row) for row in scale_rows]
    quat_w = 1.5 + jnp.tanh(quat_rows[0])
    quat_x, quat_y, quat_z = quat_rows[1:]
    inverse = lax.rsqrt(quat_w * quat_w + quat_x * quat_x + quat_y * quat_y + quat_z * quat_z)
    quat_w, quat_x, quat_y, quat_z = (
        quat_w * inverse,
        quat_x * inverse,
        quat_y * inverse,
        quat_z * inverse,
    )
    rotation = [
        [
            1.0 - 2.0 * (quat_y * quat_y + quat_z * quat_z),
            2.0 * (quat_x * quat_y - quat_w * quat_z),
            2.0 * (quat_x * quat_z + quat_w * quat_y),
        ],
        [
            2.0 * (quat_x * quat_y + quat_w * quat_z),
            1.0 - 2.0 * (quat_x * quat_x + quat_z * quat_z),
            2.0 * (quat_y * quat_z - quat_w * quat_x),
        ],
        [
            2.0 * (quat_x * quat_z - quat_w * quat_y),
            2.0 * (quat_y * quat_z + quat_w * quat_x),
            1.0 - 2.0 * (quat_x * quat_x + quat_y * quat_y),
        ],
    ]
    axes = [
        [
            (
                cam[screen][0] * rotation[0][axis]
                + cam[screen][1] * rotation[1][axis]
                + cam[screen][2] * rotation[2][axis]
            )
            * scales[axis]
            for axis in range(3)
        ]
        for screen in range(2)
    ]
    first = axes[0][0] * axes[0][0] + axes[0][1] * axes[0][1] + axes[0][2] * axes[0][2] + 0.3
    mixed = axes[0][0] * axes[1][0] + axes[0][1] * axes[1][1] + axes[0][2] * axes[1][2]
    second = axes[1][0] * axes[1][0] + axes[1][1] * axes[1][1] + axes[1][2] * axes[1][2] + 0.3
    return first, mixed, second


def owner_kernel(attr_ref, cam_ref, table_ref, jac_ref, pack_ref, feat_ref):
    count, own = attr_ref.shape
    high = own // LANES
    cam = [[cam_ref[row, col] for col in range(3)] for row in range(3)]
    for first in range(0, count, SUBS):
        number = min(SUBS, count - first)
        for place in range(high):
            pack_ref[pl.ds(first * high + place, number, stride=high), :] = attr_ref[
                first : first + number, place * LANES : (place + 1) * LANES
            ]

    def block(index, carry):
        start = pl.multiple_of(index * SUBS, SUBS)

        def row(number):
            return pack_ref[pl.ds(number * high + start, SUBS), :]

        positions = [row(number) for number in range(3)]
        shape_rows = [row(3 + number) for number in range(7)]
        jac = []
        (cov_first, cov_mixed, cov_second), pull = jax.vjp(
            lambda *rows: covariance(rows[:3], rows[3:], cam), *shape_rows
        )
        one = jnp.ones_like(cov_first)
        zero = jnp.zeros_like(cov_first)
        jac += pull((one, zero, zero))
        jac += pull((zero, one, zero))
        jac += pull((zero, zero, one))
        inverse = 1.0 / (cov_first * cov_second - cov_mixed * cov_mixed)
        conic = [cov_second * inverse, -cov_mixed * inverse, cov_first * inverse]
        centers = []
        slopes = []
        for screen in range(2):
            angle = (
                cam[screen][0] * positions[0]
                + cam[screen][1] * positions[1]
                + cam[screen][2] * positions[2]
            ) / 3.0
            centers.append(7.0 * jnp.sin(angle))
            slopes.append((7.0 / 3.0) * jnp.cos(angle))
        raw = row(10)
        decay = jnp.exp(-raw)
        log_opacity = -jnp.log(1.0 + decay)
        harmonics = [[row(11 + 16 * channel + term) for term in range(16)] for channel in range(3)]

        def colours_of(pos_x, pos_y, pos_z):
            off_x = pos_x - cam[2][0]
            off_y = pos_y - cam[2][1]
            off_z = pos_z - cam[2][2]
            scale = lax.rsqrt(off_x * off_x + off_y * off_y + off_z * off_z)
            basis = harmonic_basis(off_x * scale, off_y * scale, off_z * scale)
            colours = []
            for channel in range(3):
                total = 0.5 + SH_ZERO * harmonics[channel][0]
                for term in range(1, 16):
                    total = total + basis[term - 1] * harmonics[channel][term]
                colours.append(total)
            return tuple(colours), basis

        colours, pull_colours, basis = jax.vjp(colours_of, *positions, has_aux=True)
        jac += pull_colours((one, zero, zero))
        jac += pull_colours((zero, one, zero))
        jac += pull_colours((zero, zero, one))
        jac += slopes
        jac.append(decay / (1.0 + decay))
        jac += basis
        jac += conic
        for number, value in enumerate(jac):
            jac_ref[pl.ds(number * high + start, SUBS), :] = value
        features = centers + conic + [log_opacity] + list(colours)
        for number in range(SUBS):
            feat_ref[pl.ds(start * SUBS + number, SUBS, stride=SUBS), :] = features[number]
        feat_ref[pl.ds(high * SUBS + start, SUBS), :] = features[SUBS]
        return carry

    lax.fori_loop(0, high // SUBS, block, 0)
    for number, piece in enumerate(three_pieces(feat_ref[...])):
        table_ref[:, number * LANES : (number + 1) * LANES] = piece


def fill_numbers(got_ref, row_ref):
    lane_low = iota((1, LANES), 1) < LANES // 2
    for pair in range(got_ref.shape[0] // 2):
        row_ref[:, pair * LANES : (pair + 1) * LANES] = jnp.where(
            lane_low, got_ref[2 * pair : 2 * pair + 1, :], got_ref[2 * pair + 1 : 2 * pair + 2, :]
        )


def reply_kernel(table_ref, got_ref, out_ref, row_ref, wide_ref):
    devices = got_ref.shape[0]
    high = table_ref.shape[0] // (SUBS + 1)
    chunk = 2 * LANES
    half = LANES // 2
    fill_numbers(got_ref, row_ref)

    def step(index, carry):
        numbers = row_ref[:, pl.ds(pl.multiple_of(index * chunk, chunk), chunk)]
        low = numbers & (LANES - 1)
        top = numbers >> 7
        hot = jnp.where(iota((LANES, chunk), 0) == low, 1.0, 0.0).astype(BF16)
        wide_ref[...] = dot(
            table_ref[:, : 2 * LANES], jnp.concatenate([hot, hot], axis=0)
        ) + dot(table_ref[:, 2 * LANES :], hot)
        spread = jnp.broadcast_to(top, (SUBS, chunk))
        picked = jnp.zeros((SUBS, chunk), F32)
        for place in range(high):
            picked = jnp.where(spread == place, wide_ref[place * SUBS : (place + 1) * SUBS, :], picked)
        last = jnp.sum(
            jnp.where(iota((high, chunk), 0) == top, wide_ref[high * SUBS :, :], 0.0),
            axis=0,
            keepdims=True,
        )
        lane_low = iota((SUBS, LANES), 1) < half
        for part in range(chunk // LANES):
            eight = picked[:, part * LANES : (part + 1) * LANES]
            ninth = jnp.broadcast_to(last[:, part * LANES : (part + 1) * LANES], (SUBS, LANES))
            peer = index * 4 + part * 2
            out_ref[peer] = jnp.where(lane_low, eight, pltpu.roll(ninth, half, 1))
            out_ref[peer + 1] = jnp.where(lane_low, pltpu.roll(eight, half, 1), ninth)
        return carry

    lax.fori_loop(0, devices // 4, step, 0)


def spread_colours(feat_ref, start, size):
    same = iota((GROUP, size), 0) == (iota((GROUP, size), 1) & (GROUP - 1))
    return jnp.concatenate(
        [
            jnp.where(same, feat_ref[6 + channel : 7 + channel, start : start + size], 0.0)
            for channel in range(3)
        ],
        axis=0,
    )


def render_kernel(
    place_ref, arrived_ref, entry_ref, bias_ref, target_ref, mono_ref,
    image_ref, feat_ref, alpha_out, weight_out, send_a_ref, send_b_ref,
    wide_ref, coef_ref, alpha_ref, weight_ref, alpha_sems, weight_sems,
):
    peers = arrived_ref.shape[0]
    entries = entry_ref.shape[1]
    rows = image_ref.shape[1]
    across = image_ref.shape[2] // LANES
    groups = (rows // TILE) * across
    length = entries // (groups * GROUP)
    half = LANES // 2
    chunk = 512

    table = arrived_ref[...].reshape(peers * SUBS, LANES)
    ninth = arrived_ref[:, 0, :]
    low = iota((peers * SUBS, LANES), 1) < half
    low9 = iota((peers, LANES), 1) < half
    one, two, three = [piece.astype(F32) for piece in three_pieces(table)]
    one9, two9, three9 = [piece.astype(F32) for piece in three_pieces(ninth)]
    left = jnp.concatenate(
        [
            jnp.where(low, one, pltpu.roll(two, half, 1)),
            jnp.where(low9, pltpu.roll(two9, half, 1), one9),
        ],
        axis=0,
    ).astype(BF16)
    left_rest = jnp.concatenate(
        [jnp.where(low, three, 0.0), jnp.where(low9, 0.0, three9)], axis=0
    ).astype(BF16)
    left = jnp.concatenate([left, left_rest], axis=1)
    feat_ref[...] = jnp.zeros(feat_ref.shape, F32)
    coef_ref[...] = jnp.zeros(coef_ref.shape, F32)

    def alpha_copy(index):
        at = pl.ds(pl.multiple_of(index * chunk, chunk), chunk)
        return pltpu.make_async_copy(alpha_ref.at[at], alpha_out.at[at], alpha_sems.at[index])

    def gather(index, carry):
        start = pl.multiple_of(index * chunk, chunk)
        slot = entry_ref[:, pl.ds(start, chunk)]
        within = slot & (half - 1)
        owner = slot >> 6
        hot = jnp.where((iota((LANES, chunk), 0) & (half - 1)) == within, 1.0, 0.0).astype(BF16)
        wide_ref[...] = dot(left, jnp.concatenate([hot, hot], axis=0))
        spread = jnp.broadcast_to(owner, (SUBS, chunk))
        picked = jnp.zeros((SUBS, chunk), F32)
        for place in range(peers):
            picked = jnp.where(spread == place, wide_ref[place * SUBS : (place + 1) * SUBS, :], picked)
        last = jnp.sum(
            jnp.where(iota((peers, chunk), 0) == owner, wide_ref[peers * SUBS :, :], 0.0),
            axis=0,
            keepdims=True,
        )
        feat_ref[0:SUBS, pl.ds(start, chunk)] = picked
        feat_ref[SUBS : SUBS + 1, pl.ds(start, chunk)] = last
        center_x = picked[0:1]
        center_y = picked[1:2]
        conic_xx = picked[2:3]
        conic_xy = picked[3:4]
        conic_yy = picked[4:5]
        lin_x = conic_xx * center_x + conic_xy * center_y
        lin_y = conic_xy * center_x + conic_yy * center_y
        constant = picked[5:6] - 0.5 * (center_x * lin_x + center_y * lin_y)
        coef_ref[0:1] = (-0.5 * LOG2E) * conic_xx
        coef_ref[1:2] = -LOG2E * conic_xy
        coef_ref[2:3] = (-0.5 * LOG2E) * conic_yy
        coef_ref[3:4] = LOG2E * lin_x
        coef_ref[4:5] = LOG2E * lin_y
        coef_ref[5:6] = LOG2E * constant + bias_ref[:, pl.ds(start, chunk)]
        for number, piece in enumerate(three_pieces(coef_ref[0:SUBS])):
            coef_ref[number * SUBS : (number + 1) * SUBS] = piece.astype(F32)
        columns = jnp.transpose(coef_ref[...]).astype(BF16)
        alpha_ref[pl.ds(start, chunk), :] = jnp.exp2(dot(columns, mono_ref[...]))
        alpha_copy(index).start()
        return carry

    lax.fori_loop(0, entries // chunk, gather, 0)

    pixels = TILE * TILE
    step_rows = length * GROUP
    parts = 4
    part_rows = step_rows // parts

    def weight_copy(group, part):
        at = pl.ds(group * step_rows + part * part_rows, part_rows)
        return pltpu.make_async_copy(
            weight_ref.at[at], weight_out.at[at], weight_sems.at[group * parts + part]
        )

    def scan(number, keeps):
        new_keeps = []
        for group in range(groups):
            at = pl.ds(
                pl.multiple_of(group * step_rows + number * 2 * GROUP, 2 * GROUP), 2 * GROUP
            )
            alpha = alpha_ref[at, :]
            first = keeps[group] * alpha[0:GROUP]
            keep = keeps[group] - first
            second = keep * alpha[GROUP:]
            new_keeps.append(keep - second)
            high, rest = two_pieces(jnp.concatenate([first, second], axis=0))
            weight_ref[at, 0:pixels] = high
            weight_ref[at, pixels:] = rest
        return tuple(new_keeps)

    keeps = tuple(jnp.ones((GROUP, pixels), F32) for _ in range(groups))
    steps = length // (2 * parts)
    for part in range(parts):
        keeps = lax.fori_loop(part * steps, (part + 1) * steps, scan, keeps, unroll=4)
        for group in range(groups):
            weight_copy(group, part).start()
    for group in range(groups):
        here = slice(group * step_rows, (group + 1) * step_rows)
        left = jnp.concatenate(
            two_pieces(spread_colours(feat_ref, group * step_rows, step_rows)), axis=0
        )
        sums = dot(left, weight_ref[here, 0:pixels]) + dot(left, weight_ref[here, pixels:])
        row = (group // across) * TILE
        col = (group % across) * LANES
        for channel in range(3):
            at = channel * GROUP
            total = sums[at : at + GROUP] + sums[at + 3 * GROUP : at + 4 * GROUP]
            for part in range(2):
                image_ref[
                    channel, row + part * SUBS : row + (part + 1) * SUBS, col : col + LANES
                ] = block_transpose(total[:, part * LANES : (part + 1) * LANES])

    blocks = rows // SUBS
    lane_block = iota((SUBS, LANES), 1) // TILE
    even = place_ref[1] % 2 == 0
    for vector in range(6 * blocks // SUBS):
        at_left = jnp.zeros((SUBS, LANES), F32)
        at_right = jnp.zeros((SUBS, LANES), F32)
        for place in range(SUBS):
            number = vector * SUBS + place
            source = image_ref if number // blocks < 3 else target_ref
            channel = (number // blocks) % 3
            top = (number % blocks) * SUBS
            first = source[channel, top : top + SUBS, 0:LANES]
            final = source[channel, top : top + SUBS, (across - 1) * LANES :]
            if place:
                first = pltpu.roll(first, TILE * place, 1)
            if place != SUBS - 1:
                final = pltpu.roll(final, TILE * (place + 1), 1)
            at_left = jnp.where(lane_block == place, first, at_left)
            at_right = jnp.where(lane_block == place, final, at_right)
        send_a_ref[vector * SUBS : (vector + 1) * SUBS, :] = jnp.where(even, at_right, at_left)
        send_b_ref[vector * SUBS : (vector + 1) * SUBS, :] = jnp.where(even, at_left, at_right)
    for index in range(entries // chunk):
        alpha_copy(index).wait()
    for group in range(groups):
        for part in range(parts):
            weight_copy(group, part).wait()


def strip_kernel(place_ref, got_a_ref, got_b_ref, image_ref, target_ref, side_ref, send_a_ref, send_b_ref):
    rows = image_ref.shape[1]
    cols = image_ref.shape[2]
    blocks = rows // SUBS
    lane_block = iota((SUBS, LANES), 1) // TILE
    even = place_ref[1] % 2 == 0
    for vector in range(6 * blocks // SUBS):
        got_a = got_a_ref[vector * SUBS : (vector + 1) * SUBS, :]
        got_b = got_b_ref[vector * SUBS : (vector + 1) * SUBS, :]
        from_right = jnp.where(even, got_a, got_b)
        from_left = jnp.where(even, got_b, got_a)
        for place in range(SUBS):
            number = vector * SUBS + place
            right = pltpu.roll(from_right, LANES - TILE * place, 1) if place else from_right
            left = from_left
            if place != SUBS - 1:
                left = pltpu.roll(from_left, LANES - TILE * (place + 1), 1)
            top = (number % blocks) * SUBS
            side_ref[number // blocks, top : top + SUBS, :] = jnp.where(
                lane_block == 0, right, jnp.where(lane_block == SUBS - 1, left, 0.0)
            )
    even_row = place_ref[0] % 2 == 0
    for number in range(6):
        source = image_ref if number < 3 else target_ref
        channel = number % 3
        top = source[channel, 0:HALO, :]
        bottom = source[channel, rows - HALO :, :]
        send_a_ref[number, :, 0:cols] = jnp.where(even_row, bottom, top)
        send_b_ref[number, :, 0:cols] = jnp.where(even_row, top, bottom)
        top = side_ref[number, 0:HALO, :]
        bottom = side_ref[number, rows - HALO :, :]
        send_a_ref[number, :, cols:] = jnp.where(even_row, bottom, top)
        send_b_ref[number, :, cols:] = jnp.where(even_row, top, bottom)


def back_kernel(
    place_ref, got_a_ref, got_b_ref, image_ref, target_ref, side_ref, entry_ref, feat_ref,
    alpha_in, weight_in, down_ref, down_back_ref, across_ref, mono_ref,
    out_ref,
    raw_ref, vert_ref, blur_ref, coef_ref, grad_ref, alpha_ref, weight_ref, ahead_ref, pair_ref,
    right_ref, slope_ref, mask_ref, sum_ref, sems,
):
    rows = image_ref.shape[1]
    cols = image_ref.shape[2]
    wide = cols + LANES
    entries = entry_ref.shape[1]
    across = cols // LANES
    groups = (rows // TILE) * across
    length = entries // (groups * GROUP)
    tall = rows + 2 * HALO
    mid = rows + 2 * SUBS
    peers = out_ref.shape[0]
    half = LANES // 2

    alpha_copy = pltpu.make_async_copy(alpha_in, alpha_ref, sems.at[0])
    weight_copy = pltpu.make_async_copy(weight_in, weight_ref, sems.at[1])
    alpha_copy.start()
    weight_copy.start()
    even_row = place_ref[0] % 2 == 0
    for number in range(6):
        source = image_ref if number < 3 else target_ref
        raw_ref[number, 0:rows, 0:cols] = source[number % 3]
        raw_ref[number, 0:rows, cols:] = side_ref[number]
        got_a = got_a_ref[number]
        got_b = got_b_ref[number]
        raw_ref[number, rows : rows + HALO, :] = jnp.where(even_row, got_a, got_b)
        raw_ref[number, rows + HALO :, :] = jnp.where(even_row, got_b, got_a)
    down = down_ref[...]
    for channel in range(3):
        shown = raw_ref[channel]
        wanted = raw_ref[3 + channel]
        for number, value in enumerate(
            [shown, wanted, shown * shown, wanted * wanted, shown * wanted]
        ):
            at = (channel * 5 + number) * mid
            vert_ref[at : at + mid, :] = dot_full(down, value)
    for part in range(3):
        at = part * 5 * mid
        blur_ref[at : at + 5 * mid, :] = dot_full(vert_ref[at : at + 5 * mid, :], across_ref[...])
    line = iota((mid, wide), 0) - SUBS + place_ref[0] * rows
    spot = iota((mid, wide), 1)
    spot = jnp.where(spot < cols + half, spot, spot - wide) + place_ref[1] * cols
    inside = (
        (line >= 0) & (line < place_ref[2] * rows) & (spot >= 0) & (spot < place_ref[3] * cols)
    )
    down_back = down_back_ref[...]
    for channel in range(3):
        at = channel * 5 * mid
        mean_r, mean_t, square_r, square_t, cross = [
            blur_ref[at + number * mid : at + (number + 1) * mid, :] for number in range(5)
        ]
        upper_one = 2.0 * mean_r * mean_t + STAB_ONE
        upper_two = 2.0 * (cross - mean_r * mean_t) + STAB_TWO
        lower_one = mean_r * mean_r + mean_t * mean_t + STAB_ONE
        lower_two = (square_r - mean_r * mean_r) + (square_t - mean_t * mean_t) + STAB_TWO
        inv_one = 1.0 / lower_one
        inv_two = 1.0 / lower_two
        inverse = inv_one * inv_two
        value = upper_one * upper_two * inverse
        on_mean = (
            2.0 * mean_t * (upper_two - upper_one) * inverse
            + 2.0 * mean_r * value * (inv_two - inv_one)
        )
        on_square = -value * inv_two
        on_cross = 2.0 * upper_one * inverse
        for number, part in enumerate([on_mean, on_square, on_cross]):
            part = jnp.where(inside, -WEIGHT_SSIM * part, 0.0)
            spot_at = (channel * 3 + number) * rows
            coef_ref[spot_at : spot_at + rows, :] = dot_full(down_back, part)
    for channel in range(3):
        at = channel * 3 * rows
        back = dot_full(coef_ref[at : at + 3 * rows, :], across_ref[:, 0:cols])
        shown = image_ref[channel]
        wanted = target_ref[channel]
        gap = shown - wanted
        grad_ref[channel] = (
            (1.0 - WEIGHT_SSIM) * gap * lax.rsqrt(gap * gap + SMOOTHING * SMOOTHING)
            + back[0:rows]
            + 2.0 * shown * back[rows : 2 * rows]
            + wanted * back[2 * rows :]
        )

    pixels = TILE * TILE
    step_rows = length * GROUP
    mono = mono_ref[0 : 2 * SUBS, :]
    mono = jnp.concatenate([mono, mono], axis=1)
    same = iota((SUBS, step_rows), 0) == (iota((SUBS, step_rows), 1) & (GROUP - 1))
    slope_ref[...] = jnp.zeros(slope_ref.shape, F32)

    for group in range(groups):
        row = (group // across) * TILE
        col = (group % across) * LANES
        start = group * step_rows
        slopes = []
        for channel in range(3):
            for part in range(2):
                slopes.append(
                    block_transpose(
                        grad_ref[channel, row + part * SUBS : row + (part + 1) * SUBS, col : col + LANES]
                    )
                )
        slopes = jnp.concatenate(
            [jnp.concatenate(slopes[2 * channel : 2 * channel + 2], axis=1) for channel in range(3)],
            axis=0,
        )
        high, rest = [piece.astype(F32) for piece in two_pieces(slopes)]
        at = group * 6 * GROUP
        both = jnp.concatenate([high, rest], axis=0)
        right_ref[at : at + 6 * GROUP, 0:pixels] = both
        right_ref[at : at + 6 * GROUP, pixels:] = both
        top, low = [
            piece.astype(F32)
            for piece in two_pieces(spread_colours(feat_ref, start, step_rows))
        ]
        left = jnp.transpose(jnp.concatenate([top, low, top], axis=0)).astype(BF16)
        ahead_ref[start : start + step_rows, :] = dot(
            left, jnp.concatenate([high, high, rest], axis=0).astype(BF16)
        )

    alpha_copy.wait()
    weight_copy.wait()

    def step(number, behinds):
        new_behinds = []
        at = (length // 2 - 1 - number) * 2 * GROUP
        for group in range(groups):
            source = pl.ds(pl.multiple_of(group * step_rows + at, 2 * GROUP), 2 * GROUP)
            alpha = alpha_ref[source, :]
            ahead = ahead_ref[source, :]
            weight = weight_ref[source, 0:pixels].astype(F32) + weight_ref[source, pixels:].astype(F32)
            behind = behinds[group]
            second = ahead[GROUP:] - behind
            behind = behind + alpha[GROUP:] * second
            first = ahead[0:GROUP] - behind
            new_behinds.append(behind + alpha[0:GROUP] * first)
            high, rest = two_pieces(weight * jnp.concatenate([first, second], axis=0))
            pair_ref[source, 0:pixels] = high
            pair_ref[source, pixels:] = rest
        return tuple(new_behinds)

    zero = jnp.zeros((GROUP, pixels), F32)
    lax.fori_loop(0, length // 2, step, tuple(zero for _ in range(groups)), unroll=4)

    for group in range(groups):
        here = slice(group * step_rows, (group + 1) * step_rows)
        at = group * 6 * GROUP
        moments = jnp.transpose(dot_nt(pair_ref[here, :], mono))
        tints = jnp.transpose(
            dot_nt(weight_ref[here, :], right_ref[at : at + 6 * GROUP, :].astype(BF16))
        )
        on_xx = moments[0:1]
        on_xy = moments[1:2]
        on_yy = moments[2:3]
        on_x = moments[3:4]
        on_y = moments[4:5]
        on_one = moments[5:6]
        center_x = feat_ref[0:1, here]
        center_y = feat_ref[1:2, here]
        conic_xx = feat_ref[2:3, here]
        conic_xy = feat_ref[3:4, here]
        conic_yy = feat_ref[4:5, here]
        near_x = on_x - center_x * on_one
        near_y = on_y - center_y * on_one
        slope_ref[0:1, here] = conic_xx * near_x + conic_xy * near_y
        slope_ref[1:2, here] = conic_xy * near_x + conic_yy * near_y
        slope_ref[2:3, here] = -0.5 * (on_xx - center_x * (on_x + near_x))
        slope_ref[3:4, here] = -(on_xy - center_y * on_x - center_x * near_y)
        slope_ref[4:5, here] = -0.5 * (on_yy - center_y * (on_y + near_y))
        slope_ref[5:6, here] = on_one
        for channel in range(3):
            at = SUBS * channel
            both = tints[at : at + SUBS] + tints[at + 24 : at + 24 + SUBS]
            slope_ref[6 + channel : 7 + channel, here] = jnp.sum(
                jnp.where(same, both, 0.0), axis=0, keepdims=True
            )

    chunk = 512
    tops = peers * SUBS
    sum_ref[...] = jnp.zeros(sum_ref.shape, F32)
    pair_step = iota((2 * SUBS, chunk), 0) // SUBS

    def collect(index, carry):
        start = pl.multiple_of(index * chunk, chunk)
        slot = entry_ref[:, pl.ds(start, chunk)]
        within = slot & (half - 1)
        owner = slot >> 6
        hot = jnp.where((iota((LANES, chunk), 0) & (half - 1)) == within, 1.0, 0.0).astype(BF16)
        values = [
            piece.astype(F32) for piece in two_pieces(slope_ref[0:SUBS, pl.ds(start, chunk)])
        ]
        values = [jnp.concatenate([value, value], axis=0) for value in values]
        offset = jnp.broadcast_to(owner, (2 * SUBS, chunk)) - pair_step
        for place in range(peers // 2):
            hit = offset == 2 * place
            for number in range(2):
                at = number * (tops + peers) + place * 2 * SUBS
                mask_ref[at : at + 2 * SUBS, :] = jnp.where(hit, values[number], 0.0).astype(BF16)
        hit = iota((peers, chunk), 0) == owner
        for number, piece in enumerate(
            two_pieces(slope_ref[SUBS : SUBS + 1, pl.ds(start, chunk)])
        ):
            at = number * (tops + peers) + tops
            mask_ref[at : at + peers, :] = jnp.where(hit, piece.astype(F32), 0.0).astype(BF16)
        sum_ref[...] += dot_nt(mask_ref[...], hot)
        return carry

    lax.fori_loop(0, entries // chunk, collect, 0)
    lane_low = iota((SUBS, LANES), 1) < half
    for place in range(peers):
        at = place * SUBS
        eight = sum_ref[at : at + SUBS, :] + sum_ref[tops + peers + at : tops + peers + at + SUBS, :]
        at = tops + place
        ninth = sum_ref[at : at + 1, :] + sum_ref[tops + peers + at : tops + peers + at + 1, :]
        out_ref[place] = jnp.where(lane_low, eight, jnp.broadcast_to(ninth, (SUBS, LANES)))


def return_kernel(returned_ref, got_ref, jac_ref, cam_ref, grad_ref, row_ref, mask_ref, sum_ref, pack_ref):
    devices = got_ref.shape[0]
    count, own = grad_ref.shape
    high = own // LANES
    half = LANES // 2
    tops = high * SUBS
    part_rows = tops + high
    chunk = 4 * LANES
    cam = [[cam_ref[row, col] for col in range(3)] for row in range(3)]
    fill_numbers(got_ref, row_ref)
    sum_ref[...] = jnp.zeros(sum_ref.shape, F32)
    lane_low = iota((SUBS, LANES), 1) < half
    pair_step = iota((2 * SUBS, chunk), 0) // SUBS

    def collect(index, carry):
        numbers = row_ref[:, pl.ds(pl.multiple_of(index * chunk, chunk), chunk)]
        low = numbers & (LANES - 1)
        top = numbers >> 7
        hot = jnp.where(iota((LANES, chunk), 0) == low, 1.0, 0.0).astype(BF16)
        eights = []
        ninths = []
        for part in range(chunk // LANES):
            first = returned_ref[index * 8 + 2 * part]
            second = returned_ref[index * 8 + 2 * part + 1]
            eights.append(jnp.where(lane_low, first, pltpu.roll(second, half, 1)))
            ninths.append(jnp.where(lane_low, pltpu.roll(first, half, 1), second)[0:1])
        values = [piece.astype(F32) for piece in two_pieces(jnp.concatenate(eights, axis=1))]
        values = [jnp.concatenate([value, value], axis=0) for value in values]
        offset = jnp.broadcast_to(top, (2 * SUBS, chunk)) - pair_step
        for place in range(high // 2):
            hit = offset == 2 * place
            for number in range(2):
                at = number * part_rows + place * 2 * SUBS
                mask_ref[at : at + 2 * SUBS, :] = jnp.where(hit, values[number], 0.0).astype(BF16)
        hit = iota((high, chunk), 0) == top
        for number, piece in enumerate(two_pieces(jnp.concatenate(ninths, axis=1))):
            at = number * part_rows + tops
            mask_ref[at : at + high, :] = jnp.where(hit, piece.astype(F32), 0.0).astype(BF16)
        sum_ref[...] += dot_nt(mask_ref[...], hot)
        return carry

    lax.fori_loop(0, devices * half // chunk, collect, 0)

    def block(index, carry):
        start = pl.multiple_of(index * SUBS, SUBS)

        def jac(number):
            return jac_ref[pl.ds(number * high + start, SUBS), :]

        slopes = []
        for number in range(SUBS):
            at = start * SUBS + number
            slopes.append(
                sum_ref[pl.ds(at, SUBS, stride=SUBS), :]
                + sum_ref[pl.ds(part_rows + at, SUBS, stride=SUBS), :]
            )
        at = tops + start
        slopes.append(sum_ref[pl.ds(at, SUBS), :] + sum_ref[pl.ds(part_rows + at, SUBS), :])
        on_center = [slopes[0] * jac(30), slopes[1] * jac(31)]
        conic_xx = jac(48)
        conic_xy = jac(49)
        conic_yy = jac(50)
        on_xx, on_xy, on_yy = slopes[2:5]
        first_x = conic_xx * on_xx + conic_xy * on_xy
        first_y = conic_xy * on_xy + conic_yy * on_yy
        on_first = -(conic_xx * first_x + conic_xy * conic_xy * on_yy)
        on_second = -(conic_xy * conic_xy * on_xx + conic_yy * first_y)
        on_mixed = -(
            2.0 * conic_xx * conic_xy * on_xx
            + (conic_xx * conic_yy + conic_xy * conic_xy) * on_xy
            + 2.0 * conic_xy * conic_yy * on_yy
        )
        out = []
        for axis in range(3):
            out.append(
                cam[0][axis] * on_center[0]
                + cam[1][axis] * on_center[1]
                + slopes[6] * jac(21 + axis)
                + slopes[7] * jac(24 + axis)
                + slopes[8] * jac(27 + axis)
            )
        for number in range(7):
            out.append(
                on_first * jac(number) + on_mixed * jac(7 + number) + on_second * jac(14 + number)
            )
        out.append(slopes[5] * jac(32))
        for channel in range(3):
            out.append(SH_ZERO * slopes[6 + channel])
            for term in range(1, 16):
                out.append(slopes[6 + channel] * jac(32 + term))
        for number, value in enumerate(out):
            pack_ref[pl.ds(number * high + start, SUBS), :] = value
        return carry

    lax.fori_loop(0, high // SUBS, block, 0)
    for first in range(0, count, SUBS):
        number = min(SUBS, count - first)
        for place in range(high):
            grad_ref[first : first + number, place * LANES : (place + 1) * LANES] = pack_ref[
                pl.ds(first * high + place, number, stride=high), :
            ]


def band(outs, ins):
    taps = np.exp(-((np.arange(11) - 5.0) ** 2) / (2.0 * BLUR_SIGMA * BLUR_SIGMA))
    offset = np.asarray(ins)[None, :] - np.asarray(outs)[:, None]
    values = np.exp(-(offset**2) / (2.0 * BLUR_SIGMA * BLUR_SIGMA)) / taps.sum()
    return np.where(np.abs(offset) <= RIM, values, 0.0).astype(np.float32)


def monomials():
    pixel = np.arange(TILE * TILE)
    x = (pixel % TILE) - 7.5
    y = (pixel // TILE) - 7.5
    eight = np.stack([x * x, x * y, y * y, x, y, x * 0 + 1, x * 0, x * 0])
    return np.concatenate([eight, eight, eight, eight * 0]).astype(np.float32)


def call(body, out_shape, scratch, scalar_at, args, flops, outside=(), outs_outside=()):
    in_specs = [
        pl.BlockSpec(
            memory_space=pltpu.SMEM
            if number in scalar_at
            else pl.ANY
            if number in outside
            else pltpu.VMEM
        )
        for number in range(len(args))
    ]
    if isinstance(out_shape, tuple):
        out_specs = tuple(
            pl.BlockSpec(memory_space=pl.ANY if number in outs_outside else pltpu.VMEM)
            for number in range(len(out_shape))
        )
    else:
        out_specs = pl.BlockSpec(memory_space=pltpu.VMEM)
    return pl.pallas_call(
        body,
        out_shape=out_shape,
        in_specs=in_specs,
        out_specs=out_specs,
        scratch_shapes=scratch,
        compiler_params=pltpu.CompilerParams(vmem_limit_bytes=VMEM_BYTES),
        cost_estimate=pl.CostEstimate(flops=flops, bytes_accessed=1 << 20, transcendentals=0),
    )(*args)


def swap_pairs(count, first):
    pairs = []
    for low in range(first, count - 1, 2):
        pairs += [(low, low + 1), (low + 1, low)]
    return pairs


def swap(value_a, value_b, axis):
    count = lax.axis_size(axis)
    return (
        lax.ppermute(value_a, axis, swap_pairs(count, 0)),
        lax.ppermute(value_b, axis, swap_pairs(count, 1)),
    )


def exchange(payload):
    return lax.all_to_all(payload, ("img", "cell"), split_axis=0, concat_axis=0, tiled=True)


def shards(attributes, camera, target, visible_index, tile_lists, tile_len):
    img_count = lax.axis_size("img")
    cell_count = lax.axis_size("cell")
    devices = img_count * cell_count
    slots = visible_index.shape[1]
    per_owner = slots // devices
    count, own = attributes.shape
    high = own // LANES
    _, rows, cols = target.shape
    tiles_down, tiles_across, length = tile_lists.shape
    entries = tiles_down * tiles_across * length
    wide = cols + LANES
    mid = rows + 2 * SUBS
    tall = rows + 2 * HALO
    place = jnp.stack(
        [
            lax.axis_index("img"),
            lax.axis_index("cell"),
            jnp.int32(img_count),
            jnp.int32(cell_count),
        ]
    ).astype(jnp.int32)

    asked = visible_index.reshape(devices, per_owner)
    got = exchange(jnp.concatenate([asked, asked], axis=1))

    table, jac = call(
        owner_kernel,
        (
            jax.ShapeDtypeStruct((high * (SUBS + 1), 3 * LANES), BF16),
            jax.ShapeDtypeStruct((JAC_ROWS * high, LANES), F32),
        ),
        [pltpu.VMEM((count * high, LANES), F32), pltpu.VMEM((high * (SUBS + 1), LANES), F32)],
        (1,),
        (attributes, camera),
        1 << 24,
    )
    reply = call(
        reply_kernel,
        jax.ShapeDtypeStruct((devices, SUBS, LANES), F32),
        [pltpu.VMEM((1, slots), jnp.int32), pltpu.VMEM((high * (SUBS + 1), 2 * LANES), F32)],
        (),
        (table, got),
        1 << 24,
    )
    arrived = exchange(reply)

    order = (tiles_down, tiles_across // GROUP, GROUP, length)
    entry = tile_lists.reshape(order).transpose(0, 1, 3, 2).reshape(1, entries)
    live = jnp.arange(length, dtype=jnp.int32)[None, None, :, None] < tile_len.reshape(
        tiles_down, tiles_across // GROUP, 1, GROUP
    )
    bias = jnp.where(live, 0.0, -1e30).astype(F32).reshape(1, entries)
    mono = jnp.asarray(monomials()).astype(BF16)
    packed = 6 * rows // SUBS
    pixels = TILE * TILE
    group_rows = length * GROUP
    groups = entries // group_rows
    strip = jax.ShapeDtypeStruct((packed, LANES), F32)
    image, feat, alpha, weight, send_a, send_b = call(
        render_kernel,
        (
            jax.ShapeDtypeStruct((3, rows, cols), F32),
            jax.ShapeDtypeStruct((2 * SUBS, entries), F32),
            jax.ShapeDtypeStruct((entries, pixels), F32),
            jax.ShapeDtypeStruct((entries, 2 * pixels), BF16),
            strip,
            strip,
        ),
        [
            pltpu.VMEM((devices * (SUBS + 1), 512), F32),
            pltpu.VMEM((32, 512), F32),
            pltpu.VMEM((entries, pixels), F32),
            pltpu.VMEM((entries, 2 * pixels), BF16),
            pltpu.SemaphoreType.DMA((entries // 512,)),
            pltpu.SemaphoreType.DMA((4 * groups,)),
        ],
        (0,),
        (place, arrived, entry, bias, target, mono),
        1 << 26,
        outs_outside=(2, 3),
    )
    got_a, got_b = swap(send_a, send_b, "cell")
    edge = jax.ShapeDtypeStruct((6, HALO, wide), F32)
    side, send_a, send_b = call(
        strip_kernel,
        (jax.ShapeDtypeStruct((6, rows, LANES), F32), edge, edge),
        [],
        (0,),
        (place, got_a, got_b, image, target),
        1 << 20,
    )
    got_a, got_b = swap(send_a, send_b, "img")

    tall_at = np.arange(tall)
    tall_at = np.where(tall_at < rows + HALO, tall_at, tall_at - tall)
    mid_at = np.arange(mid) - SUBS
    wide_at = np.arange(wide)
    wide_at = np.where(wide_at < cols + LANES // 2, wide_at, wide_at - wide)
    down = jnp.asarray(band(mid_at, tall_at))
    down_back = jnp.asarray(band(np.arange(rows), mid_at))
    across = jnp.asarray(band(wide_at, wide_at))
    slot_grads = call(
        back_kernel,
        jax.ShapeDtypeStruct((devices, SUBS, LANES), F32),
        [
            pltpu.VMEM((6, tall, wide), F32),
            pltpu.VMEM((15 * mid, wide), F32),
            pltpu.VMEM((15 * mid, wide), F32),
            pltpu.VMEM((9 * rows, wide), F32),
            pltpu.VMEM((3, rows, cols), F32),
            pltpu.VMEM((entries, pixels), F32),
            pltpu.VMEM((entries, 2 * pixels), BF16),
            pltpu.VMEM((entries, pixels), F32),
            pltpu.VMEM((entries, 2 * pixels), BF16),
            pltpu.VMEM((groups * 6 * GROUP, 2 * pixels), F32),
            pltpu.VMEM((2 * SUBS, entries), F32),
            pltpu.VMEM((2 * devices * (SUBS + 1), 512), BF16),
            pltpu.VMEM((2 * devices * (SUBS + 1), LANES), F32),
            pltpu.SemaphoreType.DMA((2,)),
        ],
        (0,),
        (
            place, got_a, got_b, image, target, side, entry, feat, alpha, weight,
            down, down_back, across, mono,
        ),
        1 << 27,
        outside=(8, 9),
    )
    returned = exchange(slot_grads)
    return call(
        return_kernel,
        jax.ShapeDtypeStruct((count, own), F32),
        [
            pltpu.VMEM((1, slots), jnp.int32),
            pltpu.VMEM((2 * high * (SUBS + 1), 4 * LANES), BF16),
            pltpu.VMEM((2 * high * (SUBS + 1), LANES), F32),
            pltpu.VMEM((count * high, LANES), F32),
        ],
        (3,),
        (returned, got, jac, camera),
        1 << 26,
    )


def solution(mesh):
    return jax.shard_map(
        shards,
        mesh=mesh,
        in_specs=(
            P(None, ("img", "cell")),
            P(),
            P(None, "img", "cell"),
            P(("img", "cell"), None),
            P("img", "cell", None),
            P("img", "cell"),
        ),
        out_specs=P(None, ("img", "cell")),
        check_vma=False,
    )
```

```python
import functools
import math

import jax
import jax.numpy as jnp
import numpy as np
from jax import lax
from jax.experimental import pallas as pl
from jax.experimental.pallas import tpu as pltpu
from jax.sharding import PartitionSpec as P

TILE = 16
LANES = 128
SUBS = 8
GROUP = 8
RIM = 5
HALO = 16
WEIGHT_SSIM = 0.2
SMOOTHING = 0.01
STAB_ONE = 0.0001
STAB_TWO = 0.0009
BLUR_SIGMA = 1.5
LOG2E = 1.4426950408889634
SH_ZERO = 0.28209479177387814
SH_ONE = 0.4886025119029199
SH_TWO = (
    1.0925484305920792,
    -1.0925484305920792,
    0.31539156525252005,
    -1.0925484305920792,
    0.5462742152960396,
)
SH_THREE = (
    -0.5900435899266435,
    2.890611442640554,
    -0.4570457994644658,
    0.3731763325901154,
    -0.4570457994644658,
    1.445305721320277,
    -0.5900435899266435,
)
F32 = jnp.float32
BF16 = jnp.bfloat16
JAC_ROWS = 51
VMEM_BYTES = 56 * 1024 * 1024


def harmonic_basis(unit_x, unit_y, unit_z):
    unit_xx = unit_x * unit_x
    unit_yy = unit_y * unit_y
    unit_zz = unit_z * unit_z
    return [
        -SH_ONE * unit_y,
        SH_ONE * unit_z,
        -SH_ONE * unit_x,
        SH_TWO[0] * unit_x * unit_y,
        SH_TWO[1] * unit_y * unit_z,
        SH_TWO[2] * (2.0 * unit_zz - unit_xx - unit_yy),
        SH_TWO[3] * unit_x * unit_z,
        SH_TWO[4] * (unit_xx - unit_yy),
        SH_THREE[0] * unit_y * (3.0 * unit_xx - unit_yy),
        SH_THREE[1] * unit_x * unit_y * unit_z,
        SH_THREE[2] * unit_y * (4.0 * unit_zz - unit_xx - unit_yy),
        SH_THREE[3] * unit_z * (2.0 * unit_zz - 3.0 * unit_xx - 3.0 * unit_yy),
        SH_THREE[4] * unit_x * (4.0 * unit_zz - unit_xx - unit_yy),
        SH_THREE[5] * unit_z * (unit_xx - unit_yy),
        SH_THREE[6] * unit_x * (unit_xx - 3.0 * unit_yy),
    ]


def three_pieces(value):
    first = value.astype(BF16)
    rest = value - first.astype(F32)
    second = rest.astype(BF16)
    third = (rest - second.astype(F32)).astype(BF16)
    return first, second, third


def two_pieces(value):
    first = value.astype(BF16)
    return first, (value - first.astype(F32)).astype(BF16)


def dot(left, right):
    return jnp.dot(left, right, preferred_element_type=F32)


def dot_nt(left, right):
    return lax.dot_general(left, right, (((1,), (1,)), ((), ())), preferred_element_type=F32)


def dot_full(left, right):
    return jnp.dot(left, right, preferred_element_type=F32, precision=lax.Precision.HIGHEST)


def iota(shape, dim):
    return lax.broadcasted_iota(jnp.int32, shape, dim)


def block_transpose(block):
    turn = (iota(block.shape, 0) - iota(block.shape, 1) // TILE) & (SUBS - 1)
    out = block
    for step in range(1, SUBS):
        moved = pltpu.roll(block, LANES - TILE * step, 1)
        moved = pltpu.roll(moved, step, 0)
        out = jnp.where(turn == step, moved, out)
    return out


def covariance(scale_rows, quat_rows, cam):
    scales = [jnp.exp(row) for row in scale_rows]
    quat_w = 1.5 + jnp.tanh(quat_rows[0])
    quat_x, quat_y, quat_z = quat_rows[1:]
    inverse = lax.rsqrt(quat_w * quat_w + quat_x * quat_x + quat_y * quat_y + quat_z * quat_z)
    quat_w, quat_x, quat_y, quat_z = (
        quat_w * inverse,
        quat_x * inverse,
        quat_y * inverse,
        quat_z * inverse,
    )
    rotation = [
        [
            1.0 - 2.0 * (quat_y * quat_y + quat_z * quat_z),
            2.0 * (quat_x * quat_y - quat_w * quat_z),
            2.0 * (quat_x * quat_z + quat_w * quat_y),
        ],
        [
            2.0 * (quat_x * quat_y + quat_w * quat_z),
            1.0 - 2.0 * (quat_x * quat_x + quat_z * quat_z),
            2.0 * (quat_y * quat_z - quat_w * quat_x),
        ],
        [
            2.0 * (quat_x * quat_z - quat_w * quat_y),
            2.0 * (quat_y * quat_z + quat_w * quat_x),
            1.0 - 2.0 * (quat_x * quat_x + quat_y * quat_y),
        ],
    ]
    axes = [
        [
            (
                cam[screen][0] * rotation[0][axis]
                + cam[screen][1] * rotation[1][axis]
                + cam[screen][2] * rotation[2][axis]
            )
            * scales[axis]
            for axis in range(3)
        ]
        for screen in range(2)
    ]
    first = axes[0][0] * axes[0][0] + axes[0][1] * axes[0][1] + axes[0][2] * axes[0][2] + 0.3
    mixed = axes[0][0] * axes[1][0] + axes[0][1] * axes[1][1] + axes[0][2] * axes[1][2]
    second = axes[1][0] * axes[1][0] + axes[1][1] * axes[1][1] + axes[1][2] * axes[1][2] + 0.3
    return first, mixed, second


def owner_kernel(attr_ref, cam_ref, table_ref, jac_ref, pack_ref, feat_ref):
    count, own = attr_ref.shape
    high = own // LANES
    cam = [[cam_ref[row, col] for col in range(3)] for row in range(3)]
    for first in range(0, count, SUBS):
        number = min(SUBS, count - first)
        for place in range(high):
            pack_ref[pl.ds(first * high + place, number, stride=high), :] = attr_ref[
                first : first + number, place * LANES : (place + 1) * LANES
            ]

    def block(index, carry):
        start = pl.multiple_of(index * SUBS, SUBS)

        def row(number):
            return pack_ref[pl.ds(number * high + start, SUBS), :]

        positions = [row(number) for number in range(3)]
        shape_rows = [row(3 + number) for number in range(7)]
        jac = []
        (cov_first, cov_mixed, cov_second), pull = jax.vjp(
            lambda *rows: covariance(rows[:3], rows[3:], cam), *shape_rows
        )
        one = jnp.ones_like(cov_first)
        zero = jnp.zeros_like(cov_first)
        jac += pull((one, zero, zero))
        jac += pull((zero, one, zero))
        jac += pull((zero, zero, one))
        inverse = 1.0 / (cov_first * cov_second - cov_mixed * cov_mixed)
        conic = [cov_second * inverse, -cov_mixed * inverse, cov_first * inverse]
        centers = []
        slopes = []
        for screen in range(2):
            angle = (
                cam[screen][0] * positions[0]
                + cam[screen][1] * positions[1]
                + cam[screen][2] * positions[2]
            ) / 3.0
            centers.append(7.0 * jnp.sin(angle))
            slopes.append((7.0 / 3.0) * jnp.cos(angle))
        raw = row(10)
        decay = jnp.exp(-raw)
        log_opacity = -jnp.log(1.0 + decay)
        harmonics = [[row(11 + 16 * channel + term) for term in range(16)] for channel in range(3)]

        def colours_of(pos_x, pos_y, pos_z):
            off_x = pos_x - cam[2][0]
            off_y = pos_y - cam[2][1]
            off_z = pos_z - cam[2][2]
            scale = lax.rsqrt(off_x * off_x + off_y * off_y + off_z * off_z)
            basis = harmonic_basis(off_x * scale, off_y * scale, off_z * scale)
            colours = []
            for channel in range(3):
                total = 0.5 + SH_ZERO * harmonics[channel][0]
                for term in range(1, 16):
                    total = total + basis[term - 1] * harmonics[channel][term]
                colours.append(total)
            return tuple(colours), basis

        colours, pull_colours, basis = jax.vjp(colours_of, *positions, has_aux=True)
        jac += pull_colours((one, zero, zero))
        jac += pull_colours((zero, one, zero))
        jac += pull_colours((zero, zero, one))
        jac += slopes
        jac.append(decay / (1.0 + decay))
        jac += basis
        jac += conic
        for number, value in enumerate(jac):
            jac_ref[pl.ds(number * high + start, SUBS), :] = value
        features = centers + conic + [log_opacity] + list(colours)
        for number in range(SUBS):
            feat_ref[pl.ds(start * SUBS + number, SUBS, stride=SUBS), :] = features[number]
        feat_ref[pl.ds(high * SUBS + start, SUBS), :] = features[SUBS]
        return carry

    lax.fori_loop(0, high // SUBS, block, 0)
    for number, piece in enumerate(two_pieces(feat_ref[...])):
        table_ref[:, number * LANES : (number + 1) * LANES] = piece


def ask_kernel(index_ref, out_ref):
    for pair in range(out_ref.shape[0] // 2):
        numbers = index_ref[:, pair * LANES : (pair + 1) * LANES]
        out_ref[2 * pair : 2 * pair + 2, :] = jnp.broadcast_to(numbers, (2, LANES))


def fill_numbers(place_ref, got_ref, row_ref):
    lane_low = iota((1, LANES), 1) < LANES // 2
    odd = (place_ref[0] * place_ref[3] + place_ref[1]) % 2 == 1
    for pair in range(got_ref.shape[0] // 2):
        first = got_ref[2 * pair : 2 * pair + 1, :]
        second = got_ref[2 * pair + 1 : 2 * pair + 2, :]
        row_ref[:, pair * LANES : (pair + 1) * LANES] = jnp.where(
            odd,
            jnp.where(lane_low, pltpu.roll(first, LANES // 2, 1), second),
            jnp.where(lane_low, first, pltpu.roll(second, LANES // 2, 1)),
        )


def reply_kernel(place_ref, table_ref, got_in, out_ref, row_ref, wide_ref, got_ref, sems):
    got_copy = pltpu.make_async_copy(got_in, got_ref, sems.at[0])
    got_copy.start()
    got_copy.wait()
    devices = got_ref.shape[0]
    high = table_ref.shape[0] // (SUBS + 1)
    chunk = 2 * LANES
    half = LANES // 2
    fill_numbers(place_ref, got_ref, row_ref)

    def look(index, slot):
        numbers = row_ref[:, pl.ds(pl.multiple_of(index * chunk, chunk), chunk)]
        low = numbers & (LANES - 1)
        top = numbers >> 7
        hot = jnp.where(iota((LANES, chunk), 0) == low, 1.0, 0.0).astype(BF16)
        wide_ref[slot] = dot(table_ref[...], jnp.concatenate([hot, hot], axis=0))
        return top

    def pick(index, slot, top):
        spread = jnp.broadcast_to(top, (SUBS, chunk))
        picked = jnp.zeros((SUBS, chunk), F32)
        for place in range(high):
            picked = jnp.where(
                spread == place, wide_ref[slot, place * SUBS : (place + 1) * SUBS, :], picked
            )
        last = jnp.sum(
            jnp.where(iota((high, chunk), 0) == top, wide_ref[slot, high * SUBS :, :], 0.0),
            axis=0,
            keepdims=True,
        )
        lane_low = iota((SUBS, LANES), 1) < half
        for part in range(chunk // LANES):
            eight = picked[:, part * LANES : (part + 1) * LANES]
            ninth = jnp.broadcast_to(last[:, part * LANES : (part + 1) * LANES], (SUBS, LANES))
            peer = index * 4 + part * 2
            out_ref[peer] = jnp.where(lane_low, eight, pltpu.roll(ninth, half, 1))
            out_ref[peer + 1] = jnp.where(lane_low, pltpu.roll(eight, half, 1), ninth)

    def step(index, carry):
        tops = [look(2 * index + slot, slot) for slot in range(2)]
        for slot in range(2):
            pick(2 * index + slot, slot, tops[slot])
        return carry

    lax.fori_loop(0, devices // 8, step, 0)


def spread_colours(feat_ref, start, size):
    same = iota((GROUP, size), 0) == (iota((GROUP, size), 1) & (GROUP - 1))
    return jnp.concatenate(
        [
            jnp.where(same, feat_ref[6 + channel : 7 + channel, start : start + size], 0.0)
            for channel in range(3)
        ],
        axis=0,
    )


def render_kernel(
    place_ref, arrived_in, entry_ref, bias_ref, target_ref, mono_ref,
    image_ref, feat_ref, alpha_out, weight_out, send_a_ref, send_b_ref,
    wide_ref, coef_ref, alpha_ref, weight_ref, arrived_ref, alpha_sems, weight_sems, sems,
):
    arrived_copy = pltpu.make_async_copy(arrived_in, arrived_ref, sems.at[0])
    arrived_copy.start()
    arrived_copy.wait()
    peers = arrived_ref.shape[0]
    entries = entry_ref.shape[1]
    rows = image_ref.shape[1]
    across = image_ref.shape[2] // LANES
    groups = (rows // TILE) * across
    length = entries // (groups * GROUP)
    half = LANES // 2
    chunk = 512

    table = arrived_ref[...].reshape(peers * SUBS, LANES)
    ninth = arrived_ref[:, 0, :]
    low = iota((peers * SUBS, LANES), 1) < half
    low9 = iota((peers, LANES), 1) < half
    one, two, three = [piece.astype(F32) for piece in three_pieces(table)]
    one9, two9, three9 = [piece.astype(F32) for piece in three_pieces(ninth)]
    left = jnp.concatenate(
        [
            jnp.where(low, one, pltpu.roll(two, half, 1)),
            jnp.where(low9, pltpu.roll(two9, half, 1), one9),
        ],
        axis=0,
    ).astype(BF16)
    left_rest = jnp.concatenate(
        [jnp.where(low, three, 0.0), jnp.where(low9, 0.0, three9)], axis=0
    ).astype(BF16)
    left = jnp.concatenate([left, left_rest], axis=1)
    feat_ref[...] = jnp.zeros(feat_ref.shape, F32)
    coef_ref[...] = jnp.zeros(coef_ref.shape, F32)

    def alpha_copy(index):
        at = pl.ds(pl.multiple_of(index * chunk, chunk), chunk)
        return pltpu.make_async_copy(alpha_ref.at[at], alpha_out.at[at], alpha_sems.at[index])

    def look(index, slot_number):
        start = pl.multiple_of(index * chunk, chunk)
        slot = entry_ref[:, pl.ds(start, chunk)]
        within = slot & (half - 1)
        owner = slot >> 6
        hot = jnp.where((iota((LANES, chunk), 0) & (half - 1)) == within, 1.0, 0.0).astype(BF16)
        wide_ref[slot_number] = dot(left, jnp.concatenate([hot, hot], axis=0))
        return owner

    def gather(index, slot_number, owner):
        start = pl.multiple_of(index * chunk, chunk)
        spread = jnp.broadcast_to(owner, (SUBS, chunk))
        picked = jnp.zeros((SUBS, chunk), F32)
        for place in range(peers):
            picked = jnp.where(spread == place, wide_ref[slot_number, place * SUBS : (place + 1) * SUBS, :], picked)
        last = jnp.sum(
            jnp.where(iota((peers, chunk), 0) == owner, wide_ref[slot_number, peers * SUBS :, :], 0.0),
            axis=0,
            keepdims=True,
        )
        feat_ref[0:SUBS, pl.ds(start, chunk)] = picked
        feat_ref[SUBS : SUBS + 1, pl.ds(start, chunk)] = last
        center_x = picked[0:1]
        center_y = picked[1:2]
        conic_xx = picked[2:3]
        conic_xy = picked[3:4]
        conic_yy = picked[4:5]
        lin_x = conic_xx * center_x + conic_xy * center_y
        lin_y = conic_xy * center_x + conic_yy * center_y
        constant = picked[5:6] - 0.5 * (center_x * lin_x + center_y * lin_y)
        coef_ref[slot_number, 0:1] = (-0.5 * LOG2E) * conic_xx
        coef_ref[slot_number, 1:2] = -LOG2E * conic_xy
        coef_ref[slot_number, 2:3] = (-0.5 * LOG2E) * conic_yy
        coef_ref[slot_number, 3:4] = LOG2E * lin_x
        coef_ref[slot_number, 4:5] = LOG2E * lin_y
        coef_ref[slot_number, 5:6] = LOG2E * constant + bias_ref[:, pl.ds(start, chunk)]
        for number, piece in enumerate(three_pieces(coef_ref[slot_number, 0:SUBS])):
            coef_ref[slot_number, number * SUBS : (number + 1) * SUBS] = piece.astype(F32)
        columns = jnp.transpose(coef_ref[slot_number]).astype(BF16)
        alpha_ref[pl.ds(start, chunk), :] = jnp.exp2(dot(columns, mono_ref[...]))
        alpha_copy(index).start()

    def gather_two(index, carry):
        owners = [look(2 * index + number, number) for number in range(2)]
        for number in range(2):
            gather(2 * index + number, number, owners[number])
        return carry

    lax.fori_loop(0, entries // (2 * chunk), gather_two, 0)

    pixels = TILE * TILE
    step_rows = length * GROUP
    parts = 4
    part_rows = step_rows // parts

    def weight_copy(group, part):
        at = pl.ds(group * step_rows + part * part_rows, part_rows)
        return pltpu.make_async_copy(
            weight_ref.at[at], weight_out.at[at], weight_sems.at[group * parts + part]
        )

    def scan(number, keeps):
        new_keeps = []
        for group in range(groups):
            at = pl.ds(
                pl.multiple_of(group * step_rows + number * 2 * GROUP, 2 * GROUP), 2 * GROUP
            )
            alpha = alpha_ref[at, :]
            first = keeps[group] * alpha[0:GROUP]
            keep = keeps[group] - first
            second = keep * alpha[GROUP:]
            new_keeps.append(keep - second)
            high, rest = two_pieces(jnp.concatenate([first, second], axis=0))
            weight_ref[at, 0:pixels] = high
            weight_ref[at, pixels:] = rest
        return tuple(new_keeps)

    keeps = tuple(jnp.ones((GROUP, pixels), F32) for _ in range(groups))
    steps = length // (2 * parts)
    for part in range(parts):
        keeps = lax.fori_loop(part * steps, (part + 1) * steps, scan, keeps, unroll=4)
        for group in range(groups):
            weight_copy(group, part).start()
    for group in range(groups):
        here = slice(group * step_rows, (group + 1) * step_rows)
        left = jnp.concatenate(
            two_pieces(spread_colours(feat_ref, group * step_rows, step_rows)), axis=0
        )
        sums = dot(left, weight_ref[here, 0:pixels]) + dot(left, weight_ref[here, pixels:])
        row = (group // across) * TILE
        col = (group % across) * LANES
        for channel in range(3):
            at = channel * GROUP
            total = sums[at : at + GROUP] + sums[at + 3 * GROUP : at + 4 * GROUP]
            for part in range(2):
                image_ref[
                    channel, row + part * SUBS : row + (part + 1) * SUBS, col : col + LANES
                ] = block_transpose(total[:, part * LANES : (part + 1) * LANES])

    blocks = rows // SUBS
    lane_block = iota((SUBS, LANES), 1) // TILE
    even = place_ref[1] % 2 == 0
    for vector in range(6 * blocks // SUBS):
        at_left = jnp.zeros((SUBS, LANES), F32)
        at_right = jnp.zeros((SUBS, LANES), F32)
        for place in range(SUBS):
            number = vector * SUBS + place
            source = image_ref if number // blocks < 3 else target_ref
            channel = (number // blocks) % 3
            top = (number % blocks) * SUBS
            first = source[channel, top : top + SUBS, 0:LANES]
            final = source[channel, top : top + SUBS, (across - 1) * LANES :]
            if place:
                first = pltpu.roll(first, TILE * place, 1)
            if place != SUBS - 1:
                final = pltpu.roll(final, TILE * (place + 1), 1)
            at_left = jnp.where(lane_block == place, first, at_left)
            at_right = jnp.where(lane_block == place, final, at_right)
        send_a_ref[vector * SUBS : (vector + 1) * SUBS, :] = jnp.where(even, at_right, at_left)
        send_b_ref[vector * SUBS : (vector + 1) * SUBS, :] = jnp.where(even, at_left, at_right)
    for index in range(entries // chunk):
        alpha_copy(index).wait()
    for group in range(groups):
        for part in range(parts):
            weight_copy(group, part).wait()


def lane_shift(block, shift, axis=1):
    shift %= block.shape[axis]
    return pltpu.roll(block, shift, axis) if shift else block


def strip_kernel(
    place_ref, got_a_in, got_b_in, image_ref, target_ref, side_ref, send_a_ref, send_b_ref,
    got_a_ref, got_b_ref, sems,
):
    copies = [
        pltpu.make_async_copy(got_a_in, got_a_ref, sems.at[0]),
        pltpu.make_async_copy(got_b_in, got_b_ref, sems.at[1]),
    ]
    for copy in copies:
        copy.start()
    for copy in copies:
        copy.wait()
    rows = image_ref.shape[1]
    cols = image_ref.shape[2]
    blocks = rows // SUBS
    lane_block = iota((SUBS, LANES), 1) // TILE
    even = place_ref[1] % 2 == 0
    for vector in range(6 * blocks // SUBS):
        got_a = got_a_ref[vector * SUBS : (vector + 1) * SUBS, :]
        got_b = got_b_ref[vector * SUBS : (vector + 1) * SUBS, :]
        from_right = jnp.where(even, got_a, got_b)
        from_left = jnp.where(even, got_b, got_a)
        for place in range(SUBS):
            number = vector * SUBS + place
            right = lane_shift(from_right, -TILE * place)
            left = lane_shift(from_left, -TILE * (place + 1))
            top = (number % blocks) * SUBS
            side_ref[number // blocks, top : top + SUBS, :] = jnp.where(
                lane_block == 0, right, jnp.where(lane_block == SUBS - 1, left, 0.0)
            )

    def packed(main, rest, shift):
        wide_sub = iota((SUBS, cols), 0) // 2
        side_sub = iota((SUBS, LANES), 0) // 2
        wides = []
        sides = []
        for number in range(6):
            source = image_ref if number < 3 else target_ref
            wides.append(source[number % 3, main : main + SUBS, :])
            sides.append(side_ref[number, main : main + SUBS, :])
        for first in (0, 4):
            wide = jnp.zeros((SUBS, cols), F32)
            side = jnp.zeros((SUBS, LANES), F32)
            for number in range(first, min(first + 4, 6)):
                source = image_ref if number < 3 else target_ref
                turn = 2 * (number - first) - shift
                block = lane_shift(source[number % 3, rest : rest + SUBS, :], turn, 0)
                wide = jnp.where(wide_sub == number - first, block, wide)
                block = lane_shift(side_ref[number, rest : rest + SUBS, :], turn, 0)
                side = jnp.where(side_sub == number - first, block, side)
            wides.append(wide)
            sides.append(side)
        lane_part = iota((SUBS, LANES), 1) // (2 * TILE)
        last = []
        for first in (0, 4):
            total = jnp.zeros((SUBS, LANES), F32)
            for part in range(4):
                moved = lane_shift(sides[first + part], TILE + 2 * TILE * part)
                total = jnp.where(lane_part == part, moved, total)
            last.append(total)
        return wides, last

    even_row = place_ref[0] % 2 == 0
    top, top_last = packed(0, SUBS, 0)
    bottom, bottom_last = packed(rows - SUBS, rows - 2 * SUBS, 6)
    for number in range(SUBS):
        here = slice(number * SUBS, (number + 1) * SUBS)
        send_a_ref[here, :] = jnp.where(even_row, bottom[number], top[number])
        send_b_ref[here, :] = jnp.where(even_row, top[number], bottom[number])
    for number in range(2):
        here = slice(number * LANES, (number + 1) * LANES)
        send_a_ref[SUBS * SUBS :, here] = jnp.where(even_row, bottom_last[number], top_last[number])
        send_b_ref[SUBS * SUBS :, here] = jnp.where(even_row, top_last[number], bottom_last[number])


def back_kernel(
    place_ref, got_a_in, got_b_in, image_ref, target_ref, side_ref, entry_ref, feat_ref,
    alpha_in, weight_in, down_ref, down_back_ref, across_ref, mono_ref,
    out_ref,
    raw_ref, vert_ref, blur_ref, coef_ref, grad_ref, alpha_ref, weight_ref, ahead_ref, pair_ref,
    right_ref, slope_ref, mask_ref, sum_ref, got_a_ref, got_b_ref, sems,
):
    rows = image_ref.shape[1]
    cols = image_ref.shape[2]
    wide = cols + LANES
    entries = entry_ref.shape[1]
    across = cols // LANES
    groups = (rows // TILE) * across
    length = entries // (groups * GROUP)
    tall = rows + 2 * HALO
    mid = rows + 2 * SUBS
    peers = out_ref.shape[0]
    half = LANES // 2

    alpha_copy = pltpu.make_async_copy(alpha_in, alpha_ref, sems.at[0])
    weight_copy = pltpu.make_async_copy(weight_in, weight_ref, sems.at[1])
    got_copies = [
        pltpu.make_async_copy(got_a_in, got_a_ref, sems.at[2]),
        pltpu.make_async_copy(got_b_in, got_b_ref, sems.at[3]),
    ]
    for copy in got_copies:
        copy.start()
    alpha_copy.start()
    weight_copy.start()
    for copy in got_copies:
        copy.wait()
    even_row = place_ref[0] % 2 == 0
    for number in range(6):
        source = image_ref if number < 3 else target_ref
        raw_ref[number, 0:rows, 0:cols] = source[number % 3]
        raw_ref[number, 0:rows, cols:] = side_ref[number]
    lane_block = iota((SUBS, LANES), 1) // TILE
    border = (lane_block == 0) | (lane_block == SUBS - 1)
    for below in (True, False):
        def got(rows_here, cols_here):
            got_a = got_a_ref[rows_here, cols_here]
            got_b = got_b_ref[rows_here, cols_here]
            return jnp.where(even_row, got_a, got_b) if below else jnp.where(even_row, got_b, got_a)

        main_at = rows if below else tall - SUBS
        rest_at = rows + SUBS if below else tall - 2 * SUBS
        goal = 0 if below else 3
        wide_keep = iota((SUBS, cols), 0) // 2 == goal
        side_keep = iota((SUBS, LANES), 0) // 2 == goal
        wides = [got(slice(number * SUBS, (number + 1) * SUBS), slice(0, cols)) for number in range(SUBS)]
        lasts = [
            got(slice(SUBS * SUBS, (SUBS + 1) * SUBS), slice(number * LANES, (number + 1) * LANES))
            for number in range(2)
        ]
        sides = [
            jnp.where(border, lane_shift(lasts[number // 4], -TILE - 2 * TILE * (number % 4)), 0.0)
            for number in range(SUBS)
        ]
        for number in range(6):
            raw_ref[number, main_at : main_at + SUBS, 0:cols] = wides[number]
            raw_ref[number, main_at : main_at + SUBS, cols:] = sides[number]
            turn = 2 * (goal - number % 4)
            block = lane_shift(wides[6 + number // 4], turn, 0)
            raw_ref[number, rest_at : rest_at + SUBS, 0:cols] = jnp.where(wide_keep, block, 0.0)
            block = lane_shift(sides[6 + number // 4], turn, 0)
            raw_ref[number, rest_at : rest_at + SUBS, cols:] = jnp.where(side_keep, block, 0.0)
    down = down_ref[...]
    for channel in range(3):
        shown = raw_ref[channel]
        wanted = raw_ref[3 + channel]
        for number, value in enumerate(
            [shown, wanted, shown * shown + wanted * wanted, shown * wanted]
        ):
            at = (channel * 4 + number) * mid
            vert_ref[at : at + mid, :] = dot_full(down, value)
    for part in range(3):
        at = part * 4 * mid
        blur_ref[at : at + 4 * mid, :] = dot_full(vert_ref[at : at + 4 * mid, :], across_ref[...])
    line = iota((mid, wide), 0) - SUBS + place_ref[0] * rows
    spot = iota((mid, wide), 1)
    spot = jnp.where(spot < cols + half, spot, spot - wide) + place_ref[1] * cols
    inside = (
        (line >= 0) & (line < place_ref[2] * rows) & (spot >= 0) & (spot < place_ref[3] * cols)
    )
    down_back = down_back_ref[...]
    for channel in range(3):
        at = channel * 4 * mid
        mean_r, mean_t, squares, cross = [
            blur_ref[at + number * mid : at + (number + 1) * mid, :] for number in range(4)
        ]
        upper_one = 2.0 * mean_r * mean_t + STAB_ONE
        upper_two = 2.0 * (cross - mean_r * mean_t) + STAB_TWO
        lower_one = mean_r * mean_r + mean_t * mean_t + STAB_ONE
        lower_two = squares - mean_r * mean_r - mean_t * mean_t + STAB_TWO
        inv_one = 1.0 / lower_one
        inv_two = 1.0 / lower_two
        inverse = inv_one * inv_two
        value = upper_one * upper_two * inverse
        on_mean = (
            2.0 * mean_t * (upper_two - upper_one) * inverse
            + 2.0 * mean_r * value * (inv_two - inv_one)
        )
        on_square = -value * inv_two
        on_cross = 2.0 * upper_one * inverse
        for number, part in enumerate([on_mean, on_square, on_cross]):
            part = jnp.where(inside, -WEIGHT_SSIM * part, 0.0)
            spot_at = (channel * 3 + number) * rows
            coef_ref[spot_at : spot_at + rows, :] = dot_full(down_back, part)
    for channel in range(3):
        at = channel * 3 * rows
        back = dot_full(coef_ref[at : at + 3 * rows, :], across_ref[:, 0:cols])
        shown = image_ref[channel]
        wanted = target_ref[channel]
        gap = shown - wanted
        grad_ref[channel] = (
            (1.0 - WEIGHT_SSIM) * gap * lax.rsqrt(gap * gap + SMOOTHING * SMOOTHING)
            + back[0:rows]
            + 2.0 * shown * back[rows : 2 * rows]
            + wanted * back[2 * rows :]
        )

    pixels = TILE * TILE
    step_rows = length * GROUP
    mono = mono_ref[0 : 2 * SUBS, :]
    mono = jnp.concatenate([mono, mono], axis=1)
    same = iota((SUBS, step_rows), 0) == (iota((SUBS, step_rows), 1) & (GROUP - 1))
    slope_ref[...] = jnp.zeros(slope_ref.shape, F32)

    for group in range(groups):
        row = (group // across) * TILE
        col = (group % across) * LANES
        start = group * step_rows
        slopes = []
        for channel in range(3):
            for part in range(2):
                slopes.append(
                    block_transpose(
                        grad_ref[channel, row + part * SUBS : row + (part + 1) * SUBS, col : col + LANES]
                    )
                )
        slopes = jnp.concatenate(
            [jnp.concatenate(slopes[2 * channel : 2 * channel + 2], axis=1) for channel in range(3)],
            axis=0,
        )
        high, rest = [piece.astype(F32) for piece in two_pieces(slopes)]
        at = group * 6 * GROUP
        both = jnp.concatenate([high, rest], axis=0)
        right_ref[at : at + 6 * GROUP, 0:pixels] = both
        right_ref[at : at + 6 * GROUP, pixels:] = both
        top, low = [
            piece.astype(F32)
            for piece in two_pieces(spread_colours(feat_ref, start, step_rows))
        ]
        left = jnp.transpose(jnp.concatenate([top, low, top], axis=0)).astype(BF16)
        ahead_ref[start : start + step_rows, :] = dot(
            left, jnp.concatenate([high, high, rest], axis=0).astype(BF16)
        )

    alpha_copy.wait()
    weight_copy.wait()

    def step(number, behinds):
        new_behinds = []
        at = (length // 2 - 1 - number) * 2 * GROUP
        for group in range(groups):
            source = pl.ds(pl.multiple_of(group * step_rows + at, 2 * GROUP), 2 * GROUP)
            alpha = alpha_ref[source, :]
            ahead = ahead_ref[source, :]
            weight = weight_ref[source, 0:pixels].astype(F32) + weight_ref[source, pixels:].astype(F32)
            behind = behinds[group]
            second = ahead[GROUP:] - behind
            behind = behind + alpha[GROUP:] * second
            first = ahead[0:GROUP] - behind
            new_behinds.append(behind + alpha[0:GROUP] * first)
            high, rest = two_pieces(weight * jnp.concatenate([first, second], axis=0))
            pair_ref[source, 0:pixels] = high
            pair_ref[source, pixels:] = rest
        return tuple(new_behinds)

    zero = jnp.zeros((GROUP, pixels), F32)
    lax.fori_loop(0, length // 2, step, tuple(zero for _ in range(groups)), unroll=4)

    for group in range(groups):
        here = slice(group * step_rows, (group + 1) * step_rows)
        at = group * 6 * GROUP
        moments = dot_nt(mono, pair_ref[here, :])
        tints = dot_nt(right_ref[at : at + 6 * GROUP, :].astype(BF16), weight_ref[here, :])
        on_xx = moments[0:1]
        on_xy = moments[1:2]
        on_yy = moments[2:3]
        on_x = moments[3:4]
        on_y = moments[4:5]
        on_one = moments[5:6]
        center_x = feat_ref[0:1, here]
        center_y = feat_ref[1:2, here]
        conic_xx = feat_ref[2:3, here]
        conic_xy = feat_ref[3:4, here]
        conic_yy = feat_ref[4:5, here]
        near_x = on_x - center_x * on_one
        near_y = on_y - center_y * on_one
        slope_ref[0:1, here] = conic_xx * near_x + conic_xy * near_y
        slope_ref[1:2, here] = conic_xy * near_x + conic_yy * near_y
        slope_ref[2:3, here] = -0.5 * (on_xx - center_x * (on_x + near_x))
        slope_ref[3:4, here] = -(on_xy - center_y * on_x - center_x * near_y)
        slope_ref[4:5, here] = -0.5 * (on_yy - center_y * (on_y + near_y))
        slope_ref[5:6, here] = on_one
        for channel in range(3):
            at = SUBS * channel
            both = tints[at : at + SUBS] + tints[at + 24 : at + 24 + SUBS]
            slope_ref[6 + channel : 7 + channel, here] = jnp.sum(
                jnp.where(same, both, 0.0), axis=0, keepdims=True
            )

    chunk = 512
    tops = peers * SUBS
    sum_ref[...] = jnp.zeros(sum_ref.shape, F32)
    pair_step = iota((2 * SUBS, chunk), 0) // SUBS

    def collect(index, carry):
        start = pl.multiple_of(index * chunk, chunk)
        slot = entry_ref[:, pl.ds(start, chunk)]
        within = slot & (half - 1)
        owner = slot >> 6
        hot = jnp.where((iota((LANES, chunk), 0) & (half - 1)) == within, 1.0, 0.0).astype(BF16)
        values = [
            piece.astype(F32) for piece in two_pieces(slope_ref[0:SUBS, pl.ds(start, chunk)])
        ]
        values = [jnp.concatenate([value, value], axis=0) for value in values]
        offset = jnp.broadcast_to(owner, (2 * SUBS, chunk)) - pair_step
        for place in range(peers // 2):
            hit = offset == 2 * place
            for number in range(2):
                at = number * (tops + peers) + place * 2 * SUBS
                mask_ref[at : at + 2 * SUBS, :] = jnp.where(hit, values[number], 0.0).astype(BF16)
        hit = iota((peers, chunk), 0) == owner
        for number, piece in enumerate(
            two_pieces(slope_ref[SUBS : SUBS + 1, pl.ds(start, chunk)])
        ):
            at = number * (tops + peers) + tops
            mask_ref[at : at + peers, :] = jnp.where(hit, piece.astype(F32), 0.0).astype(BF16)
        sum_ref[...] += dot_nt(mask_ref[...], hot)
        return carry

    lax.fori_loop(0, entries // chunk, collect, 0)
    lane_low = iota((SUBS, LANES), 1) < half
    for place in range(peers):
        at = place * SUBS
        eight = sum_ref[at : at + SUBS, :] + sum_ref[tops + peers + at : tops + peers + at + SUBS, :]
        at = tops + place
        ninth = sum_ref[at : at + 1, :] + sum_ref[tops + peers + at : tops + peers + at + 1, :]
        out_ref[place] = jnp.where(lane_low, eight, jnp.broadcast_to(ninth, (SUBS, LANES)))


def return_kernel(place_ref, returned_ref, got_ref, jac_ref, cam_ref, grad_ref, row_ref, mask_ref, sum_ref, pack_ref):
    devices = got_ref.shape[0]
    count, own = grad_ref.shape
    high = own // LANES
    half = LANES // 2
    tops = high * SUBS
    part_rows = tops + high
    chunk = 4 * LANES
    cam = [[cam_ref[row, col] for col in range(3)] for row in range(3)]
    fill_numbers(place_ref, got_ref, row_ref)
    sum_ref[...] = jnp.zeros(sum_ref.shape, F32)
    lane_low = iota((SUBS, LANES), 1) < half
    pair_step = iota((2 * SUBS, chunk), 0) // SUBS

    def collect(index, carry):
        numbers = row_ref[:, pl.ds(pl.multiple_of(index * chunk, chunk), chunk)]
        low = numbers & (LANES - 1)
        top = numbers >> 7
        hot = jnp.where(iota((LANES, chunk), 0) == low, 1.0, 0.0).astype(BF16)
        eights = []
        ninths = []
        for part in range(chunk // LANES):
            first = returned_ref[index * 8 + 2 * part]
            second = returned_ref[index * 8 + 2 * part + 1]
            eights.append(jnp.where(lane_low, first, pltpu.roll(second, half, 1)))
            ninths.append(jnp.where(lane_low, pltpu.roll(first, half, 1), second)[0:1])
        values = [piece.astype(F32) for piece in two_pieces(jnp.concatenate(eights, axis=1))]
        values = [jnp.concatenate([value, value], axis=0) for value in values]
        offset = jnp.broadcast_to(top, (2 * SUBS, chunk)) - pair_step
        for place in range(high // 2):
            hit = offset == 2 * place
            for number in range(2):
                at = number * part_rows + place * 2 * SUBS
                mask_ref[at : at + 2 * SUBS, :] = jnp.where(hit, values[number], 0.0).astype(BF16)
        hit = iota((high, chunk), 0) == top
        for number, piece in enumerate(two_pieces(jnp.concatenate(ninths, axis=1))):
            at = number * part_rows + tops
            mask_ref[at : at + high, :] = jnp.where(hit, piece.astype(F32), 0.0).astype(BF16)
        sum_ref[...] += dot_nt(mask_ref[...], hot)
        return carry

    lax.fori_loop(0, devices * half // chunk, collect, 0)

    def block(index, carry):
        start = pl.multiple_of(index * SUBS, SUBS)

        def jac(number):
            return jac_ref[pl.ds(number * high + start, SUBS), :]

        slopes = []
        for number in range(SUBS):
            at = start * SUBS + number
            slopes.append(
                sum_ref[pl.ds(at, SUBS, stride=SUBS), :]
                + sum_ref[pl.ds(part_rows + at, SUBS, stride=SUBS), :]
            )
        at = tops + start
        slopes.append(sum_ref[pl.ds(at, SUBS), :] + sum_ref[pl.ds(part_rows + at, SUBS), :])
        on_center = [slopes[0] * jac(30), slopes[1] * jac(31)]
        conic_xx = jac(48)
        conic_xy = jac(49)
        conic_yy = jac(50)
        on_xx, on_xy, on_yy = slopes[2:5]
        first_x = conic_xx * on_xx + conic_xy * on_xy
        first_y = conic_xy * on_xy + conic_yy * on_yy
        on_first = -(conic_xx * first_x + conic_xy * conic_xy * on_yy)
        on_second = -(conic_xy * conic_xy * on_xx + conic_yy * first_y)
        on_mixed = -(
            2.0 * conic_xx * conic_xy * on_xx
            + (conic_xx * conic_yy + conic_xy * conic_xy) * on_xy
            + 2.0 * conic_xy * conic_yy * on_yy
        )
        out = []
        for axis in range(3):
            out.append(
                cam[0][axis] * on_center[0]
                + cam[1][axis] * on_center[1]
                + slopes[6] * jac(21 + axis)
                + slopes[7] * jac(24 + axis)
                + slopes[8] * jac(27 + axis)
            )
        for number in range(7):
            out.append(
                on_first * jac(number) + on_mixed * jac(7 + number) + on_second * jac(14 + number)
            )
        out.append(slopes[5] * jac(32))
        for channel in range(3):
            out.append(SH_ZERO * slopes[6 + channel])
            for term in range(1, 16):
                out.append(slopes[6 + channel] * jac(32 + term))
        for number, value in enumerate(out):
            pack_ref[pl.ds(number * high + start, SUBS), :] = value
        return carry

    lax.fori_loop(0, high // SUBS, block, 0)
    for first in range(0, count, SUBS):
        number = min(SUBS, count - first)
        for place in range(high):
            grad_ref[first : first + number, place * LANES : (place + 1) * LANES] = pack_ref[
                pl.ds(first * high + place, number, stride=high), :
            ]


def band(outs, ins):
    taps = np.exp(-((np.arange(11) - 5.0) ** 2) / (2.0 * BLUR_SIGMA * BLUR_SIGMA))
    offset = np.asarray(ins)[None, :] - np.asarray(outs)[:, None]
    values = np.exp(-(offset**2) / (2.0 * BLUR_SIGMA * BLUR_SIGMA)) / taps.sum()
    return np.where(np.abs(offset) <= RIM, values, 0.0).astype(np.float32)


def monomials():
    pixel = np.arange(TILE * TILE)
    x = (pixel % TILE) - 7.5
    y = (pixel // TILE) - 7.5
    eight = np.stack([x * x, x * y, y * y, x, y, x * 0 + 1, x * 0, x * 0])
    return np.concatenate([eight, eight, eight, eight * 0]).astype(np.float32)


def call(body, out_shape, scratch, scalar_at, args, flops, outside=(), outs_outside=()):
    in_specs = [
        pl.BlockSpec(
            memory_space=pltpu.SMEM
            if number in scalar_at
            else pl.ANY
            if number in outside
            else pltpu.VMEM
        )
        for number in range(len(args))
    ]
    if isinstance(out_shape, tuple):
        out_specs = tuple(
            pl.BlockSpec(memory_space=pl.ANY if number in outs_outside else pltpu.VMEM)
            for number in range(len(out_shape))
        )
    else:
        out_specs = pl.BlockSpec(memory_space=pltpu.VMEM)
    return pl.pallas_call(
        body,
        out_shape=out_shape,
        in_specs=in_specs,
        out_specs=out_specs,
        scratch_shapes=scratch,
        compiler_params=pltpu.CompilerParams(vmem_limit_bytes=VMEM_BYTES),
        cost_estimate=pl.CostEstimate(flops=flops, bytes_accessed=1 << 20, transcendentals=0),
    )(*args)


def swap_pairs(count, first):
    pairs = []
    for low in range(first, count - 1, 2):
        pairs += [(low, low + 1), (low + 1, low)]
    return pairs


def swap(value_a, value_b, axis):
    count = lax.axis_size(axis)
    return (
        lax.ppermute(value_a, axis, swap_pairs(count, 0)),
        lax.ppermute(value_b, axis, swap_pairs(count, 1)),
    )


def exchange(payload):
    return lax.all_to_all(payload, ("img", "cell"), split_axis=0, concat_axis=0, tiled=True)


def shards(attributes, camera, target, visible_index, tile_lists, tile_len):
    img_count = lax.axis_size("img")
    cell_count = lax.axis_size("cell")
    devices = img_count * cell_count
    slots = visible_index.shape[1]
    count, own = attributes.shape
    high = own // LANES
    _, rows, cols = target.shape
    tiles_down, tiles_across, length = tile_lists.shape
    entries = tiles_down * tiles_across * length
    wide = cols + LANES
    mid = rows + 2 * SUBS
    tall = rows + 2 * HALO
    place = jnp.stack(
        [
            lax.axis_index("img"),
            lax.axis_index("cell"),
            jnp.int32(img_count),
            jnp.int32(cell_count),
        ]
    ).astype(jnp.int32)

    assert 2 * (slots // devices) == LANES
    asked = call(
        ask_kernel,
        jax.ShapeDtypeStruct((devices, LANES), jnp.int32),
        [],
        (),
        (visible_index,),
        1 << 14,
    )
    got = exchange(asked)

    table, jac = call(
        owner_kernel,
        (
            jax.ShapeDtypeStruct((high * (SUBS + 1), 2 * LANES), BF16),
            jax.ShapeDtypeStruct((JAC_ROWS * high, LANES), F32),
        ),
        [pltpu.VMEM((count * high, LANES), F32), pltpu.VMEM((high * (SUBS + 1), LANES), F32)],
        (1,),
        (attributes, camera),
        1 << 24,
    )
    reply = call(
        reply_kernel,
        jax.ShapeDtypeStruct((devices, SUBS, LANES), F32),
        [
            pltpu.VMEM((1, slots), jnp.int32),
            pltpu.VMEM((2, high * (SUBS + 1), 2 * LANES), F32),
            pltpu.VMEM((devices, LANES), jnp.int32),
            pltpu.SemaphoreType.DMA((1,)),
        ],
        (0,),
        (place, table, got),
        1 << 24,
        outside=(2,),
    )
    arrived = exchange(reply)

    order = (tiles_down, tiles_across // GROUP, GROUP, length)
    entry = tile_lists.reshape(order).transpose(0, 1, 3, 2).reshape(1, entries)
    live = jnp.arange(length, dtype=jnp.int32)[None, None, :, None] < tile_len.reshape(
        tiles_down, tiles_across // GROUP, 1, GROUP
    )
    bias = jnp.where(live, 0.0, -1e30).astype(F32).reshape(1, entries)
    mono = jnp.asarray(monomials()).astype(BF16)
    packed = 6 * rows // SUBS
    pixels = TILE * TILE
    group_rows = length * GROUP
    groups = entries // group_rows
    strip = jax.ShapeDtypeStruct((packed, LANES), F32)
    image, feat, alpha, weight, send_a, send_b = call(
        render_kernel,
        (
            jax.ShapeDtypeStruct((3, rows, cols), F32),
            jax.ShapeDtypeStruct((2 * SUBS, entries), F32),
            jax.ShapeDtypeStruct((entries, pixels), F32),
            jax.ShapeDtypeStruct((entries, 2 * pixels), BF16),
            strip,
            strip,
        ),
        [
            pltpu.VMEM((2, devices * (SUBS + 1), 512), F32),
            pltpu.VMEM((2, 32, 512), F32),
            pltpu.VMEM((entries, pixels), F32),
            pltpu.VMEM((entries, 2 * pixels), BF16),
            pltpu.VMEM((devices, SUBS, LANES), F32),
            pltpu.SemaphoreType.DMA((entries // 512,)),
            pltpu.SemaphoreType.DMA((4 * groups,)),
            pltpu.SemaphoreType.DMA((1,)),
        ],
        (0,),
        (place, arrived, entry, bias, target, mono),
        1 << 26,
        outside=(1,),
        outs_outside=(2, 3),
    )
    got_a, got_b = swap(send_a, send_b, "cell")
    edge = jax.ShapeDtypeStruct(((SUBS + 1) * SUBS, cols), F32)
    side, send_a, send_b = call(
        strip_kernel,
        (jax.ShapeDtypeStruct((6, rows, LANES), F32), edge, edge),
        [
            pltpu.VMEM((packed, LANES), F32),
            pltpu.VMEM((packed, LANES), F32),
            pltpu.SemaphoreType.DMA((2,)),
        ],
        (0,),
        (place, got_a, got_b, image, target),
        1 << 20,
        outside=(1, 2),
    )
    got_a, got_b = swap(send_a, send_b, "img")

    tall_at = np.arange(tall)
    tall_at = np.where(tall_at < rows + HALO, tall_at, tall_at - tall)
    mid_at = np.arange(mid) - SUBS
    wide_at = np.arange(wide)
    wide_at = np.where(wide_at < cols + LANES // 2, wide_at, wide_at - wide)
    down = jnp.asarray(band(mid_at, tall_at))
    down_back = jnp.asarray(band(np.arange(rows), mid_at))
    across = jnp.asarray(band(wide_at, wide_at))
    slot_grads = call(
        back_kernel,
        jax.ShapeDtypeStruct((devices, SUBS, LANES), F32),
        [
            pltpu.VMEM((6, tall, wide), F32),
            pltpu.VMEM((12 * mid, wide), F32),
            pltpu.VMEM((12 * mid, wide), F32),
            pltpu.VMEM((9 * rows, wide), F32),
            pltpu.VMEM((3, rows, cols), F32),
            pltpu.VMEM((entries, pixels), F32),
            pltpu.VMEM((entries, 2 * pixels), BF16),
            pltpu.VMEM((entries, pixels), F32),
            pltpu.VMEM((entries, 2 * pixels), BF16),
            pltpu.VMEM((groups * 6 * GROUP, 2 * pixels), F32),
            pltpu.VMEM((2 * SUBS, entries), F32),
            pltpu.VMEM((2 * devices * (SUBS + 1), 512), BF16),
            pltpu.VMEM((2 * devices * (SUBS + 1), LANES), F32),
            pltpu.VMEM(((SUBS + 1) * SUBS, cols), F32),
            pltpu.VMEM(((SUBS + 1) * SUBS, cols), F32),
            pltpu.SemaphoreType.DMA((4,)),
        ],
        (0,),
        (
            place, got_a, got_b, image, target, side, entry, feat, alpha, weight,
            down, down_back, across, mono,
        ),
        1 << 27,
        outside=(1, 2, 8, 9),
    )
    returned = exchange(slot_grads)
    return call(
        return_kernel,
        jax.ShapeDtypeStruct((count, own), F32),
        [
            pltpu.VMEM((1, slots), jnp.int32),
            pltpu.VMEM((2 * high * (SUBS + 1), 4 * LANES), BF16),
            pltpu.VMEM((2 * high * (SUBS + 1), LANES), F32),
            pltpu.VMEM((count * high, LANES), F32),
        ],
        (0, 4),
        (place, returned, got, jac, camera),
        1 << 26,
    )


def solution(mesh):
    return jax.shard_map(
        shards,
        mesh=mesh,
        in_specs=(
            P(None, ("img", "cell")),
            P(),
            P(None, "img", "cell"),
            P(("img", "cell"), None),
            P("img", "cell", None),
            P("img", "cell"),
        ),
        out_specs=P(None, ("img", "cell")),
        check_vma=False,
    )
```

```python
import functools
import math

import jax
import jax.numpy as jnp
import numpy as np
from jax import lax
from jax.experimental import pallas as pl
from jax.experimental.pallas import tpu as pltpu
from jax.sharding import PartitionSpec as P

TILE = 16
LANES = 128
SUBS = 8
GROUP = 8
RIM = 5
HALO = 16
WEIGHT_SSIM = 0.2
SMOOTHING = 0.01
STAB_ONE = 0.0001
STAB_TWO = 0.0009
BLUR_SIGMA = 1.5
LOG2E = 1.4426950408889634
SH_ZERO = 0.28209479177387814
SH_ONE = 0.4886025119029199
SH_TWO = (
    1.0925484305920792,
    -1.0925484305920792,
    0.31539156525252005,
    -1.0925484305920792,
    0.5462742152960396,
)
SH_THREE = (
    -0.5900435899266435,
    2.890611442640554,
    -0.4570457994644658,
    0.3731763325901154,
    -0.4570457994644658,
    1.445305721320277,
    -0.5900435899266435,
)
F32 = jnp.float32
BF16 = jnp.bfloat16
JAC_ROWS = 51
MIB = 1024 * 1024


def harmonic_basis(unit_x, unit_y, unit_z):
    unit_xx = unit_x * unit_x
    unit_yy = unit_y * unit_y
    unit_zz = unit_z * unit_z
    return [
        -SH_ONE * unit_y,
        SH_ONE * unit_z,
        -SH_ONE * unit_x,
        SH_TWO[0] * unit_x * unit_y,
        SH_TWO[1] * unit_y * unit_z,
        SH_TWO[2] * (2.0 * unit_zz - unit_xx - unit_yy),
        SH_TWO[3] * unit_x * unit_z,
        SH_TWO[4] * (unit_xx - unit_yy),
        SH_THREE[0] * unit_y * (3.0 * unit_xx - unit_yy),
        SH_THREE[1] * unit_x * unit_y * unit_z,
        SH_THREE[2] * unit_y * (4.0 * unit_zz - unit_xx - unit_yy),
        SH_THREE[3] * unit_z * (2.0 * unit_zz - 3.0 * unit_xx - 3.0 * unit_yy),
        SH_THREE[4] * unit_x * (4.0 * unit_zz - unit_xx - unit_yy),
        SH_THREE[5] * unit_z * (unit_xx - unit_yy),
        SH_THREE[6] * unit_x * (unit_xx - 3.0 * unit_yy),
    ]


def three_pieces(value):
    first = value.astype(BF16)
    rest = value - first.astype(F32)
    second = rest.astype(BF16)
    third = (rest - second.astype(F32)).astype(BF16)
    return first, second, third


def two_pieces(value):
    first = value.astype(BF16)
    return first, (value - first.astype(F32)).astype(BF16)


def dot(left, right):
    return jnp.dot(left, right, preferred_element_type=F32)


def dot_nt(left, right):
    return lax.dot_general(left, right, (((1,), (1,)), ((), ())), preferred_element_type=F32)


def dot_full(left, right):
    return jnp.dot(left, right, preferred_element_type=F32, precision=lax.Precision.HIGHEST)


def iota(shape, dim):
    return lax.broadcasted_iota(jnp.int32, shape, dim)


def block_transpose(block):
    turn = (iota(block.shape, 0) - iota(block.shape, 1) // TILE) & (SUBS - 1)
    out = block
    for step in range(1, SUBS):
        moved = pltpu.roll(block, LANES - TILE * step, 1)
        moved = pltpu.roll(moved, step, 0)
        out = jnp.where(turn == step, moved, out)
    return out


def covariance(scale_rows, quat_rows, cam):
    scales = [jnp.exp(row) for row in scale_rows]
    quat_w = 1.5 + jnp.tanh(quat_rows[0])
    quat_x, quat_y, quat_z = quat_rows[1:]
    inverse = lax.rsqrt(quat_w * quat_w + quat_x * quat_x + quat_y * quat_y + quat_z * quat_z)
    quat_w, quat_x, quat_y, quat_z = (
        quat_w * inverse,
        quat_x * inverse,
        quat_y * inverse,
        quat_z * inverse,
    )
    rotation = [
        [
            1.0 - 2.0 * (quat_y * quat_y + quat_z * quat_z),
            2.0 * (quat_x * quat_y - quat_w * quat_z),
            2.0 * (quat_x * quat_z + quat_w * quat_y),
        ],
        [
            2.0 * (quat_x * quat_y + quat_w * quat_z),
            1.0 - 2.0 * (quat_x * quat_x + quat_z * quat_z),
            2.0 * (quat_y * quat_z - quat_w * quat_x),
        ],
        [
            2.0 * (quat_x * quat_z - quat_w * quat_y),
            2.0 * (quat_y * quat_z + quat_w * quat_x),
            1.0 - 2.0 * (quat_x * quat_x + quat_y * quat_y),
        ],
    ]
    axes = [
        [
            (
                cam[screen][0] * rotation[0][axis]
                + cam[screen][1] * rotation[1][axis]
                + cam[screen][2] * rotation[2][axis]
            )
            * scales[axis]
            for axis in range(3)
        ]
        for screen in range(2)
    ]
    first = axes[0][0] * axes[0][0] + axes[0][1] * axes[0][1] + axes[0][2] * axes[0][2] + 0.3
    mixed = axes[0][0] * axes[1][0] + axes[0][1] * axes[1][1] + axes[0][2] * axes[1][2]
    second = axes[1][0] * axes[1][0] + axes[1][1] * axes[1][1] + axes[1][2] * axes[1][2] + 0.3
    return first, mixed, second


def owner_kernel(attr_ref, cam_ref, table_ref, jac_ref, pack_ref, feat_ref):
    count, own = attr_ref.shape
    high = own // LANES
    cam = [[cam_ref[row, col] for col in range(3)] for row in range(3)]
    for first in range(0, count, SUBS):
        number = min(SUBS, count - first)
        for place in range(high):
            pack_ref[pl.ds(first * high + place, number, stride=high), :] = attr_ref[
                first : first + number, place * LANES : (place + 1) * LANES
            ]

    def block(index, carry):
        start = pl.multiple_of(index * SUBS, SUBS)

        def row(number):
            return pack_ref[pl.ds(number * high + start, SUBS), :]

        positions = [row(number) for number in range(3)]
        shape_rows = [row(3 + number) for number in range(7)]
        jac = []
        (cov_first, cov_mixed, cov_second), pull = jax.vjp(
            lambda *rows: covariance(rows[:3], rows[3:], cam), *shape_rows
        )
        one = jnp.ones_like(cov_first)
        zero = jnp.zeros_like(cov_first)
        jac += pull((one, zero, zero))
        jac += pull((zero, one, zero))
        jac += pull((zero, zero, one))
        inverse = 1.0 / (cov_first * cov_second - cov_mixed * cov_mixed)
        conic = [cov_second * inverse, -cov_mixed * inverse, cov_first * inverse]
        centers = []
        slopes = []
        for screen in range(2):
            angle = (
                cam[screen][0] * positions[0]
                + cam[screen][1] * positions[1]
                + cam[screen][2] * positions[2]
            ) / 3.0
            centers.append(7.0 * jnp.sin(angle))
            slopes.append((7.0 / 3.0) * jnp.cos(angle))
        raw = row(10)
        decay = jnp.exp(-raw)
        log_opacity = -jnp.log(1.0 + decay)
        harmonics = [[row(11 + 16 * channel + term) for term in range(16)] for channel in range(3)]

        def colours_of(pos_x, pos_y, pos_z):
            off_x = pos_x - cam[2][0]
            off_y = pos_y - cam[2][1]
            off_z = pos_z - cam[2][2]
            scale = lax.rsqrt(off_x * off_x + off_y * off_y + off_z * off_z)
            basis = harmonic_basis(off_x * scale, off_y * scale, off_z * scale)
            colours = []
            for channel in range(3):
                total = 0.5 + SH_ZERO * harmonics[channel][0]
                for term in range(1, 16):
                    total = total + basis[term - 1] * harmonics[channel][term]
                colours.append(total)
            return tuple(colours), basis

        colours, pull_colours, basis = jax.vjp(colours_of, *positions, has_aux=True)
        jac += pull_colours((one, zero, zero))
        jac += pull_colours((zero, one, zero))
        jac += pull_colours((zero, zero, one))
        jac += slopes
        jac.append(decay / (1.0 + decay))
        jac += basis
        jac += conic
        for number, value in enumerate(jac):
            jac_ref[pl.ds(number * high + start, SUBS), :] = value
        features = centers + conic + [log_opacity] + list(colours)
        for number in range(SUBS):
            feat_ref[pl.ds(start * SUBS + number, SUBS, stride=SUBS), :] = features[number]
        feat_ref[pl.ds(high * SUBS + start, SUBS), :] = features[SUBS]
        return carry

    lax.fori_loop(0, high // SUBS, block, 0)
    for number, piece in enumerate(two_pieces(feat_ref[...])):
        table_ref[:, number * LANES : (number + 1) * LANES] = piece


def ask_kernel(index_ref, out_ref):
    for pair in range(out_ref.shape[0] // 2):
        numbers = index_ref[:, pair * LANES : (pair + 1) * LANES]
        out_ref[2 * pair : 2 * pair + 2, :] = jnp.broadcast_to(numbers, (2, LANES))


def fill_numbers(place_ref, got_ref, row_ref):
    lane_low = iota((1, LANES), 1) < LANES // 2
    odd = (place_ref[0] * place_ref[3] + place_ref[1]) % 2 == 1
    for pair in range(got_ref.shape[0] // 2):
        first = got_ref[2 * pair : 2 * pair + 1, :]
        second = got_ref[2 * pair + 1 : 2 * pair + 2, :]
        row_ref[:, pair * LANES : (pair + 1) * LANES] = jnp.where(
            odd,
            jnp.where(lane_low, pltpu.roll(first, LANES // 2, 1), second),
            jnp.where(lane_low, first, pltpu.roll(second, LANES // 2, 1)),
        )


def reply_kernel(place_ref, table_ref, got_in, out_ref, row_ref, wide_ref, got_ref, sems):
    got_copy = pltpu.make_async_copy(got_in, got_ref, sems.at[0])
    got_copy.start()
    got_copy.wait()
    devices = got_ref.shape[0]
    high = table_ref.shape[0] // (SUBS + 1)
    chunk = 2 * LANES
    half = LANES // 2
    fill_numbers(place_ref, got_ref, row_ref)

    def look(index, slot):
        numbers = row_ref[:, pl.ds(pl.multiple_of(index * chunk, chunk), chunk)]
        low = numbers & (LANES - 1)
        top = numbers >> 7
        hot = jnp.where(iota((LANES, chunk), 0) == low, 1.0, 0.0).astype(BF16)
        wide_ref[slot] = dot(table_ref[...], jnp.concatenate([hot, hot], axis=0))
        return top

    def pick(index, slot, top):
        spread = jnp.broadcast_to(top, (SUBS, chunk))
        picked = jnp.zeros((SUBS, chunk), F32)
        for place in range(high):
            picked = jnp.where(
                spread == place, wide_ref[slot, place * SUBS : (place + 1) * SUBS, :], picked
            )
        last = jnp.sum(
            jnp.where(iota((high, chunk), 0) == top, wide_ref[slot, high * SUBS :, :], 0.0),
            axis=0,
            keepdims=True,
        )
        lane_low = iota((SUBS, LANES), 1) < half
        for part in range(chunk // LANES):
            eight = picked[:, part * LANES : (part + 1) * LANES]
            ninth = jnp.broadcast_to(last[:, part * LANES : (part + 1) * LANES], (SUBS, LANES))
            peer = index * 4 + part * 2
            out_ref[peer] = jnp.where(lane_low, eight, pltpu.roll(ninth, half, 1))
            out_ref[peer + 1] = jnp.where(lane_low, pltpu.roll(eight, half, 1), ninth)

    def step(index, carry):
        tops = [look(2 * index + slot, slot) for slot in range(2)]
        for slot in range(2):
            pick(2 * index + slot, slot, tops[slot])
        return carry

    lax.fori_loop(0, devices // 8, step, 0)


def spread_colours(feat_ref, start, size):
    same = iota((GROUP, size), 0) == (iota((GROUP, size), 1) & (GROUP - 1))
    return jnp.concatenate(
        [
            jnp.where(same, feat_ref[6 + channel : 7 + channel, start : start + size], 0.0)
            for channel in range(3)
        ],
        axis=0,
    )


def render_kernel(
    place_ref, arrived_in, entry_ref, bias_ref, target_ref, mono_ref,
    image_ref, feat_ref, alpha_out, weight_out, send_a_ref, send_b_ref,
    wide_ref, coef_ref, alpha_ref, weight_ref, arrived_ref, alpha_sems, weight_sems, sems,
):
    arrived_copy = pltpu.make_async_copy(arrived_in, arrived_ref, sems.at[0])
    arrived_copy.start()
    arrived_copy.wait()
    peers = arrived_ref.shape[0]
    entries = entry_ref.shape[1]
    rows = image_ref.shape[1]
    across = image_ref.shape[2] // LANES
    groups = (rows // TILE) * across
    length = entries // (groups * GROUP)
    half = LANES // 2
    chunk = 512

    table = arrived_ref[...].reshape(peers * SUBS, LANES)
    ninth = arrived_ref[:, 0, :]
    low = iota((peers * SUBS, LANES), 1) < half
    low9 = iota((peers, LANES), 1) < half
    one, two, three = [piece.astype(F32) for piece in three_pieces(table)]
    one9, two9, three9 = [piece.astype(F32) for piece in three_pieces(ninth)]
    left = jnp.concatenate(
        [
            jnp.where(low, one, pltpu.roll(two, half, 1)),
            jnp.where(low9, pltpu.roll(two9, half, 1), one9),
        ],
        axis=0,
    ).astype(BF16)
    left_rest = jnp.concatenate(
        [jnp.where(low, three, 0.0), jnp.where(low9, 0.0, three9)], axis=0
    ).astype(BF16)
    left = jnp.concatenate([left, left_rest], axis=1)
    feat_ref[...] = jnp.zeros(feat_ref.shape, F32)
    coef_ref[...] = jnp.zeros(coef_ref.shape, F32)

    def alpha_copy(index):
        at = pl.ds(pl.multiple_of(index * chunk, chunk), chunk)
        return pltpu.make_async_copy(alpha_ref.at[at], alpha_out.at[at], alpha_sems.at[index])

    def look(index, slot_number):
        start = pl.multiple_of(index * chunk, chunk)
        slot = entry_ref[:, pl.ds(start, chunk)]
        within = slot & (half - 1)
        owner = slot >> 6
        hot = jnp.where((iota((LANES, chunk), 0) & (half - 1)) == within, 1.0, 0.0).astype(BF16)
        wide_ref[slot_number] = dot(left, jnp.concatenate([hot, hot], axis=0))
        return owner

    def gather(index, slot_number, owner):
        start = pl.multiple_of(index * chunk, chunk)
        spread = jnp.broadcast_to(owner, (SUBS, chunk))
        picked = jnp.zeros((SUBS, chunk), F32)
        for place in range(peers):
            picked = jnp.where(spread == place, wide_ref[slot_number, place * SUBS : (place + 1) * SUBS, :], picked)
        last = jnp.sum(
            jnp.where(iota((peers, chunk), 0) == owner, wide_ref[slot_number, peers * SUBS :, :], 0.0),
            axis=0,
            keepdims=True,
        )
        feat_ref[0:SUBS, pl.ds(start, chunk)] = picked
        feat_ref[SUBS : SUBS + 1, pl.ds(start, chunk)] = last
        center_x = picked[0:1]
        center_y = picked[1:2]
        conic_xx = picked[2:3]
        conic_xy = picked[3:4]
        conic_yy = picked[4:5]
        lin_x = conic_xx * center_x + conic_xy * center_y
        lin_y = conic_xy * center_x + conic_yy * center_y
        constant = picked[5:6] - 0.5 * (center_x * lin_x + center_y * lin_y)
        coef_ref[slot_number, 0:1] = (-0.5 * LOG2E) * conic_xx
        coef_ref[slot_number, 1:2] = -LOG2E * conic_xy
        coef_ref[slot_number, 2:3] = (-0.5 * LOG2E) * conic_yy
        coef_ref[slot_number, 3:4] = LOG2E * lin_x
        coef_ref[slot_number, 4:5] = LOG2E * lin_y
        coef_ref[slot_number, 5:6] = LOG2E * constant + bias_ref[:, pl.ds(start, chunk)]
        for number, piece in enumerate(three_pieces(coef_ref[slot_number, 0:SUBS])):
            coef_ref[slot_number, number * SUBS : (number + 1) * SUBS] = piece.astype(F32)
        columns = jnp.transpose(coef_ref[slot_number]).astype(BF16)
        alpha_ref[pl.ds(start, chunk), :] = jnp.exp2(dot(columns, mono_ref[...]))
        alpha_copy(index).start()

    def gather_two(index, carry):
        owners = [look(2 * index + number, number) for number in range(2)]
        for number in range(2):
            gather(2 * index + number, number, owners[number])
        return carry

    lax.fori_loop(0, entries // (2 * chunk), gather_two, 0)

    pixels = TILE * TILE
    step_rows = length * GROUP
    parts = 4
    part_rows = step_rows // parts

    def weight_copy(group, part):
        at = pl.ds(group * step_rows + part * part_rows, part_rows)
        return pltpu.make_async_copy(
            weight_ref.at[at], weight_out.at[at], weight_sems.at[group * parts + part]
        )

    def scan(number, keeps):
        new_keeps = []
        for group in range(groups):
            at = pl.ds(
                pl.multiple_of(group * step_rows + number * 2 * GROUP, 2 * GROUP), 2 * GROUP
            )
            alpha = alpha_ref[at, :]
            first = keeps[group] * alpha[0:GROUP]
            keep = keeps[group] - first
            second = keep * alpha[GROUP:]
            new_keeps.append(keep - second)
            high, rest = two_pieces(jnp.concatenate([first, second], axis=0))
            weight_ref[at, 0:pixels] = high
            weight_ref[at, pixels:] = rest
        return tuple(new_keeps)

    keeps = tuple(jnp.ones((GROUP, pixels), F32) for _ in range(groups))
    steps = length // (2 * parts)
    for part in range(parts):
        keeps = lax.fori_loop(part * steps, (part + 1) * steps, scan, keeps, unroll=4)
        for group in range(groups):
            weight_copy(group, part).start()
    for group in range(groups):
        here = slice(group * step_rows, (group + 1) * step_rows)
        left = jnp.concatenate(
            two_pieces(spread_colours(feat_ref, group * step_rows, step_rows)), axis=0
        )
        sums = dot(left, weight_ref[here, 0:pixels]) + dot(left, weight_ref[here, pixels:])
        row = (group // across) * TILE
        col = (group % across) * LANES
        for channel in range(3):
            at = channel * GROUP
            total = sums[at : at + GROUP] + sums[at + 3 * GROUP : at + 4 * GROUP]
            for part in range(2):
                image_ref[
                    channel, row + part * SUBS : row + (part + 1) * SUBS, col : col + LANES
                ] = block_transpose(total[:, part * LANES : (part + 1) * LANES])

    blocks = rows // SUBS
    lane_block = iota((SUBS, LANES), 1) // TILE
    even = place_ref[1] % 2 == 0
    for vector in range(6 * blocks // SUBS):
        at_left = jnp.zeros((SUBS, LANES), F32)
        at_right = jnp.zeros((SUBS, LANES), F32)
        for place in range(SUBS):
            number = vector * SUBS + place
            source = image_ref if number // blocks < 3 else target_ref
            channel = (number // blocks) % 3
            top = (number % blocks) * SUBS
            first = source[channel, top : top + SUBS, 0:LANES]
            final = source[channel, top : top + SUBS, (across - 1) * LANES :]
            if place:
                first = pltpu.roll(first, TILE * place, 1)
            if place != SUBS - 1:
                final = pltpu.roll(final, TILE * (place + 1), 1)
            at_left = jnp.where(lane_block == place, first, at_left)
            at_right = jnp.where(lane_block == place, final, at_right)
        send_a_ref[vector * SUBS : (vector + 1) * SUBS, :] = jnp.where(even, at_right, at_left)
        send_b_ref[vector * SUBS : (vector + 1) * SUBS, :] = jnp.where(even, at_left, at_right)
    for index in range(entries // chunk):
        alpha_copy(index).wait()
    for group in range(groups):
        for part in range(parts):
            weight_copy(group, part).wait()


def lane_shift(block, shift, axis=1):
    shift %= block.shape[axis]
    return pltpu.roll(block, shift, axis) if shift else block


def strip_kernel(
    place_ref, got_a_in, got_b_in, image_ref, target_ref, side_ref, send_a_ref, send_b_ref,
    got_a_ref, got_b_ref, sems,
):
    copies = [
        pltpu.make_async_copy(got_a_in, got_a_ref, sems.at[0]),
        pltpu.make_async_copy(got_b_in, got_b_ref, sems.at[1]),
    ]
    for copy in copies:
        copy.start()
    for copy in copies:
        copy.wait()
    rows = image_ref.shape[1]
    cols = image_ref.shape[2]
    blocks = rows // SUBS
    lane_block = iota((SUBS, LANES), 1) // TILE
    even = place_ref[1] % 2 == 0
    for vector in range(6 * blocks // SUBS):
        got_a = got_a_ref[vector * SUBS : (vector + 1) * SUBS, :]
        got_b = got_b_ref[vector * SUBS : (vector + 1) * SUBS, :]
        from_right = jnp.where(even, got_a, got_b)
        from_left = jnp.where(even, got_b, got_a)
        for place in range(SUBS):
            number = vector * SUBS + place
            right = lane_shift(from_right, -TILE * place)
            left = lane_shift(from_left, -TILE * (place + 1))
            top = (number % blocks) * SUBS
            side_ref[number // blocks, top : top + SUBS, :] = jnp.where(
                lane_block == 0, right, jnp.where(lane_block == SUBS - 1, left, 0.0)
            )

    def packed(main, rest, shift):
        wide_sub = iota((SUBS, cols), 0) // 2
        side_sub = iota((SUBS, LANES), 0) // 2
        wides = []
        sides = []
        for number in range(6):
            source = image_ref if number < 3 else target_ref
            wides.append(source[number % 3, main : main + SUBS, :])
            sides.append(side_ref[number, main : main + SUBS, :])
        for first in (0, 4):
            wide = jnp.zeros((SUBS, cols), F32)
            side = jnp.zeros((SUBS, LANES), F32)
            for number in range(first, min(first + 4, 6)):
                source = image_ref if number < 3 else target_ref
                turn = 2 * (number - first) - shift
                block = lane_shift(source[number % 3, rest : rest + SUBS, :], turn, 0)
                wide = jnp.where(wide_sub == number - first, block, wide)
                block = lane_shift(side_ref[number, rest : rest + SUBS, :], turn, 0)
                side = jnp.where(side_sub == number - first, block, side)
            wides.append(wide)
            sides.append(side)
        lane_part = iota((SUBS, LANES), 1) // (2 * TILE)
        last = []
        for first in (0, 4):
            total = jnp.zeros((SUBS, LANES), F32)
            for part in range(4):
                moved = lane_shift(sides[first + part], TILE + 2 * TILE * part)
                total = jnp.where(lane_part == part, moved, total)
            last.append(total)
        return wides, last

    even_row = place_ref[0] % 2 == 0
    top, top_last = packed(0, SUBS, 0)
    bottom, bottom_last = packed(rows - SUBS, rows - 2 * SUBS, 6)
    for number in range(SUBS):
        here = slice(number * SUBS, (number + 1) * SUBS)
        send_a_ref[here, :] = jnp.where(even_row, bottom[number], top[number])
        send_b_ref[here, :] = jnp.where(even_row, top[number], bottom[number])
    for number in range(2):
        here = slice(number * LANES, (number + 1) * LANES)
        send_a_ref[SUBS * SUBS :, here] = jnp.where(even_row, bottom_last[number], top_last[number])
        send_b_ref[SUBS * SUBS :, here] = jnp.where(even_row, top_last[number], bottom_last[number])


def back_kernel(
    place_ref, got_a_in, got_b_in, image_ref, target_ref, side_ref, entry_ref, feat_ref,
    alpha_in, weight_in, down_ref, down_back_ref, across_ref, mono_ref,
    out_ref,
    raw_ref, vert_ref, blur_ref, coef_ref, grad_ref, alpha_ref, weight_ref, ahead_ref, pair_ref,
    right_ref, slope_ref, mask_ref, sum_ref, got_a_ref, got_b_ref, sems,
):
    rows = image_ref.shape[1]
    cols = image_ref.shape[2]
    wide = cols + LANES
    entries = entry_ref.shape[1]
    across = cols // LANES
    groups = (rows // TILE) * across
    length = entries // (groups * GROUP)
    tall = rows + 2 * HALO
    mid = rows + 2 * SUBS
    peers = out_ref.shape[0]
    half = LANES // 2

    alpha_copy = pltpu.make_async_copy(alpha_in, alpha_ref, sems.at[0])
    weight_copy = pltpu.make_async_copy(weight_in, weight_ref, sems.at[1])
    got_copies = [
        pltpu.make_async_copy(got_a_in, got_a_ref, sems.at[2]),
        pltpu.make_async_copy(got_b_in, got_b_ref, sems.at[3]),
    ]
    for copy in got_copies:
        copy.start()
    alpha_copy.start()
    weight_copy.start()
    for copy in got_copies:
        copy.wait()
    even_row = place_ref[0] % 2 == 0
    for number in range(6):
        source = image_ref if number < 3 else target_ref
        raw_ref[number, 0:rows, 0:cols] = source[number % 3]
        raw_ref[number, 0:rows, cols:] = side_ref[number]
    lane_block = iota((SUBS, LANES), 1) // TILE
    border = (lane_block == 0) | (lane_block == SUBS - 1)
    for below in (True, False):
        def got(rows_here, cols_here):
            got_a = got_a_ref[rows_here, cols_here]
            got_b = got_b_ref[rows_here, cols_here]
            return jnp.where(even_row, got_a, got_b) if below else jnp.where(even_row, got_b, got_a)

        main_at = rows if below else tall - SUBS
        rest_at = rows + SUBS if below else tall - 2 * SUBS
        goal = 0 if below else 3
        wide_keep = iota((SUBS, cols), 0) // 2 == goal
        side_keep = iota((SUBS, LANES), 0) // 2 == goal
        wides = [got(slice(number * SUBS, (number + 1) * SUBS), slice(0, cols)) for number in range(SUBS)]
        lasts = [
            got(slice(SUBS * SUBS, (SUBS + 1) * SUBS), slice(number * LANES, (number + 1) * LANES))
            for number in range(2)
        ]
        sides = [
            jnp.where(border, lane_shift(lasts[number // 4], -TILE - 2 * TILE * (number % 4)), 0.0)
            for number in range(SUBS)
        ]
        for number in range(6):
            raw_ref[number, main_at : main_at + SUBS, 0:cols] = wides[number]
            raw_ref[number, main_at : main_at + SUBS, cols:] = sides[number]
            turn = 2 * (goal - number % 4)
            block = lane_shift(wides[6 + number // 4], turn, 0)
            raw_ref[number, rest_at : rest_at + SUBS, 0:cols] = jnp.where(wide_keep, block, 0.0)
            block = lane_shift(sides[6 + number // 4], turn, 0)
            raw_ref[number, rest_at : rest_at + SUBS, cols:] = jnp.where(side_keep, block, 0.0)
    down = down_ref[...]
    for channel in range(3):
        shown = raw_ref[channel]
        wanted = raw_ref[3 + channel]
        for number, value in enumerate(
            [shown, wanted, shown * shown + wanted * wanted, shown * wanted]
        ):
            at = (channel * 4 + number) * mid
            vert_ref[at : at + mid, :] = dot_full(down, value)
    for part in range(3):
        at = part * 4 * mid
        blur_ref[at : at + 4 * mid, :] = dot_full(vert_ref[at : at + 4 * mid, :], across_ref[...])
    line = iota((mid, wide), 0) - SUBS + place_ref[0] * rows
    spot = iota((mid, wide), 1)
    spot = jnp.where(spot < cols + half, spot, spot - wide) + place_ref[1] * cols
    inside = (
        (line >= 0) & (line < place_ref[2] * rows) & (spot >= 0) & (spot < place_ref[3] * cols)
    )
    down_back = down_back_ref[...]
    for channel in range(3):
        at = channel * 4 * mid
        mean_r, mean_t, squares, cross = [
            blur_ref[at + number * mid : at + (number + 1) * mid, :] for number in range(4)
        ]
        upper_one = 2.0 * mean_r * mean_t + STAB_ONE
        upper_two = 2.0 * (cross - mean_r * mean_t) + STAB_TWO
        lower_one = mean_r * mean_r + mean_t * mean_t + STAB_ONE
        lower_two = squares - mean_r * mean_r - mean_t * mean_t + STAB_TWO
        inv_one = 1.0 / lower_one
        inv_two = 1.0 / lower_two
        inverse = inv_one * inv_two
        value = upper_one * upper_two * inverse
        on_mean = (
            2.0 * mean_t * (upper_two - upper_one) * inverse
            + 2.0 * mean_r * value * (inv_two - inv_one)
        )
        on_square = -value * inv_two
        on_cross = 2.0 * upper_one * inverse
        for number, part in enumerate([on_mean, on_square, on_cross]):
            part = jnp.where(inside, -WEIGHT_SSIM * part, 0.0)
            spot_at = (channel * 3 + number) * rows
            coef_ref[spot_at : spot_at + rows, :] = dot_full(down_back, part)
    for channel in range(3):
        at = channel * 3 * rows
        back = dot_full(coef_ref[at : at + 3 * rows, :], across_ref[:, 0:cols])
        shown = image_ref[channel]
        wanted = target_ref[channel]
        gap = shown - wanted
        grad_ref[channel] = (
            (1.0 - WEIGHT_SSIM) * gap * lax.rsqrt(gap * gap + SMOOTHING * SMOOTHING)
            + back[0:rows]
            + 2.0 * shown * back[rows : 2 * rows]
            + wanted * back[2 * rows :]
        )

    pixels = TILE * TILE
    step_rows = length * GROUP
    mono = mono_ref[0 : 2 * SUBS, :]
    mono = jnp.concatenate([mono, mono], axis=1)
    same = iota((SUBS, step_rows), 0) == (iota((SUBS, step_rows), 1) & (GROUP - 1))
    slope_ref[...] = jnp.zeros(slope_ref.shape, F32)

    for group in range(groups):
        row = (group // across) * TILE
        col = (group % across) * LANES
        start = group * step_rows
        slopes = []
        for channel in range(3):
            for part in range(2):
                slopes.append(
                    block_transpose(
                        grad_ref[channel, row + part * SUBS : row + (part + 1) * SUBS, col : col + LANES]
                    )
                )
        slopes = jnp.concatenate(
            [jnp.concatenate(slopes[2 * channel : 2 * channel + 2], axis=1) for channel in range(3)],
            axis=0,
        )
        high, rest = [piece.astype(F32) for piece in two_pieces(slopes)]
        at = group * 6 * GROUP
        both = jnp.concatenate([high, rest], axis=0)
        right_ref[at : at + 6 * GROUP, 0:pixels] = both
        right_ref[at : at + 6 * GROUP, pixels:] = both
        top, low = [
            piece.astype(F32)
            for piece in two_pieces(spread_colours(feat_ref, start, step_rows))
        ]
        left = jnp.transpose(jnp.concatenate([top, low, top], axis=0)).astype(BF16)
        ahead_ref[start : start + step_rows, :] = dot(
            left, jnp.concatenate([high, high, rest], axis=0).astype(BF16)
        )

    alpha_copy.wait()
    weight_copy.wait()

    def step(number, behinds):
        new_behinds = []
        at = (length // 2 - 1 - number) * 2 * GROUP
        for group in range(groups):
            source = pl.ds(pl.multiple_of(group * step_rows + at, 2 * GROUP), 2 * GROUP)
            alpha = alpha_ref[source, :]
            ahead = ahead_ref[source, :]
            weight = weight_ref[source, 0:pixels].astype(F32) + weight_ref[source, pixels:].astype(F32)
            behind = behinds[group]
            second = ahead[GROUP:] - behind
            behind = behind + alpha[GROUP:] * second
            first = ahead[0:GROUP] - behind
            new_behinds.append(behind + alpha[0:GROUP] * first)
            high, rest = two_pieces(weight * jnp.concatenate([first, second], axis=0))
            pair_ref[source, 0:pixels] = high
            pair_ref[source, pixels:] = rest
        return tuple(new_behinds)

    zero = jnp.zeros((GROUP, pixels), F32)
    lax.fori_loop(0, length // 2, step, tuple(zero for _ in range(groups)), unroll=4)

    for group in range(groups):
        here = slice(group * step_rows, (group + 1) * step_rows)
        at = group * 6 * GROUP
        moments = dot_nt(mono, pair_ref[here, :])
        tints = dot_nt(right_ref[at : at + 6 * GROUP, :].astype(BF16), weight_ref[here, :])
        on_xx = moments[0:1]
        on_xy = moments[1:2]
        on_yy = moments[2:3]
        on_x = moments[3:4]
        on_y = moments[4:5]
        on_one = moments[5:6]
        center_x = feat_ref[0:1, here]
        center_y = feat_ref[1:2, here]
        conic_xx = feat_ref[2:3, here]
        conic_xy = feat_ref[3:4, here]
        conic_yy = feat_ref[4:5, here]
        near_x = on_x - center_x * on_one
        near_y = on_y - center_y * on_one
        slope_ref[0:1, here] = conic_xx * near_x + conic_xy * near_y
        slope_ref[1:2, here] = conic_xy * near_x + conic_yy * near_y
        slope_ref[2:3, here] = -0.5 * (on_xx - center_x * (on_x + near_x))
        slope_ref[3:4, here] = -(on_xy - center_y * on_x - center_x * near_y)
        slope_ref[4:5, here] = -0.5 * (on_yy - center_y * (on_y + near_y))
        slope_ref[5:6, here] = on_one
        for channel in range(3):
            at = SUBS * channel
            both = tints[at : at + SUBS] + tints[at + 24 : at + 24 + SUBS]
            slope_ref[6 + channel : 7 + channel, here] = jnp.sum(
                jnp.where(same, both, 0.0), axis=0, keepdims=True
            )

    chunk = 512
    tops = peers * SUBS
    sum_ref[...] = jnp.zeros(sum_ref.shape, F32)
    pair_step = iota((2 * SUBS, chunk), 0) // SUBS

    def collect(index, carry):
        start = pl.multiple_of(index * chunk, chunk)
        slot = entry_ref[:, pl.ds(start, chunk)]
        within = slot & (half - 1)
        owner = slot >> 6
        hot = jnp.where((iota((LANES, chunk), 0) & (half - 1)) == within, 1.0, 0.0).astype(BF16)
        values = [
            piece.astype(F32) for piece in two_pieces(slope_ref[0:SUBS, pl.ds(start, chunk)])
        ]
        values = [jnp.concatenate([value, value], axis=0) for value in values]
        offset = jnp.broadcast_to(owner, (2 * SUBS, chunk)) - pair_step
        for place in range(peers // 2):
            hit = offset == 2 * place
            for number in range(2):
                at = number * (tops + peers) + place * 2 * SUBS
                mask_ref[at : at + 2 * SUBS, :] = jnp.where(hit, values[number], 0.0).astype(BF16)
        hit = iota((peers, chunk), 0) == owner
        for number, piece in enumerate(
            two_pieces(slope_ref[SUBS : SUBS + 1, pl.ds(start, chunk)])
        ):
            at = number * (tops + peers) + tops
            mask_ref[at : at + peers, :] = jnp.where(hit, piece.astype(F32), 0.0).astype(BF16)
        sum_ref[...] += dot_nt(mask_ref[...], hot)
        return carry

    lax.fori_loop(0, entries // chunk, collect, 0)
    lane_low = iota((SUBS, LANES), 1) < half
    for place in range(peers):
        at = place * SUBS
        eight = sum_ref[at : at + SUBS, :] + sum_ref[tops + peers + at : tops + peers + at + SUBS, :]
        at = tops + place
        ninth = sum_ref[at : at + 1, :] + sum_ref[tops + peers + at : tops + peers + at + 1, :]
        out_ref[place] = jnp.where(lane_low, eight, jnp.broadcast_to(ninth, (SUBS, LANES)))


def return_kernel(
    place_ref, returned_ref, got_ref, jac_in, cam_ref, grad_out,
    row_ref, mask_ref, sum_ref, pack_ref, jac_ref, grad_ref, sems, jac_sems,
):
    jac_copy = pltpu.make_async_copy(jac_in, jac_ref, jac_sems.at[0])
    jac_copy.start()
    devices = got_ref.shape[0]
    count, own = grad_ref.shape
    high = own // LANES
    half = LANES // 2
    tops = high * SUBS
    part_rows = tops + high
    chunk = 4 * LANES
    cam = [[cam_ref[row, col] for col in range(3)] for row in range(3)]
    fill_numbers(place_ref, got_ref, row_ref)
    sum_ref[...] = jnp.zeros(sum_ref.shape, F32)
    lane_low = iota((SUBS, LANES), 1) < half
    pair_step = iota((2 * SUBS, chunk), 0) // SUBS

    def collect(index, carry):
        numbers = row_ref[:, pl.ds(pl.multiple_of(index * chunk, chunk), chunk)]
        low = numbers & (LANES - 1)
        top = numbers >> 7
        hot = jnp.where(iota((LANES, chunk), 0) == low, 1.0, 0.0).astype(BF16)
        eights = []
        ninths = []
        for part in range(chunk // LANES):
            first = returned_ref[index * 8 + 2 * part]
            second = returned_ref[index * 8 + 2 * part + 1]
            eights.append(jnp.where(lane_low, first, pltpu.roll(second, half, 1)))
            ninths.append(jnp.where(lane_low, pltpu.roll(first, half, 1), second)[0:1])
        values = [piece.astype(F32) for piece in two_pieces(jnp.concatenate(eights, axis=1))]
        values = [jnp.concatenate([value, value], axis=0) for value in values]
        offset = jnp.broadcast_to(top, (2 * SUBS, chunk)) - pair_step
        for place in range(high // 2):
            hit = offset == 2 * place
            for number in range(2):
                at = number * part_rows + place * 2 * SUBS
                mask_ref[at : at + 2 * SUBS, :] = jnp.where(hit, values[number], 0.0).astype(BF16)
        hit = iota((high, chunk), 0) == top
        for number, piece in enumerate(two_pieces(jnp.concatenate(ninths, axis=1))):
            at = number * part_rows + tops
            mask_ref[at : at + high, :] = jnp.where(hit, piece.astype(F32), 0.0).astype(BF16)
        sum_ref[...] += dot_nt(mask_ref[...], hot)
        return carry

    lax.fori_loop(0, devices * half // chunk, collect, 0)
    jac_copy.wait()

    def grad_copy(index):
        at = pl.ds(pl.multiple_of(index * SUBS * LANES, SUBS * LANES), SUBS * LANES)
        return pltpu.make_async_copy(grad_ref.at[:, at], grad_out.at[:, at], sems.at[index])

    def block(index, carry):
        start = pl.multiple_of(index * SUBS, SUBS)

        def jac(number):
            return jac_ref[pl.ds(number * high + start, SUBS), :]

        slopes = []
        for number in range(SUBS):
            at = start * SUBS + number
            slopes.append(
                sum_ref[pl.ds(at, SUBS, stride=SUBS), :]
                + sum_ref[pl.ds(part_rows + at, SUBS, stride=SUBS), :]
            )
        at = tops + start
        slopes.append(sum_ref[pl.ds(at, SUBS), :] + sum_ref[pl.ds(part_rows + at, SUBS), :])
        on_center = [slopes[0] * jac(30), slopes[1] * jac(31)]
        conic_xx = jac(48)
        conic_xy = jac(49)
        conic_yy = jac(50)
        on_xx, on_xy, on_yy = slopes[2:5]
        first_x = conic_xx * on_xx + conic_xy * on_xy
        first_y = conic_xy * on_xy + conic_yy * on_yy
        on_first = -(conic_xx * first_x + conic_xy * conic_xy * on_yy)
        on_second = -(conic_xy * conic_xy * on_xx + conic_yy * first_y)
        on_mixed = -(
            2.0 * conic_xx * conic_xy * on_xx
            + (conic_xx * conic_yy + conic_xy * conic_xy) * on_xy
            + 2.0 * conic_xy * conic_yy * on_yy
        )
        out = []
        for axis in range(3):
            out.append(
                cam[0][axis] * on_center[0]
                + cam[1][axis] * on_center[1]
                + slopes[6] * jac(21 + axis)
                + slopes[7] * jac(24 + axis)
                + slopes[8] * jac(27 + axis)
            )
        for number in range(7):
            out.append(
                on_first * jac(number) + on_mixed * jac(7 + number) + on_second * jac(14 + number)
            )
        out.append(slopes[5] * jac(32))
        for channel in range(3):
            out.append(SH_ZERO * slopes[6 + channel])
            for term in range(1, 16):
                out.append(slopes[6 + channel] * jac(32 + term))
        for number, value in enumerate(out):
            pack_ref[number * SUBS : (number + 1) * SUBS, :] = value
        for first in range(0, count, SUBS):
            number = min(SUBS, count - first)
            for place in range(SUBS):
                at = pl.ds(pl.multiple_of((start + place) * LANES, LANES), LANES)
                grad_ref[first : first + number, at] = pack_ref[
                    pl.ds(first * SUBS + place, number, stride=SUBS), :
                ]
        grad_copy(index).start()
        return carry

    lax.fori_loop(0, high // SUBS, block, 0)
    for index in range(high // SUBS):
        grad_copy(index).wait()


def band(outs, ins):
    taps = np.exp(-((np.arange(11) - 5.0) ** 2) / (2.0 * BLUR_SIGMA * BLUR_SIGMA))
    offset = np.asarray(ins)[None, :] - np.asarray(outs)[:, None]
    values = np.exp(-(offset**2) / (2.0 * BLUR_SIGMA * BLUR_SIGMA)) / taps.sum()
    return np.where(np.abs(offset) <= RIM, values, 0.0).astype(np.float32)


def monomials():
    pixel = np.arange(TILE * TILE)
    x = (pixel % TILE) - 7.5
    y = (pixel // TILE) - 7.5
    eight = np.stack([x * x, x * y, y * y, x, y, x * 0 + 1, x * 0, x * 0])
    return np.concatenate([eight, eight, eight, eight * 0]).astype(np.float32)


def call(body, out_shape, scratch, scalar_at, args, flops, vmem, outside=(), outs_outside=()):
    in_specs = [
        pl.BlockSpec(
            memory_space=pltpu.SMEM
            if number in scalar_at
            else pl.ANY
            if number in outside
            else pltpu.VMEM
        )
        for number in range(len(args))
    ]
    if isinstance(out_shape, tuple):
        out_specs = tuple(
            pl.BlockSpec(memory_space=pl.ANY if number in outs_outside else pltpu.VMEM)
            for number in range(len(out_shape))
        )
    else:
        out_specs = pl.BlockSpec(memory_space=pl.ANY if outs_outside else pltpu.VMEM)
    return pl.pallas_call(
        body,
        out_shape=out_shape,
        in_specs=in_specs,
        out_specs=out_specs,
        scratch_shapes=scratch,
        compiler_params=pltpu.CompilerParams(vmem_limit_bytes=vmem * MIB),
        cost_estimate=pl.CostEstimate(flops=flops, bytes_accessed=1 << 20, transcendentals=0),
    )(*args)


def swap_pairs(count, first):
    pairs = []
    for low in range(first, count - 1, 2):
        pairs += [(low, low + 1), (low + 1, low)]
    return pairs


def swap(value_a, value_b, axis):
    count = lax.axis_size(axis)
    return (
        lax.ppermute(value_a, axis, swap_pairs(count, 0)),
        lax.ppermute(value_b, axis, swap_pairs(count, 1)),
    )


def exchange(payload):
    return lax.all_to_all(payload, ("img", "cell"), split_axis=0, concat_axis=0, tiled=True)


def shards(attributes, camera, target, visible_index, tile_lists, tile_len):
    img_count = lax.axis_size("img")
    cell_count = lax.axis_size("cell")
    devices = img_count * cell_count
    slots = visible_index.shape[1]
    count, own = attributes.shape
    high = own // LANES
    _, rows, cols = target.shape
    tiles_down, tiles_across, length = tile_lists.shape
    entries = tiles_down * tiles_across * length
    wide = cols + LANES
    mid = rows + 2 * SUBS
    tall = rows + 2 * HALO
    place = jnp.stack(
        [
            lax.axis_index("img"),
            lax.axis_index("cell"),
            jnp.int32(img_count),
            jnp.int32(cell_count),
        ]
    ).astype(jnp.int32)

    assert 2 * (slots // devices) == LANES
    asked = call(
        ask_kernel,
        jax.ShapeDtypeStruct((devices, LANES), jnp.int32),
        [],
        (),
        (visible_index,),
        1 << 14,
        2,
    )
    got = exchange(asked)

    table, jac = call(
        owner_kernel,
        (
            jax.ShapeDtypeStruct((high * (SUBS + 1), 2 * LANES), BF16),
            jax.ShapeDtypeStruct((JAC_ROWS * high, LANES), F32),
        ),
        [pltpu.VMEM((count * high, LANES), F32), pltpu.VMEM((high * (SUBS + 1), LANES), F32)],
        (1,),
        (attributes, camera),
        1 << 24,
        12,
    )
    reply = call(
        reply_kernel,
        jax.ShapeDtypeStruct((devices, SUBS, LANES), F32),
        [
            pltpu.VMEM((1, slots), jnp.int32),
            pltpu.VMEM((2, high * (SUBS + 1), 2 * LANES), F32),
            pltpu.VMEM((devices, LANES), jnp.int32),
            pltpu.SemaphoreType.DMA((1,)),
        ],
        (0,),
        (place, table, got),
        1 << 24,
        2 + slots // 128,
        outside=(2,),
    )
    arrived = exchange(reply)

    order = (tiles_down, tiles_across // GROUP, GROUP, length)
    entry = tile_lists.reshape(order).transpose(0, 1, 3, 2).reshape(1, entries)
    live = jnp.arange(length, dtype=jnp.int32)[None, None, :, None] < tile_len.reshape(
        tiles_down, tiles_across // GROUP, 1, GROUP
    )
    bias = jnp.where(live, 0.0, -1e30).astype(F32).reshape(1, entries)
    mono = jnp.asarray(monomials()).astype(BF16)
    packed = 6 * rows // SUBS
    pixels = TILE * TILE
    group_rows = length * GROUP
    groups = entries // group_rows
    strip = jax.ShapeDtypeStruct((packed, LANES), F32)
    image, feat, alpha, weight, send_a, send_b = call(
        render_kernel,
        (
            jax.ShapeDtypeStruct((3, rows, cols), F32),
            jax.ShapeDtypeStruct((2 * SUBS, entries), F32),
            jax.ShapeDtypeStruct((entries, pixels), F32),
            jax.ShapeDtypeStruct((entries, 2 * pixels), BF16),
            strip,
            strip,
        ),
        [
            pltpu.VMEM((2, devices * (SUBS + 1), 512), F32),
            pltpu.VMEM((2, 32, 512), F32),
            pltpu.VMEM((entries, pixels), F32),
            pltpu.VMEM((entries, 2 * pixels), BF16),
            pltpu.VMEM((devices, SUBS, LANES), F32),
            pltpu.SemaphoreType.DMA((entries // 512,)),
            pltpu.SemaphoreType.DMA((4 * groups,)),
            pltpu.SemaphoreType.DMA((1,)),
        ],
        (0,),
        (place, arrived, entry, bias, target, mono),
        1 << 26,
        16 + devices // 8,
        outside=(1,),
        outs_outside=(2, 3),
    )
    got_a, got_b = swap(send_a, send_b, "cell")
    edge = jax.ShapeDtypeStruct(((SUBS + 1) * SUBS, cols), F32)
    side, send_a, send_b = call(
        strip_kernel,
        (jax.ShapeDtypeStruct((6, rows, LANES), F32), edge, edge),
        [
            pltpu.VMEM((packed, LANES), F32),
            pltpu.VMEM((packed, LANES), F32),
            pltpu.SemaphoreType.DMA((2,)),
        ],
        (0,),
        (place, got_a, got_b, image, target),
        1 << 20,
        4,
        outside=(1, 2),
    )
    got_a, got_b = swap(send_a, send_b, "img")

    tall_at = np.arange(tall)
    tall_at = np.where(tall_at < rows + HALO, tall_at, tall_at - tall)
    mid_at = np.arange(mid) - SUBS
    wide_at = np.arange(wide)
    wide_at = np.where(wide_at < cols + LANES // 2, wide_at, wide_at - wide)
    down = jnp.asarray(band(mid_at, tall_at))
    down_back = jnp.asarray(band(np.arange(rows), mid_at))
    across = jnp.asarray(band(wide_at, wide_at))
    slot_grads = call(
        back_kernel,
        jax.ShapeDtypeStruct((devices, SUBS, LANES), F32),
        [
            pltpu.VMEM((6, tall, wide), F32),
            pltpu.VMEM((12 * mid, wide), F32),
            pltpu.VMEM((12 * mid, wide), F32),
            pltpu.VMEM((9 * rows, wide), F32),
            pltpu.VMEM((3, rows, cols), F32),
            pltpu.VMEM((entries, pixels), F32),
            pltpu.VMEM((entries, 2 * pixels), BF16),
            pltpu.VMEM((entries, pixels), F32),
            pltpu.VMEM((entries, 2 * pixels), BF16),
            pltpu.VMEM((groups * 6 * GROUP, 2 * pixels), F32),
            pltpu.VMEM((2 * SUBS, entries), F32),
            pltpu.VMEM((2 * devices * (SUBS + 1), 512), BF16),
            pltpu.VMEM((2 * devices * (SUBS + 1), LANES), F32),
            pltpu.VMEM(((SUBS + 1) * SUBS, cols), F32),
            pltpu.VMEM(((SUBS + 1) * SUBS, cols), F32),
            pltpu.SemaphoreType.DMA((4,)),
        ],
        (0,),
        (
            place, got_a, got_b, image, target, side, entry, feat, alpha, weight,
            down, down_back, across, mono,
        ),
        1 << 27,
        32 + devices // 8,
        outside=(1, 2, 8, 9),
    )
    returned = exchange(slot_grads)
    return call(
        return_kernel,
        jax.ShapeDtypeStruct((count, own), F32),
        [
            pltpu.VMEM((1, slots), jnp.int32),
            pltpu.VMEM((2 * high * (SUBS + 1), 4 * LANES), BF16),
            pltpu.VMEM((2 * high * (SUBS + 1), LANES), F32),
            pltpu.VMEM((count * SUBS, LANES), F32),
            pltpu.VMEM((JAC_ROWS * high, LANES), F32),
            pltpu.VMEM((count, own), F32),
            pltpu.SemaphoreType.DMA((high // SUBS,)),
            pltpu.SemaphoreType.DMA((1,)),
        ],
        (0, 4),
        (place, returned, got, jac, camera),
        1 << 26,
        12,
        outside=(3,),
        outs_outside=(0,),
    )


def solution(mesh):
    return jax.shard_map(
        shards,
        mesh=mesh,
        in_specs=(
            P(None, ("img", "cell")),
            P(),
            P(None, "img", "cell"),
            P(("img", "cell"), None),
            P("img", "cell", None),
            P("img", "cell"),
        ),
        out_specs=P(None, ("img", "cell")),
        check_vma=False,
    )
```

```python
import jax
import jax.numpy as jnp
import ml_dtypes
import numpy as np
from jax import lax
from jax.experimental import pallas as pl
from jax.experimental.pallas import tpu as pltpu
from jax.sharding import PartitionSpec as P

TILE = 16
LANES = 128
SUBS = 8
GROUP = 8
RIM = 5
HALO = 16
WEIGHT_SSIM = 0.2
SMOOTHING = 0.01
STAB_ONE = 0.0001
STAB_TWO = 0.0009
BLUR_SIGMA = 1.5
LOG2E = 1.4426950408889634
SH_ZERO = 0.28209479177387814
SH_ONE = 0.4886025119029199
SH_TWO = (
    1.0925484305920792,
    -1.0925484305920792,
    0.31539156525252005,
    -1.0925484305920792,
    0.5462742152960396,
)
SH_THREE = (
    -0.5900435899266435,
    2.890611442640554,
    -0.4570457994644658,
    0.3731763325901154,
    -0.4570457994644658,
    1.445305721320277,
    -0.5900435899266435,
)
F32 = jnp.float32
BF16 = jnp.bfloat16
JAC_ROWS = 51
MIB = 1024 * 1024


def harmonic_basis(unit_x, unit_y, unit_z):
    unit_xx = unit_x * unit_x
    unit_yy = unit_y * unit_y
    unit_zz = unit_z * unit_z
    return [
        -SH_ONE * unit_y,
        SH_ONE * unit_z,
        -SH_ONE * unit_x,
        SH_TWO[0] * unit_x * unit_y,
        SH_TWO[1] * unit_y * unit_z,
        SH_TWO[2] * (2.0 * unit_zz - unit_xx - unit_yy),
        SH_TWO[3] * unit_x * unit_z,
        SH_TWO[4] * (unit_xx - unit_yy),
        SH_THREE[0] * unit_y * (3.0 * unit_xx - unit_yy),
        SH_THREE[1] * unit_x * unit_y * unit_z,
        SH_THREE[2] * unit_y * (4.0 * unit_zz - unit_xx - unit_yy),
        SH_THREE[3] * unit_z * (2.0 * unit_zz - 3.0 * unit_xx - 3.0 * unit_yy),
        SH_THREE[4] * unit_x * (4.0 * unit_zz - unit_xx - unit_yy),
        SH_THREE[5] * unit_z * (unit_xx - unit_yy),
        SH_THREE[6] * unit_x * (unit_xx - 3.0 * unit_yy),
    ]


def three_pieces(value):
    first = value.astype(BF16)
    rest = value - first.astype(F32)
    second = rest.astype(BF16)
    third = (rest - second.astype(F32)).astype(BF16)
    return first, second, third


def two_pieces(value):
    first = value.astype(BF16)
    return first, (value - first.astype(F32)).astype(BF16)


def dot(left, right):
    return jnp.dot(left, right, preferred_element_type=F32)


def dot_nt(left, right):
    return lax.dot_general(left, right, (((1,), (1,)), ((), ())), preferred_element_type=F32)


def dot_full(left, right):
    return jnp.dot(left, right, preferred_element_type=F32, precision=lax.Precision.HIGHEST)


def iota(shape, dim):
    return lax.broadcasted_iota(jnp.int32, shape, dim)


def block_transpose(block):
    turn = (iota(block.shape, 0) - iota(block.shape, 1) // TILE) & (SUBS - 1)
    out = block
    for step in range(1, SUBS):
        moved = pltpu.roll(block, LANES - TILE * step, 1)
        moved = pltpu.roll(moved, step, 0)
        out = jnp.where(turn == step, moved, out)
    return out


def covariance(scale_rows, quat_rows, cam):
    scales = [jnp.exp(row) for row in scale_rows]
    quat_w = 1.5 + jnp.tanh(quat_rows[0])
    quat_x, quat_y, quat_z = quat_rows[1:]
    inverse = lax.rsqrt(quat_w * quat_w + quat_x * quat_x + quat_y * quat_y + quat_z * quat_z)
    quat_w, quat_x, quat_y, quat_z = (
        quat_w * inverse,
        quat_x * inverse,
        quat_y * inverse,
        quat_z * inverse,
    )
    rotation = [
        [
            1.0 - 2.0 * (quat_y * quat_y + quat_z * quat_z),
            2.0 * (quat_x * quat_y - quat_w * quat_z),
            2.0 * (quat_x * quat_z + quat_w * quat_y),
        ],
        [
            2.0 * (quat_x * quat_y + quat_w * quat_z),
            1.0 - 2.0 * (quat_x * quat_x + quat_z * quat_z),
            2.0 * (quat_y * quat_z - quat_w * quat_x),
        ],
        [
            2.0 * (quat_x * quat_z - quat_w * quat_y),
            2.0 * (quat_y * quat_z + quat_w * quat_x),
            1.0 - 2.0 * (quat_x * quat_x + quat_y * quat_y),
        ],
    ]
    axes = [
        [
            (
                cam[screen][0] * rotation[0][axis]
                + cam[screen][1] * rotation[1][axis]
                + cam[screen][2] * rotation[2][axis]
            )
            * scales[axis]
            for axis in range(3)
        ]
        for screen in range(2)
    ]
    first = axes[0][0] * axes[0][0] + axes[0][1] * axes[0][1] + axes[0][2] * axes[0][2] + 0.3
    mixed = axes[0][0] * axes[1][0] + axes[0][1] * axes[1][1] + axes[0][2] * axes[1][2]
    second = axes[1][0] * axes[1][0] + axes[1][1] * axes[1][1] + axes[1][2] * axes[1][2] + 0.3
    return first, mixed, second


def owner_kernel(attr_ref, cam_ref, table_ref, jac_ref, pack_ref, feat_ref):
    count, own = attr_ref.shape
    high = own // LANES
    cam = [[cam_ref[row, col] for col in range(3)] for row in range(3)]
    for first in range(0, count, SUBS):
        number = min(SUBS, count - first)
        for place in range(high):
            pack_ref[pl.ds(first * high + place, number, stride=high), :] = attr_ref[
                first : first + number, place * LANES : (place + 1) * LANES
            ]

    def block(index, carry):
        start = pl.multiple_of(index * SUBS, SUBS)

        def row(number):
            return pack_ref[pl.ds(number * high + start, SUBS), :]

        positions = [row(number) for number in range(3)]
        shape_rows = [row(3 + number) for number in range(7)]
        jac = []
        (cov_first, cov_mixed, cov_second), pull = jax.vjp(
            lambda *rows: covariance(rows[:3], rows[3:], cam), *shape_rows
        )
        one = jnp.ones_like(cov_first)
        zero = jnp.zeros_like(cov_first)
        jac += pull((one, zero, zero))
        jac += pull((zero, one, zero))
        jac += pull((zero, zero, one))
        inverse = 1.0 / (cov_first * cov_second - cov_mixed * cov_mixed)
        conic = [cov_second * inverse, -cov_mixed * inverse, cov_first * inverse]
        centers = []
        slopes = []
        for screen in range(2):
            angle = (
                cam[screen][0] * positions[0]
                + cam[screen][1] * positions[1]
                + cam[screen][2] * positions[2]
            ) / 3.0
            centers.append(7.0 * jnp.sin(angle))
            slopes.append((7.0 / 3.0) * jnp.cos(angle))
        raw = row(10)
        decay = jnp.exp(-raw)
        log_opacity = -jnp.log(1.0 + decay)
        harmonics = [[row(11 + 16 * channel + term) for term in range(16)] for channel in range(3)]

        def colours_of(pos_x, pos_y, pos_z):
            off_x = pos_x - cam[2][0]
            off_y = pos_y - cam[2][1]
            off_z = pos_z - cam[2][2]
            scale = lax.rsqrt(off_x * off_x + off_y * off_y + off_z * off_z)
            basis = harmonic_basis(off_x * scale, off_y * scale, off_z * scale)
            colours = []
            for channel in range(3):
                total = 0.5 + SH_ZERO * harmonics[channel][0]
                for term in range(1, 16):
                    total = total + basis[term - 1] * harmonics[channel][term]
                colours.append(total)
            return tuple(colours), basis

        colours, pull_colours, basis = jax.vjp(colours_of, *positions, has_aux=True)
        jac += pull_colours((one, zero, zero))
        jac += pull_colours((zero, one, zero))
        jac += pull_colours((zero, zero, one))
        jac += slopes
        jac.append(decay / (1.0 + decay))
        jac += basis
        jac += conic
        for number, value in enumerate(jac):
            jac_ref[pl.ds(number * high + start, SUBS), :] = value
        features = centers + conic + [log_opacity] + list(colours)
        for number in range(SUBS):
            feat_ref[pl.ds(start * SUBS + number, SUBS, stride=SUBS), :] = features[number]
        feat_ref[pl.ds(high * SUBS + start, SUBS), :] = features[SUBS]
        return carry

    lax.fori_loop(0, high // SUBS, block, 0)
    for number, piece in enumerate(two_pieces(feat_ref[...])):
        table_ref[:, number * LANES : (number + 1) * LANES] = piece


def ask_kernel(index_ref, out_ref):
    for pair in range(out_ref.shape[0] // 2):
        numbers = index_ref[:, pair * LANES : (pair + 1) * LANES]
        out_ref[2 * pair : 2 * pair + 2, :] = jnp.broadcast_to(numbers, (2, LANES))


def fill_numbers(place_ref, got_ref, row_ref):
    lane_low = iota((1, LANES), 1) < LANES // 2
    odd = (place_ref[0] * place_ref[3] + place_ref[1]) % 2 == 1
    for pair in range(got_ref.shape[0] // 2):
        first = got_ref[2 * pair : 2 * pair + 1, :]
        second = got_ref[2 * pair + 1 : 2 * pair + 2, :]
        row_ref[:, pair * LANES : (pair + 1) * LANES] = jnp.where(
            odd,
            jnp.where(lane_low, pltpu.roll(first, LANES // 2, 1), second),
            jnp.where(lane_low, first, pltpu.roll(second, LANES // 2, 1)),
        )


def reply_kernel(place_ref, table_ref, got_in, out_ref, row_ref, wide_ref, got_ref, sems):
    got_copy = pltpu.make_async_copy(got_in, got_ref, sems.at[0])
    got_copy.start()
    got_copy.wait()
    devices = got_ref.shape[0]
    high = table_ref.shape[0] // (SUBS + 1)
    chunk = 2 * LANES
    half = LANES // 2
    fill_numbers(place_ref, got_ref, row_ref)

    def look(index, slot):
        numbers = row_ref[:, pl.ds(pl.multiple_of(index * chunk, chunk), chunk)]
        low = numbers & (LANES - 1)
        top = numbers >> 7
        hot = jnp.where(iota((LANES, chunk), 0) == low, 1.0, 0.0).astype(BF16)
        wide_ref[slot] = dot(table_ref[...], jnp.concatenate([hot, hot], axis=0))
        return top

    def pick(index, slot, top):
        spread = jnp.broadcast_to(top, (SUBS, chunk))
        picked = jnp.zeros((SUBS, chunk), F32)
        for place in range(high):
            picked = jnp.where(
                spread == place, wide_ref[slot, place * SUBS : (place + 1) * SUBS, :], picked
            )
        last = jnp.sum(
            jnp.where(iota((high, chunk), 0) == top, wide_ref[slot, high * SUBS :, :], 0.0),
            axis=0,
            keepdims=True,
        )
        lane_low = iota((SUBS, LANES), 1) < half
        for part in range(chunk // LANES):
            eight = picked[:, part * LANES : (part + 1) * LANES]
            ninth = jnp.broadcast_to(last[:, part * LANES : (part + 1) * LANES], (SUBS, LANES))
            peer = index * 4 + part * 2
            out_ref[peer] = jnp.where(lane_low, eight, pltpu.roll(ninth, half, 1))
            out_ref[peer + 1] = jnp.where(lane_low, pltpu.roll(eight, half, 1), ninth)

    def step(index, carry):
        tops = [look(2 * index + slot, slot) for slot in range(2)]
        for slot in range(2):
            pick(2 * index + slot, slot, tops[slot])
        return carry

    lax.fori_loop(0, devices // 8, step, 0)


def spread_colours(feat_ref, start, size):
    same = iota((GROUP, size), 0) == (iota((GROUP, size), 1) & (GROUP - 1))
    return jnp.concatenate(
        [
            jnp.where(same, feat_ref[6 + channel : 7 + channel, start : start + size], 0.0)
            for channel in range(3)
        ],
        axis=0,
    )


def render_kernel(
    place_ref, arrived_in, entry_ref, bias_ref, target_ref, mono_ref,
    image_ref, feat_ref, alpha_ref, weight_ref, send_a_ref, send_b_ref,
    wide_ref, coef_ref, arrived_ref, sems,
):
    arrived_copy = pltpu.make_async_copy(arrived_in, arrived_ref, sems.at[0])
    arrived_copy.start()
    arrived_copy.wait()
    peers = arrived_ref.shape[0]
    entries = entry_ref.shape[1]
    rows = image_ref.shape[1]
    across = image_ref.shape[2] // LANES
    groups = (rows // TILE) * across
    length = entries // (groups * GROUP)
    half = LANES // 2
    chunk = 512

    table = arrived_ref[...].reshape(peers * SUBS, LANES)
    ninth = arrived_ref[:, 0, :]
    low = iota((peers * SUBS, LANES), 1) < half
    low9 = iota((peers, LANES), 1) < half
    one, two, three = [piece.astype(F32) for piece in three_pieces(table)]
    one9, two9, three9 = [piece.astype(F32) for piece in three_pieces(ninth)]
    left = jnp.concatenate(
        [
            jnp.where(low, one, pltpu.roll(two, half, 1)),
            jnp.where(low9, pltpu.roll(two9, half, 1), one9),
        ],
        axis=0,
    ).astype(BF16)
    left_rest = jnp.concatenate(
        [jnp.where(low, three, 0.0), jnp.where(low9, 0.0, three9)], axis=0
    ).astype(BF16)
    left = jnp.concatenate([left, left_rest], axis=1)
    feat_ref[...] = jnp.zeros(feat_ref.shape, F32)
    coef_ref[...] = jnp.zeros(coef_ref.shape, F32)

    def look(index, slot_number):
        start = pl.multiple_of(index * chunk, chunk)
        slot = entry_ref[:, pl.ds(start, chunk)]
        within = slot & (half - 1)
        owner = slot >> 6
        hot = jnp.where((iota((LANES, chunk), 0) & (half - 1)) == within, 1.0, 0.0).astype(BF16)
        wide_ref[slot_number] = dot(left, jnp.concatenate([hot, hot], axis=0))
        return owner

    def gather(index, slot_number, owner):
        start = pl.multiple_of(index * chunk, chunk)
        spread = jnp.broadcast_to(owner, (SUBS, chunk))
        picked = jnp.zeros((SUBS, chunk), F32)
        for place in range(peers):
            picked = jnp.where(spread == place, wide_ref[slot_number, place * SUBS : (place + 1) * SUBS, :], picked)
        last = jnp.sum(
            jnp.where(iota((peers, chunk), 0) == owner, wide_ref[slot_number, peers * SUBS :, :], 0.0),
            axis=0,
            keepdims=True,
        )
        feat_ref[0:SUBS, pl.ds(start, chunk)] = picked
        feat_ref[SUBS : SUBS + 1, pl.ds(start, chunk)] = last
        center_x = picked[0:1]
        center_y = picked[1:2]
        conic_xx = picked[2:3]
        conic_xy = picked[3:4]
        conic_yy = picked[4:5]
        lin_x = conic_xx * center_x + conic_xy * center_y
        lin_y = conic_xy * center_x + conic_yy * center_y
        constant = picked[5:6] - 0.5 * (center_x * lin_x + center_y * lin_y)
        coef_ref[slot_number, 0:1] = (-0.5 * LOG2E) * conic_xx
        coef_ref[slot_number, 1:2] = -LOG2E * conic_xy
        coef_ref[slot_number, 2:3] = (-0.5 * LOG2E) * conic_yy
        coef_ref[slot_number, 3:4] = LOG2E * lin_x
        coef_ref[slot_number, 4:5] = LOG2E * lin_y
        coef_ref[slot_number, 5:6] = LOG2E * constant + bias_ref[:, pl.ds(start, chunk)]
        for number, piece in enumerate(three_pieces(coef_ref[slot_number, 0:SUBS])):
            coef_ref[slot_number, number * SUBS : (number + 1) * SUBS] = piece.astype(F32)
        columns = jnp.transpose(coef_ref[slot_number]).astype(BF16)
        alpha_ref[pl.ds(start, chunk), :] = jnp.exp2(dot(columns, mono_ref[...]))

    def gather_two(index, carry):
        owners = [look(2 * index + number, number) for number in range(2)]
        for number in range(2):
            gather(2 * index + number, number, owners[number])
        return carry

    lax.fori_loop(0, entries // (2 * chunk), gather_two, 0)

    pixels = TILE * TILE
    step_rows = length * GROUP

    def scan(number, keeps):
        new_keeps = []
        for group in range(groups):
            at = pl.ds(
                pl.multiple_of(group * step_rows + number * 2 * GROUP, 2 * GROUP), 2 * GROUP
            )
            alpha = alpha_ref[at, :]
            first = keeps[group] * alpha[0:GROUP]
            keep = keeps[group] - first
            second = keep * alpha[GROUP:]
            new_keeps.append(keep - second)
            high, rest = two_pieces(jnp.concatenate([first, second], axis=0))
            weight_ref[at, 0:pixels] = high
            weight_ref[at, pixels:] = rest
        return tuple(new_keeps)

    keeps = tuple(jnp.ones((GROUP, pixels), F32) for _ in range(groups))
    lax.fori_loop(0, length // 2, scan, keeps, unroll=4)
    for group in range(groups):
        here = slice(group * step_rows, (group + 1) * step_rows)
        left = jnp.concatenate(
            two_pieces(spread_colours(feat_ref, group * step_rows, step_rows)), axis=0
        )
        sums = dot(left, weight_ref[here, 0:pixels]) + dot(left, weight_ref[here, pixels:])
        row = (group // across) * TILE
        col = (group % across) * LANES
        for channel in range(3):
            at = channel * GROUP
            total = sums[at : at + GROUP] + sums[at + 3 * GROUP : at + 4 * GROUP]
            for part in range(2):
                image_ref[
                    channel, row + part * SUBS : row + (part + 1) * SUBS, col : col + LANES
                ] = block_transpose(total[:, part * LANES : (part + 1) * LANES])

    blocks = rows // SUBS
    lane_block = iota((SUBS, LANES), 1) // TILE
    even = place_ref[1] % 2 == 0
    for vector in range(6 * blocks // SUBS):
        at_left = jnp.zeros((SUBS, LANES), F32)
        at_right = jnp.zeros((SUBS, LANES), F32)
        for place in range(SUBS):
            number = vector * SUBS + place
            source = image_ref if number // blocks < 3 else target_ref
            channel = (number // blocks) % 3
            top = (number % blocks) * SUBS
            first = source[channel, top : top + SUBS, 0:LANES]
            final = source[channel, top : top + SUBS, (across - 1) * LANES :]
            if place:
                first = pltpu.roll(first, TILE * place, 1)
            if place != SUBS - 1:
                final = pltpu.roll(final, TILE * (place + 1), 1)
            at_left = jnp.where(lane_block == place, first, at_left)
            at_right = jnp.where(lane_block == place, final, at_right)
        send_a_ref[vector * SUBS : (vector + 1) * SUBS, :] = jnp.where(even, at_right, at_left)
        send_b_ref[vector * SUBS : (vector + 1) * SUBS, :] = jnp.where(even, at_left, at_right)


def lane_shift(block, shift, axis=1):
    shift %= block.shape[axis]
    return pltpu.roll(block, shift, axis) if shift else block


def strip_kernel(
    place_ref, got_a_in, got_b_in, image_ref, target_ref, side_ref, send_a_ref, send_b_ref,
    got_a_ref, got_b_ref, sems,
):
    copies = [
        pltpu.make_async_copy(got_a_in, got_a_ref, sems.at[0]),
        pltpu.make_async_copy(got_b_in, got_b_ref, sems.at[1]),
    ]
    for copy in copies:
        copy.start()
    for copy in copies:
        copy.wait()
    rows = image_ref.shape[1]
    cols = image_ref.shape[2]
    blocks = rows // SUBS
    lane_block = iota((SUBS, LANES), 1) // TILE
    even = place_ref[1] % 2 == 0
    for vector in range(6 * blocks // SUBS):
        got_a = got_a_ref[vector * SUBS : (vector + 1) * SUBS, :]
        got_b = got_b_ref[vector * SUBS : (vector + 1) * SUBS, :]
        from_right = jnp.where(even, got_a, got_b)
        from_left = jnp.where(even, got_b, got_a)
        for place in range(SUBS):
            number = vector * SUBS + place
            right = lane_shift(from_right, -TILE * place)
            left = lane_shift(from_left, -TILE * (place + 1))
            top = (number % blocks) * SUBS
            side_ref[number // blocks, top : top + SUBS, :] = jnp.where(
                lane_block == 0, right, jnp.where(lane_block == SUBS - 1, left, 0.0)
            )

    def packed(main, rest, shift):
        wide_sub = iota((SUBS, cols), 0) // 2
        side_sub = iota((SUBS, LANES), 0) // 2
        wides = []
        sides = []
        for number in range(6):
            source = image_ref if number < 3 else target_ref
            wides.append(source[number % 3, main : main + SUBS, :])
            sides.append(side_ref[number, main : main + SUBS, :])
        for first in (0, 4):
            wide = jnp.zeros((SUBS, cols), F32)
            side = jnp.zeros((SUBS, LANES), F32)
            for number in range(first, min(first + 4, 6)):
                source = image_ref if number < 3 else target_ref
                turn = 2 * (number - first) - shift
                block = lane_shift(source[number % 3, rest : rest + SUBS, :], turn, 0)
                wide = jnp.where(wide_sub == number - first, block, wide)
                block = lane_shift(side_ref[number, rest : rest + SUBS, :], turn, 0)
                side = jnp.where(side_sub == number - first, block, side)
            wides.append(wide)
            sides.append(side)
        lane_part = iota((SUBS, LANES), 1) // (2 * TILE)
        last = []
        for first in (0, 4):
            total = jnp.zeros((SUBS, LANES), F32)
            for part in range(4):
                moved = lane_shift(sides[first + part], TILE + 2 * TILE * part)
                total = jnp.where(lane_part == part, moved, total)
            last.append(total)
        return wides, last

    even_row = place_ref[0] % 2 == 0
    top, top_last = packed(0, SUBS, 0)
    bottom, bottom_last = packed(rows - SUBS, rows - 2 * SUBS, 6)
    for number in range(SUBS):
        here = slice(number * SUBS, (number + 1) * SUBS)
        send_a_ref[here, :] = jnp.where(even_row, bottom[number], top[number])
        send_b_ref[here, :] = jnp.where(even_row, top[number], bottom[number])
    for number in range(2):
        here = slice(number * LANES, (number + 1) * LANES)
        send_a_ref[SUBS * SUBS :, here] = jnp.where(even_row, bottom_last[number], top_last[number])
        send_b_ref[SUBS * SUBS :, here] = jnp.where(even_row, top_last[number], bottom_last[number])


def back_kernel(
    place_ref, got_a_in, got_b_in, image_ref, target_ref, side_ref, entry_ref, feat_ref,
    alpha_ref, weight_ref, down_ref, down_back_ref, across_ref, across_back_ref, mono_ref,
    out_ref,
    raw_ref, vert_ref, blur_ref, coef_ref, grad_ref, ahead_ref, pair_ref,
    right_ref, slope_ref, mask_ref, sum_ref, got_a_ref, got_b_ref, sems,
):
    rows = image_ref.shape[1]
    cols = image_ref.shape[2]
    wide = cols + LANES
    entries = entry_ref.shape[1]
    across = cols // LANES
    groups = (rows // TILE) * across
    length = entries // (groups * GROUP)
    tall = rows + 2 * HALO
    mid = rows + 2 * SUBS
    peers = out_ref.shape[0]
    half = LANES // 2

    got_copies = [
        pltpu.make_async_copy(got_a_in, got_a_ref, sems.at[0]),
        pltpu.make_async_copy(got_b_in, got_b_ref, sems.at[1]),
    ]
    for copy in got_copies:
        copy.start()
    for copy in got_copies:
        copy.wait()
    even_row = place_ref[0] % 2 == 0
    for number in range(6):
        source = image_ref if number < 3 else target_ref
        raw_ref[number, 0:rows, 0:cols] = source[number % 3]
        raw_ref[number, 0:rows, cols:] = side_ref[number]
    lane_block = iota((SUBS, LANES), 1) // TILE
    border = (lane_block == 0) | (lane_block == SUBS - 1)
    for below in (True, False):
        def got(rows_here, cols_here):
            got_a = got_a_ref[rows_here, cols_here]
            got_b = got_b_ref[rows_here, cols_here]
            return jnp.where(even_row, got_a, got_b) if below else jnp.where(even_row, got_b, got_a)

        main_at = rows if below else tall - SUBS
        rest_at = rows + SUBS if below else tall - 2 * SUBS
        goal = 0 if below else 3
        wide_keep = iota((SUBS, cols), 0) // 2 == goal
        side_keep = iota((SUBS, LANES), 0) // 2 == goal
        wides = [got(slice(number * SUBS, (number + 1) * SUBS), slice(0, cols)) for number in range(SUBS)]
        lasts = [
            got(slice(SUBS * SUBS, (SUBS + 1) * SUBS), slice(number * LANES, (number + 1) * LANES))
            for number in range(2)
        ]
        sides = [
            jnp.where(border, lane_shift(lasts[number // 4], -TILE - 2 * TILE * (number % 4)), 0.0)
            for number in range(SUBS)
        ]
        for number in range(6):
            raw_ref[number, main_at : main_at + SUBS, 0:cols] = wides[number]
            raw_ref[number, main_at : main_at + SUBS, cols:] = sides[number]
            turn = 2 * (goal - number % 4)
            block = lane_shift(wides[6 + number // 4], turn, 0)
            raw_ref[number, rest_at : rest_at + SUBS, 0:cols] = jnp.where(wide_keep, block, 0.0)
            block = lane_shift(sides[6 + number // 4], turn, 0)
            raw_ref[number, rest_at : rest_at + SUBS, cols:] = jnp.where(side_keep, block, 0.0)
    down = down_ref[...]
    for channel in range(3):
        shown = raw_ref[channel]
        wanted = raw_ref[3 + channel]
        for number, value in enumerate(
            [shown, wanted, shown * shown + wanted * wanted, shown * wanted]
        ):
            at = (channel * 4 + number) * mid
            vert_ref[at : at + mid, :] = dot_full(down, value)
    for part in range(3):
        at = part * 4 * mid
        blur_ref[at : at + 4 * mid, :] = dot_full(vert_ref[at : at + 4 * mid, :], across_ref[...])
    line = iota((mid, wide), 0) - SUBS + place_ref[0] * rows
    spot = iota((mid, wide), 1)
    spot = jnp.where(spot < cols + half, spot, spot - wide) + place_ref[1] * cols
    inside = (
        (line >= 0) & (line < place_ref[2] * rows) & (spot >= 0) & (spot < place_ref[3] * cols)
    )
    down_back = down_back_ref[...]
    for channel in range(3):
        at = channel * 4 * mid
        mean_r, mean_t, squares, cross = [
            blur_ref[at + number * mid : at + (number + 1) * mid, :] for number in range(4)
        ]
        upper_one = 2.0 * mean_r * mean_t + STAB_ONE
        upper_two = 2.0 * (cross - mean_r * mean_t) + STAB_TWO
        lower_one = mean_r * mean_r + mean_t * mean_t + STAB_ONE
        lower_two = squares - mean_r * mean_r - mean_t * mean_t + STAB_TWO
        inv_one = 1.0 / lower_one
        inv_two = 1.0 / lower_two
        inverse = inv_one * inv_two
        value = upper_one * upper_two * inverse
        on_mean = (
            2.0 * mean_t * (upper_two - upper_one) * inverse
            + 2.0 * mean_r * value * (inv_two - inv_one)
        )
        on_square = -value * inv_two
        on_cross = 2.0 * upper_one * inverse
        for number, part in enumerate([on_mean, on_square, on_cross]):
            part = jnp.where(inside, -WEIGHT_SSIM * part, 0.0)
            spot_at = (channel * 3 + number) * rows
            high, rest = two_pieces(part)
            coef_ref[spot_at : spot_at + rows, :] = dot(
                down_back, jnp.concatenate([high, rest, high], axis=0)
            )
    for channel in range(3):
        at = channel * 3 * rows
        high, rest = two_pieces(coef_ref[at : at + 3 * rows, :])
        back = dot(jnp.concatenate([high, rest, high], axis=1), across_back_ref[...])
        shown = image_ref[channel]
        wanted = target_ref[channel]
        gap = shown - wanted
        grad_ref[channel] = (
            (1.0 - WEIGHT_SSIM) * gap * lax.rsqrt(gap * gap + SMOOTHING * SMOOTHING)
            + back[0:rows]
            + 2.0 * shown * back[rows : 2 * rows]
            + wanted * back[2 * rows :]
        )

    pixels = TILE * TILE
    step_rows = length * GROUP
    mono = mono_ref[0 : 2 * SUBS, :]
    mono = jnp.concatenate([mono, mono], axis=1)
    same = iota((SUBS, step_rows), 0) == (iota((SUBS, step_rows), 1) & (GROUP - 1))
    slope_ref[...] = jnp.zeros(slope_ref.shape, F32)

    for group in range(groups):
        row = (group // across) * TILE
        col = (group % across) * LANES
        start = group * step_rows
        slopes = []
        for channel in range(3):
            for part in range(2):
                slopes.append(
                    block_transpose(
                        grad_ref[channel, row + part * SUBS : row + (part + 1) * SUBS, col : col + LANES]
                    )
                )
        slopes = jnp.concatenate(
            [jnp.concatenate(slopes[2 * channel : 2 * channel + 2], axis=1) for channel in range(3)],
            axis=0,
        )
        high, rest = [piece.astype(F32) for piece in two_pieces(slopes)]
        at = group * 6 * GROUP
        both = jnp.concatenate([high, rest], axis=0)
        right_ref[at : at + 6 * GROUP, 0:pixels] = both
        right_ref[at : at + 6 * GROUP, pixels:] = both
        top, low = [
            piece.astype(F32)
            for piece in two_pieces(spread_colours(feat_ref, start, step_rows))
        ]
        left = jnp.transpose(jnp.concatenate([top, low, top], axis=0)).astype(BF16)
        ahead_ref[start : start + step_rows, :] = dot(
            left, jnp.concatenate([high, high, rest], axis=0).astype(BF16)
        )

    def step(number, behinds):
        new_behinds = []
        at = (length // 2 - 1 - number) * 2 * GROUP
        for group in range(groups):
            source = pl.ds(pl.multiple_of(group * step_rows + at, 2 * GROUP), 2 * GROUP)
            alpha = alpha_ref[source, :]
            ahead = ahead_ref[source, :]
            weight = weight_ref[source, 0:pixels].astype(F32) + weight_ref[source, pixels:].astype(F32)
            behind = behinds[group]
            second = ahead[GROUP:] - behind
            behind = behind + alpha[GROUP:] * second
            first = ahead[0:GROUP] - behind
            new_behinds.append(behind + alpha[0:GROUP] * first)
            high, rest = two_pieces(weight * jnp.concatenate([first, second], axis=0))
            pair_ref[source, 0:pixels] = high
            pair_ref[source, pixels:] = rest
        return tuple(new_behinds)

    zero = jnp.zeros((GROUP, pixels), F32)
    lax.fori_loop(0, length // 2, step, tuple(zero for _ in range(groups)), unroll=4)

    for group in range(groups):
        here = slice(group * step_rows, (group + 1) * step_rows)
        at = group * 6 * GROUP
        moments = dot_nt(mono, pair_ref[here, :])
        tints = dot_nt(right_ref[at : at + 6 * GROUP, :].astype(BF16), weight_ref[here, :])
        on_xx = moments[0:1]
        on_xy = moments[1:2]
        on_yy = moments[2:3]
        on_x = moments[3:4]
        on_y = moments[4:5]
        on_one = moments[5:6]
        center_x = feat_ref[0:1, here]
        center_y = feat_ref[1:2, here]
        conic_xx = feat_ref[2:3, here]
        conic_xy = feat_ref[3:4, here]
        conic_yy = feat_ref[4:5, here]
        near_x = on_x - center_x * on_one
        near_y = on_y - center_y * on_one
        slope_ref[0:1, here] = conic_xx * near_x + conic_xy * near_y
        slope_ref[1:2, here] = conic_xy * near_x + conic_yy * near_y
        slope_ref[2:3, here] = -0.5 * (on_xx - center_x * (on_x + near_x))
        slope_ref[3:4, here] = -(on_xy - center_y * on_x - center_x * near_y)
        slope_ref[4:5, here] = -0.5 * (on_yy - center_y * (on_y + near_y))
        slope_ref[5:6, here] = on_one
        for channel in range(3):
            at = SUBS * channel
            both = tints[at : at + SUBS] + tints[at + 24 : at + 24 + SUBS]
            slope_ref[6 + channel : 7 + channel, here] = jnp.sum(
                jnp.where(same, both, 0.0), axis=0, keepdims=True
            )

    chunk = 512
    tops = peers * SUBS
    sum_ref[...] = jnp.zeros(sum_ref.shape, F32)
    pair_step = iota((2 * SUBS, chunk), 0) // SUBS

    def collect(index, part):
        start = pl.multiple_of(index * chunk, chunk)
        slot = entry_ref[:, pl.ds(start, chunk)]
        within = slot & (half - 1)
        owner = slot >> 6
        hot = jnp.where((iota((LANES, chunk), 0) & (half - 1)) == within, 1.0, 0.0).astype(BF16)
        values = [
            piece.astype(F32) for piece in two_pieces(slope_ref[0:SUBS, pl.ds(start, chunk)])
        ]
        values = [jnp.concatenate([value, value], axis=0) for value in values]
        offset = jnp.broadcast_to(owner, (2 * SUBS, chunk)) - pair_step
        for place in range(peers // 2):
            hit = offset == 2 * place
            for number in range(2):
                at = number * (tops + peers) + place * 2 * SUBS
                mask_ref[part, at : at + 2 * SUBS, :] = jnp.where(hit, values[number], 0.0).astype(BF16)
        hit = iota((peers, chunk), 0) == owner
        for number, piece in enumerate(
            two_pieces(slope_ref[SUBS : SUBS + 1, pl.ds(start, chunk)])
        ):
            at = number * (tops + peers) + tops
            mask_ref[part, at : at + peers, :] = jnp.where(hit, piece.astype(F32), 0.0).astype(BF16)
        return dot_nt(mask_ref[part], hot)

    def collect_two(index, carry):
        sum_ref[...] += collect(2 * index, 0) + collect(2 * index + 1, 1)
        return carry

    lax.fori_loop(0, entries // (2 * chunk), collect_two, 0)
    lane_low = iota((SUBS, LANES), 1) < half
    for place in range(peers):
        at = place * SUBS
        eight = sum_ref[at : at + SUBS, :] + sum_ref[tops + peers + at : tops + peers + at + SUBS, :]
        at = tops + place
        ninth = sum_ref[at : at + 1, :] + sum_ref[tops + peers + at : tops + peers + at + 1, :]
        out_ref[place] = jnp.where(lane_low, eight, jnp.broadcast_to(ninth, (SUBS, LANES)))


def return_kernel(
    place_ref, returned_ref, got_ref, jac_in, cam_ref, grad_out,
    row_ref, mask_ref, sum_ref, pack_ref, jac_ref, grad_ref, sems, jac_sems,
):
    jac_copy = pltpu.make_async_copy(jac_in, jac_ref, jac_sems.at[0])
    jac_copy.start()
    devices = got_ref.shape[0]
    count, own = grad_ref.shape
    high = own // LANES
    half = LANES // 2
    tops = high * SUBS
    part_rows = tops + high
    chunk = 4 * LANES
    cam = [[cam_ref[row, col] for col in range(3)] for row in range(3)]
    fill_numbers(place_ref, got_ref, row_ref)
    sum_ref[...] = jnp.zeros(sum_ref.shape, F32)
    lane_low = iota((SUBS, LANES), 1) < half
    pair_step = iota((2 * SUBS, chunk), 0) // SUBS

    def collect(index, part):
        numbers = row_ref[:, pl.ds(pl.multiple_of(index * chunk, chunk), chunk)]
        low = numbers & (LANES - 1)
        top = numbers >> 7
        hot = jnp.where(iota((LANES, chunk), 0) == low, 1.0, 0.0).astype(BF16)
        eights = []
        ninths = []
        for pair in range(chunk // LANES):
            first = returned_ref[index * 8 + 2 * pair]
            second = returned_ref[index * 8 + 2 * pair + 1]
            eights.append(jnp.where(lane_low, first, pltpu.roll(second, half, 1)))
            ninths.append(jnp.where(lane_low, pltpu.roll(first, half, 1), second)[0:1])
        values = [piece.astype(F32) for piece in two_pieces(jnp.concatenate(eights, axis=1))]
        values = [jnp.concatenate([value, value], axis=0) for value in values]
        offset = jnp.broadcast_to(top, (2 * SUBS, chunk)) - pair_step
        for place in range(high // 2):
            hit = offset == 2 * place
            for number in range(2):
                at = number * part_rows + place * 2 * SUBS
                mask_ref[part, at : at + 2 * SUBS, :] = jnp.where(hit, values[number], 0.0).astype(BF16)
        hit = iota((high, chunk), 0) == top
        for number, piece in enumerate(two_pieces(jnp.concatenate(ninths, axis=1))):
            at = number * part_rows + tops
            mask_ref[part, at : at + high, :] = jnp.where(hit, piece.astype(F32), 0.0).astype(BF16)
        return dot_nt(mask_ref[part], hot)

    def collect_two(index, carry):
        sum_ref[...] += collect(2 * index, 0) + collect(2 * index + 1, 1)
        return carry

    lax.fori_loop(0, devices * half // (2 * chunk), collect_two, 0)
    jac_copy.wait()

    def grad_copy(index):
        at = pl.ds(pl.multiple_of(index * SUBS * LANES, SUBS * LANES), SUBS * LANES)
        return pltpu.make_async_copy(grad_ref.at[:, at], grad_out.at[:, at], sems.at[index])

    def block(index, carry):
        start = pl.multiple_of(index * SUBS, SUBS)

        def jac(number):
            return jac_ref[pl.ds(number * high + start, SUBS), :]

        slopes = []
        for number in range(SUBS):
            at = start * SUBS + number
            slopes.append(
                sum_ref[pl.ds(at, SUBS, stride=SUBS), :]
                + sum_ref[pl.ds(part_rows + at, SUBS, stride=SUBS), :]
            )
        at = tops + start
        slopes.append(sum_ref[pl.ds(at, SUBS), :] + sum_ref[pl.ds(part_rows + at, SUBS), :])
        on_center = [slopes[0] * jac(30), slopes[1] * jac(31)]
        conic_xx = jac(48)
        conic_xy = jac(49)
        conic_yy = jac(50)
        on_xx, on_xy, on_yy = slopes[2:5]
        first_x = conic_xx * on_xx + conic_xy * on_xy
        first_y = conic_xy * on_xy + conic_yy * on_yy
        on_first = -(conic_xx * first_x + conic_xy * conic_xy * on_yy)
        on_second = -(conic_xy * conic_xy * on_xx + conic_yy * first_y)
        on_mixed = -(
            2.0 * conic_xx * conic_xy * on_xx
            + (conic_xx * conic_yy + conic_xy * conic_xy) * on_xy
            + 2.0 * conic_xy * conic_yy * on_yy
        )
        out = []
        for axis in range(3):
            out.append(
                cam[0][axis] * on_center[0]
                + cam[1][axis] * on_center[1]
                + slopes[6] * jac(21 + axis)
                + slopes[7] * jac(24 + axis)
                + slopes[8] * jac(27 + axis)
            )
        for number in range(7):
            out.append(
                on_first * jac(number) + on_mixed * jac(7 + number) + on_second * jac(14 + number)
            )
        out.append(slopes[5] * jac(32))
        for channel in range(3):
            out.append(SH_ZERO * slopes[6 + channel])
            for term in range(1, 16):
                out.append(slopes[6 + channel] * jac(32 + term))
        for number, value in enumerate(out):
            pack_ref[number * SUBS : (number + 1) * SUBS, :] = value
        for first in range(0, count, SUBS):
            number = min(SUBS, count - first)
            for place in range(SUBS):
                at = pl.ds(pl.multiple_of((start + place) * LANES, LANES), LANES)
                grad_ref[first : first + number, at] = pack_ref[
                    pl.ds(first * SUBS + place, number, stride=SUBS), :
                ]
        grad_copy(index).start()
        return carry

    lax.fori_loop(0, high // SUBS, block, 0)
    for index in range(high // SUBS):
        grad_copy(index).wait()


def band(outs, ins):
    taps = np.exp(-((np.arange(11) - 5.0) ** 2) / (2.0 * BLUR_SIGMA * BLUR_SIGMA))
    offset = np.asarray(ins)[None, :] - np.asarray(outs)[:, None]
    values = np.exp(-(offset**2) / (2.0 * BLUR_SIGMA * BLUR_SIGMA)) / taps.sum()
    return np.where(np.abs(offset) <= RIM, values, 0.0).astype(np.float32)


def band_pieces(values):
    high = values.astype(ml_dtypes.bfloat16)
    rest = (values - high.astype(np.float32)).astype(ml_dtypes.bfloat16)
    return [high, high, rest]


def monomials():
    pixel = np.arange(TILE * TILE)
    x = (pixel % TILE) - 7.5
    y = (pixel // TILE) - 7.5
    eight = np.stack([x * x, x * y, y * y, x, y, x * 0 + 1, x * 0, x * 0])
    return np.concatenate([eight, eight, eight, eight * 0]).astype(np.float32)


def call(body, out_shape, scratch, scalar_at, args, flops, vmem, outside=(), outs_outside=()):
    in_specs = [
        pl.BlockSpec(
            memory_space=pltpu.SMEM
            if number in scalar_at
            else pl.ANY
            if number in outside
            else pltpu.VMEM
        )
        for number in range(len(args))
    ]
    if isinstance(out_shape, tuple):
        out_specs = tuple(
            pl.BlockSpec(memory_space=pl.ANY if number in outs_outside else pltpu.VMEM)
            for number in range(len(out_shape))
        )
    else:
        out_specs = pl.BlockSpec(memory_space=pl.ANY if outs_outside else pltpu.VMEM)
    return pl.pallas_call(
        body,
        out_shape=out_shape,
        in_specs=in_specs,
        out_specs=out_specs,
        scratch_shapes=scratch,
        compiler_params=pltpu.CompilerParams(vmem_limit_bytes=vmem * MIB),
        cost_estimate=pl.CostEstimate(flops=flops, bytes_accessed=1 << 20, transcendentals=0),
    )(*args)


def swap_pairs(count, first):
    pairs = []
    for low in range(first, count - 1, 2):
        pairs += [(low, low + 1), (low + 1, low)]
    return pairs


def swap(value_a, value_b, axis):
    count = lax.axis_size(axis)
    got_b = lax.ppermute(value_b, axis, swap_pairs(count, 1))
    got_a = lax.ppermute(value_a, axis, swap_pairs(count, 0))
    return got_a, got_b


def exchange(payload):
    return lax.all_to_all(payload, ("img", "cell"), split_axis=0, concat_axis=0, tiled=True)


def shards(attributes, camera, target, visible_index, tile_lists, tile_len):
    img_count = lax.axis_size("img")
    cell_count = lax.axis_size("cell")
    devices = img_count * cell_count
    slots = visible_index.shape[1]
    count, own = attributes.shape
    high = own // LANES
    _, rows, cols = target.shape
    tiles_down, tiles_across, length = tile_lists.shape
    entries = tiles_down * tiles_across * length
    wide = cols + LANES
    mid = rows + 2 * SUBS
    tall = rows + 2 * HALO
    place = jnp.stack(
        [
            lax.axis_index("img"),
            lax.axis_index("cell"),
            jnp.int32(img_count),
            jnp.int32(cell_count),
        ]
    ).astype(jnp.int32)

    assert 2 * (slots // devices) == LANES
    asked = call(
        ask_kernel,
        jax.ShapeDtypeStruct((devices, LANES), jnp.int32),
        [],
        (),
        (visible_index,),
        1 << 14,
        2,
    )
    got = exchange(asked)

    table, jac = call(
        owner_kernel,
        (
            jax.ShapeDtypeStruct((high * (SUBS + 1), 2 * LANES), BF16),
            jax.ShapeDtypeStruct((JAC_ROWS * high, LANES), F32),
        ),
        [pltpu.VMEM((count * high, LANES), F32), pltpu.VMEM((high * (SUBS + 1), LANES), F32)],
        (1,),
        (attributes, camera),
        1 << 24,
        12,
    )
    reply = call(
        reply_kernel,
        jax.ShapeDtypeStruct((devices, SUBS, LANES), F32),
        [
            pltpu.VMEM((1, slots), jnp.int32),
            pltpu.VMEM((2, high * (SUBS + 1), 2 * LANES), F32),
            pltpu.VMEM((devices, LANES), jnp.int32),
            pltpu.SemaphoreType.DMA((1,)),
        ],
        (0,),
        (place, table, got),
        1 << 24,
        2 + slots // 128,
        outside=(2,),
    )
    arrived = exchange(reply)

    order = (tiles_down, tiles_across // GROUP, GROUP, length)
    entry = tile_lists.reshape(order).transpose(0, 1, 3, 2).reshape(1, entries)
    live = jnp.arange(length, dtype=jnp.int32)[None, None, :, None] < tile_len.reshape(
        tiles_down, tiles_across // GROUP, 1, GROUP
    )
    bias = jnp.where(live, 0.0, -1e30).astype(F32).reshape(1, entries)
    mono = jnp.asarray(monomials()).astype(BF16)
    packed = 6 * rows // SUBS
    pixels = TILE * TILE
    group_rows = length * GROUP
    groups = entries // group_rows
    strip = jax.ShapeDtypeStruct((packed, LANES), F32)
    image, feat, alpha, weight, send_a, send_b = call(
        render_kernel,
        (
            jax.ShapeDtypeStruct((3, rows, cols), F32),
            jax.ShapeDtypeStruct((2 * SUBS, entries), F32),
            jax.ShapeDtypeStruct((entries, pixels), F32),
            jax.ShapeDtypeStruct((entries, 2 * pixels), BF16),
            strip,
            strip,
        ),
        [
            pltpu.VMEM((2, devices * (SUBS + 1), 512), F32),
            pltpu.VMEM((2, 32, 512), F32),
            pltpu.VMEM((devices, SUBS, LANES), F32),
            pltpu.SemaphoreType.DMA((1,)),
        ],
        (0,),
        (place, arrived, entry, bias, target, mono),
        1 << 26,
        16 + devices // 8,
        outside=(1,),
    )
    got_a, got_b = swap(send_a, send_b, "cell")
    edge = jax.ShapeDtypeStruct(((SUBS + 1) * SUBS, cols), F32)
    side, send_a, send_b = call(
        strip_kernel,
        (jax.ShapeDtypeStruct((6, rows, LANES), F32), edge, edge),
        [
            pltpu.VMEM((packed, LANES), F32),
            pltpu.VMEM((packed, LANES), F32),
            pltpu.SemaphoreType.DMA((2,)),
        ],
        (0,),
        (place, got_a, got_b, image, target),
        1 << 20,
        4,
        outside=(1, 2),
    )
    got_a, got_b = swap(send_a, send_b, "img")

    tall_at = np.arange(tall)
    tall_at = np.where(tall_at < rows + HALO, tall_at, tall_at - tall)
    mid_at = np.arange(mid) - SUBS
    wide_at = np.arange(wide)
    wide_at = np.where(wide_at < cols + LANES // 2, wide_at, wide_at - wide)
    down = jnp.asarray(band(mid_at, tall_at))
    down_back = jnp.asarray(np.concatenate(band_pieces(band(np.arange(rows), mid_at)), axis=1))
    across = jnp.asarray(band(wide_at, wide_at))
    across_back = jnp.asarray(np.concatenate(band_pieces(band(wide_at, np.arange(cols))), axis=0))
    slot_grads = call(
        back_kernel,
        jax.ShapeDtypeStruct((devices, SUBS, LANES), F32),
        [
            pltpu.VMEM((6, tall, wide), F32),
            pltpu.VMEM((12 * mid, wide), F32),
            pltpu.VMEM((12 * mid, wide), F32),
            pltpu.VMEM((9 * rows, wide), F32),
            pltpu.VMEM((3, rows, cols), F32),
            pltpu.VMEM((entries, pixels), F32),
            pltpu.VMEM((entries, 2 * pixels), BF16),
            pltpu.VMEM((groups * 6 * GROUP, 2 * pixels), F32),
            pltpu.VMEM((2 * SUBS, entries), F32),
            pltpu.VMEM((2, 2 * devices * (SUBS + 1), 512), BF16),
            pltpu.VMEM((2 * devices * (SUBS + 1), LANES), F32),
            pltpu.VMEM(((SUBS + 1) * SUBS, cols), F32),
            pltpu.VMEM(((SUBS + 1) * SUBS, cols), F32),
            pltpu.SemaphoreType.DMA((2,)),
        ],
        (0,),
        (
            place, got_a, got_b, image, target, side, entry, feat, alpha, weight,
            down, down_back, across, across_back, mono,
        ),
        1 << 27,
        32 + devices // 8,
        outside=(1, 2),
    )
    returned = exchange(slot_grads)
    return call(
        return_kernel,
        jax.ShapeDtypeStruct((count, own), F32),
        [
            pltpu.VMEM((1, slots), jnp.int32),
            pltpu.VMEM((2, 2 * high * (SUBS + 1), 4 * LANES), BF16),
            pltpu.VMEM((2 * high * (SUBS + 1), LANES), F32),
            pltpu.VMEM((count * SUBS, LANES), F32),
            pltpu.VMEM((JAC_ROWS * high, LANES), F32),
            pltpu.VMEM((count, own), F32),
            pltpu.SemaphoreType.DMA((high // SUBS,)),
            pltpu.SemaphoreType.DMA((1,)),
        ],
        (0, 4),
        (place, returned, got, jac, camera),
        1 << 26,
        12,
        outside=(3,),
        outs_outside=(0,),
    )


def solution(mesh):
    return jax.shard_map(
        shards,
        mesh=mesh,
        in_specs=(
            P(None, ("img", "cell")),
            P(),
            P(None, "img", "cell"),
            P(("img", "cell"), None),
            P("img", "cell", None),
            P("img", "cell"),
        ),
        out_specs=P(None, ("img", "cell")),
        check_vma=False,
    )
```

```python
import jax
import jax.numpy as jnp
import ml_dtypes
import numpy as np
from jax import lax
from jax.experimental import pallas as pl
from jax.experimental.pallas import tpu as pltpu
from jax.sharding import PartitionSpec as P

TILE = 16
LANES = 128
SUBS = 8
GROUP = 8
RIM = 5
HALO = 16
WEIGHT_SSIM = 0.2
SMOOTHING = 0.01
STAB_ONE = 0.0001
STAB_TWO = 0.0009
BLUR_SIGMA = 1.5
LOG2E = 1.4426950408889634
SH_ZERO = 0.28209479177387814
SH_ONE = 0.4886025119029199
SH_TWO = (
    1.0925484305920792,
    -1.0925484305920792,
    0.31539156525252005,
    -1.0925484305920792,
    0.5462742152960396,
)
SH_THREE = (
    -0.5900435899266435,
    2.890611442640554,
    -0.4570457994644658,
    0.3731763325901154,
    -0.4570457994644658,
    1.445305721320277,
    -0.5900435899266435,
)
UNROLL = 4
F32 = jnp.float32
BF16 = jnp.bfloat16
JAC_ROWS = 51
MIB = 1024 * 1024


def harmonic_basis(unit_x, unit_y, unit_z):
    unit_xx = unit_x * unit_x
    unit_yy = unit_y * unit_y
    unit_zz = unit_z * unit_z
    return [
        -SH_ONE * unit_y,
        SH_ONE * unit_z,
        -SH_ONE * unit_x,
        SH_TWO[0] * unit_x * unit_y,
        SH_TWO[1] * unit_y * unit_z,
        SH_TWO[2] * (2.0 * unit_zz - unit_xx - unit_yy),
        SH_TWO[3] * unit_x * unit_z,
        SH_TWO[4] * (unit_xx - unit_yy),
        SH_THREE[0] * unit_y * (3.0 * unit_xx - unit_yy),
        SH_THREE[1] * unit_x * unit_y * unit_z,
        SH_THREE[2] * unit_y * (4.0 * unit_zz - unit_xx - unit_yy),
        SH_THREE[3] * unit_z * (2.0 * unit_zz - 3.0 * unit_xx - 3.0 * unit_yy),
        SH_THREE[4] * unit_x * (4.0 * unit_zz - unit_xx - unit_yy),
        SH_THREE[5] * unit_z * (unit_xx - unit_yy),
        SH_THREE[6] * unit_x * (unit_xx - 3.0 * unit_yy),
    ]


def three_pieces(value):
    first = value.astype(BF16)
    rest = value - first.astype(F32)
    second = rest.astype(BF16)
    third = (rest - second.astype(F32)).astype(BF16)
    return first, second, third


def two_pieces(value):
    first = value.astype(BF16)
    return first, (value - first.astype(F32)).astype(BF16)


def dot(left, right):
    return jnp.dot(left, right, preferred_element_type=F32)


def dot_nt(left, right):
    return lax.dot_general(left, right, (((1,), (1,)), ((), ())), preferred_element_type=F32)


def dot_full(left, right):
    return jnp.dot(left, right, preferred_element_type=F32, precision=lax.Precision.HIGHEST)


def iota(shape, dim):
    return lax.broadcasted_iota(jnp.int32, shape, dim)


def block_transpose(block):
    turn = (iota(block.shape, 0) - iota(block.shape, 1) // TILE) & (SUBS - 1)
    out = block
    for step in range(1, SUBS):
        moved = pltpu.roll(block, LANES - TILE * step, 1)
        moved = pltpu.roll(moved, step, 0)
        out = jnp.where(turn == step, moved, out)
    return out


def covariance(scale_rows, quat_rows, cam):
    scales = [jnp.exp(row) for row in scale_rows]
    quat_w = 1.5 + jnp.tanh(quat_rows[0])
    quat_x, quat_y, quat_z = quat_rows[1:]
    inverse = lax.rsqrt(quat_w * quat_w + quat_x * quat_x + quat_y * quat_y + quat_z * quat_z)
    quat_w, quat_x, quat_y, quat_z = (
        quat_w * inverse,
        quat_x * inverse,
        quat_y * inverse,
        quat_z * inverse,
    )
    rotation = [
        [
            1.0 - 2.0 * (quat_y * quat_y + quat_z * quat_z),
            2.0 * (quat_x * quat_y - quat_w * quat_z),
            2.0 * (quat_x * quat_z + quat_w * quat_y),
        ],
        [
            2.0 * (quat_x * quat_y + quat_w * quat_z),
            1.0 - 2.0 * (quat_x * quat_x + quat_z * quat_z),
            2.0 * (quat_y * quat_z - quat_w * quat_x),
        ],
        [
            2.0 * (quat_x * quat_z - quat_w * quat_y),
            2.0 * (quat_y * quat_z + quat_w * quat_x),
            1.0 - 2.0 * (quat_x * quat_x + quat_y * quat_y),
        ],
    ]
    axes = [
        [
            (
                cam[screen][0] * rotation[0][axis]
                + cam[screen][1] * rotation[1][axis]
                + cam[screen][2] * rotation[2][axis]
            )
            * scales[axis]
            for axis in range(3)
        ]
        for screen in range(2)
    ]
    first = axes[0][0] * axes[0][0] + axes[0][1] * axes[0][1] + axes[0][2] * axes[0][2] + 0.3
    mixed = axes[0][0] * axes[1][0] + axes[0][1] * axes[1][1] + axes[0][2] * axes[1][2]
    second = axes[1][0] * axes[1][0] + axes[1][1] * axes[1][1] + axes[1][2] * axes[1][2] + 0.3
    return first, mixed, second


def owner_kernel(attr_ref, cam_ref, table_ref, jac_ref, pack_ref, feat_ref):
    count, own = attr_ref.shape
    high = own // LANES
    cam = [[cam_ref[row, col] for col in range(3)] for row in range(3)]
    for first in range(0, count, SUBS):
        number = min(SUBS, count - first)
        for place in range(high):
            pack_ref[pl.ds(first * high + place, number, stride=high), :] = attr_ref[
                first : first + number, place * LANES : (place + 1) * LANES
            ]

    def block(index, carry):
        start = pl.multiple_of(index * SUBS, SUBS)

        def row(number):
            return pack_ref[pl.ds(number * high + start, SUBS), :]

        positions = [row(number) for number in range(3)]
        shape_rows = [row(3 + number) for number in range(7)]
        jac = []
        (cov_first, cov_mixed, cov_second), pull = jax.vjp(
            lambda *rows: covariance(rows[:3], rows[3:], cam), *shape_rows
        )
        one = jnp.ones_like(cov_first)
        zero = jnp.zeros_like(cov_first)
        jac += pull((one, zero, zero))
        jac += pull((zero, one, zero))
        jac += pull((zero, zero, one))
        inverse = 1.0 / (cov_first * cov_second - cov_mixed * cov_mixed)
        conic = [cov_second * inverse, -cov_mixed * inverse, cov_first * inverse]
        centers = []
        slopes = []
        for screen in range(2):
            angle = (
                cam[screen][0] * positions[0]
                + cam[screen][1] * positions[1]
                + cam[screen][2] * positions[2]
            ) / 3.0
            centers.append(7.0 * jnp.sin(angle))
            slopes.append((7.0 / 3.0) * jnp.cos(angle))
        raw = row(10)
        decay = jnp.exp(-raw)
        log_opacity = -jnp.log(1.0 + decay)
        harmonics = [[row(11 + 16 * channel + term) for term in range(16)] for channel in range(3)]

        def colours_of(pos_x, pos_y, pos_z):
            off_x = pos_x - cam[2][0]
            off_y = pos_y - cam[2][1]
            off_z = pos_z - cam[2][2]
            scale = lax.rsqrt(off_x * off_x + off_y * off_y + off_z * off_z)
            basis = harmonic_basis(off_x * scale, off_y * scale, off_z * scale)
            colours = []
            for channel in range(3):
                total = 0.5 + SH_ZERO * harmonics[channel][0]
                for term in range(1, 16):
                    total = total + basis[term - 1] * harmonics[channel][term]
                colours.append(total)
            return tuple(colours), basis

        colours, pull_colours, basis = jax.vjp(colours_of, *positions, has_aux=True)
        jac += pull_colours((one, zero, zero))
        jac += pull_colours((zero, one, zero))
        jac += pull_colours((zero, zero, one))
        jac += slopes
        jac.append(decay / (1.0 + decay))
        jac += basis
        jac += conic
        for number, value in enumerate(jac):
            jac_ref[pl.ds(number * high + start, SUBS), :] = value
        features = centers + conic + [log_opacity] + list(colours)
        for number in range(SUBS):
            feat_ref[pl.ds(start * SUBS + number, SUBS, stride=SUBS), :] = features[number]
        feat_ref[pl.ds(high * SUBS + start, SUBS), :] = features[SUBS]
        return carry

    lax.fori_loop(0, high // SUBS, block, 0)
    for number, piece in enumerate(two_pieces(feat_ref[...])):
        table_ref[:, number * LANES : (number + 1) * LANES] = piece


def ask_kernel(index_ref, out_ref):
    for pair in range(out_ref.shape[0] // 2):
        numbers = index_ref[:, pair * LANES : (pair + 1) * LANES]
        out_ref[2 * pair : 2 * pair + 2, :] = jnp.broadcast_to(numbers, (2, LANES))


def fill_numbers(place_ref, got_ref, row_ref):
    lane_low = iota((1, LANES), 1) < LANES // 2
    odd = (place_ref[0] * place_ref[3] + place_ref[1]) % 2 == 1
    for pair in range(got_ref.shape[0] // 2):
        first = got_ref[2 * pair : 2 * pair + 1, :]
        second = got_ref[2 * pair + 1 : 2 * pair + 2, :]
        row_ref[:, pair * LANES : (pair + 1) * LANES] = jnp.where(
            odd,
            jnp.where(lane_low, pltpu.roll(first, LANES // 2, 1), second),
            jnp.where(lane_low, first, pltpu.roll(second, LANES // 2, 1)),
        )


def reply_kernel(place_ref, table_ref, got_in, out_ref, row_ref, wide_ref, got_ref, sems):
    got_copy = pltpu.make_async_copy(got_in, got_ref, sems.at[0])
    got_copy.start()
    got_copy.wait()
    devices = got_ref.shape[0]
    high = table_ref.shape[0] // (SUBS + 1)
    chunk = 2 * LANES
    half = LANES // 2
    fill_numbers(place_ref, got_ref, row_ref)

    def look(index, slot):
        numbers = row_ref[:, pl.ds(pl.multiple_of(index * chunk, chunk), chunk)]
        low = numbers & (LANES - 1)
        top = numbers >> 7
        hot = jnp.where(iota((LANES, chunk), 0) == low, 1.0, 0.0).astype(BF16)
        wide_ref[slot] = dot(table_ref[...], jnp.concatenate([hot, hot], axis=0))
        return top

    def pick(index, slot, top):
        spread = jnp.broadcast_to(top, (SUBS, chunk))
        picked = jnp.zeros((SUBS, chunk), F32)
        for place in range(high):
            picked = jnp.where(
                spread == place, wide_ref[slot, place * SUBS : (place + 1) * SUBS, :], picked
            )
        last = jnp.sum(
            jnp.where(iota((high, chunk), 0) == top, wide_ref[slot, high * SUBS :, :], 0.0),
            axis=0,
            keepdims=True,
        )
        lane_low = iota((SUBS, LANES), 1) < half
        for part in range(chunk // LANES):
            eight = picked[:, part * LANES : (part + 1) * LANES]
            ninth = jnp.broadcast_to(last[:, part * LANES : (part + 1) * LANES], (SUBS, LANES))
            peer = index * 4 + part * 2
            out_ref[peer] = jnp.where(lane_low, eight, pltpu.roll(ninth, half, 1))
            out_ref[peer + 1] = jnp.where(lane_low, pltpu.roll(eight, half, 1), ninth)

    def step(index, carry):
        tops = [look(UNROLL * index + slot, slot) for slot in range(UNROLL)]
        for slot in range(UNROLL):
            pick(UNROLL * index + slot, slot, tops[slot])
        return carry

    lax.fori_loop(0, devices // (4 * UNROLL), step, 0)


def spread_colours(feat_ref, start, size):
    same = iota((GROUP, size), 0) == (iota((GROUP, size), 1) & (GROUP - 1))
    return jnp.concatenate(
        [
            jnp.where(same, feat_ref[6 + channel : 7 + channel, start : start + size], 0.0)
            for channel in range(3)
        ],
        axis=0,
    )


def render_kernel(
    place_ref, arrived_in, entry_ref, bias_ref, target_ref, mono_ref,
    image_ref, feat_ref, alpha_ref, weight_ref, send_a_ref, send_b_ref,
    wide_ref, coef_ref, arrived_ref, sems,
):
    arrived_copy = pltpu.make_async_copy(arrived_in, arrived_ref, sems.at[0])
    arrived_copy.start()
    arrived_copy.wait()
    peers = arrived_ref.shape[0]
    entries = entry_ref.shape[1]
    rows = image_ref.shape[1]
    across = image_ref.shape[2] // LANES
    groups = (rows // TILE) * across
    length = entries // (groups * GROUP)
    half = LANES // 2
    chunk = 512

    table = arrived_ref[...].reshape(peers * SUBS, LANES)
    ninth = arrived_ref[:, 0, :]
    low = iota((peers * SUBS, LANES), 1) < half
    low9 = iota((peers, LANES), 1) < half
    one, two, three = [piece.astype(F32) for piece in three_pieces(table)]
    one9, two9, three9 = [piece.astype(F32) for piece in three_pieces(ninth)]
    left = jnp.concatenate(
        [
            jnp.where(low, one, pltpu.roll(two, half, 1)),
            jnp.where(low9, pltpu.roll(two9, half, 1), one9),
        ],
        axis=0,
    ).astype(BF16)
    left_rest = jnp.concatenate(
        [jnp.where(low, three, 0.0), jnp.where(low9, 0.0, three9)], axis=0
    ).astype(BF16)
    left = jnp.concatenate([left, left_rest], axis=1)
    feat_ref[...] = jnp.zeros(feat_ref.shape, F32)
    coef_ref[...] = jnp.zeros(coef_ref.shape, F32)

    def look(index, slot_number):
        start = pl.multiple_of(index * chunk, chunk)
        slot = entry_ref[:, pl.ds(start, chunk)]
        within = slot & (half - 1)
        owner = slot >> 6
        hot = jnp.where((iota((LANES, chunk), 0) & (half - 1)) == within, 1.0, 0.0).astype(BF16)
        wide_ref[slot_number] = dot(left, jnp.concatenate([hot, hot], axis=0))
        return owner

    def gather(index, slot_number, owner):
        start = pl.multiple_of(index * chunk, chunk)
        spread = jnp.broadcast_to(owner, (SUBS, chunk))
        picked = jnp.zeros((SUBS, chunk), F32)
        for place in range(peers):
            picked = jnp.where(spread == place, wide_ref[slot_number, place * SUBS : (place + 1) * SUBS, :], picked)
        last = jnp.sum(
            jnp.where(iota((peers, chunk), 0) == owner, wide_ref[slot_number, peers * SUBS :, :], 0.0),
            axis=0,
            keepdims=True,
        )
        feat_ref[0:SUBS, pl.ds(start, chunk)] = picked
        feat_ref[SUBS : SUBS + 1, pl.ds(start, chunk)] = last
        center_x = picked[0:1]
        center_y = picked[1:2]
        conic_xx = picked[2:3]
        conic_xy = picked[3:4]
        conic_yy = picked[4:5]
        lin_x = conic_xx * center_x + conic_xy * center_y
        lin_y = conic_xy * center_x + conic_yy * center_y
        constant = picked[5:6] - 0.5 * (center_x * lin_x + center_y * lin_y)
        coef_ref[slot_number, 0:1] = (-0.5 * LOG2E) * conic_xx
        coef_ref[slot_number, 1:2] = -LOG2E * conic_xy
        coef_ref[slot_number, 2:3] = (-0.5 * LOG2E) * conic_yy
        coef_ref[slot_number, 3:4] = LOG2E * lin_x
        coef_ref[slot_number, 4:5] = LOG2E * lin_y
        coef_ref[slot_number, 5:6] = LOG2E * constant + bias_ref[:, pl.ds(start, chunk)]
        for number, piece in enumerate(three_pieces(coef_ref[slot_number, 0:SUBS])):
            coef_ref[slot_number, number * SUBS : (number + 1) * SUBS] = piece.astype(F32)
        columns = jnp.transpose(coef_ref[slot_number]).astype(BF16)
        alpha_ref[pl.ds(start, chunk), :] = jnp.exp2(dot(columns, mono_ref[...]))

    def gather_some(index, carry):
        owners = [look(UNROLL * index + number, number) for number in range(UNROLL)]
        for number in range(UNROLL):
            gather(UNROLL * index + number, number, owners[number])
        return carry

    lax.fori_loop(0, entries // (UNROLL * chunk), gather_some, 0)

    pixels = TILE * TILE
    step_rows = length * GROUP

    def scan(number, keeps):
        new_keeps = []
        for group in range(groups):
            at = pl.ds(
                pl.multiple_of(group * step_rows + number * 2 * GROUP, 2 * GROUP), 2 * GROUP
            )
            alpha = alpha_ref[at, :]
            first = keeps[group] * alpha[0:GROUP]
            keep = keeps[group] - first
            second = keep * alpha[GROUP:]
            new_keeps.append(keep - second)
            high, rest = two_pieces(jnp.concatenate([first, second], axis=0))
            weight_ref[at, 0:pixels] = high
            weight_ref[at, pixels:] = rest
        return tuple(new_keeps)

    keeps = tuple(jnp.ones((GROUP, pixels), F32) for _ in range(groups))
    lax.fori_loop(0, length // 2, scan, keeps, unroll=4)
    for group in range(groups):
        here = slice(group * step_rows, (group + 1) * step_rows)
        left = jnp.concatenate(
            two_pieces(spread_colours(feat_ref, group * step_rows, step_rows)), axis=0
        )
        sums = dot(left, weight_ref[here, 0:pixels]) + dot(left, weight_ref[here, pixels:])
        row = (group // across) * TILE
        col = (group % across) * LANES
        for channel in range(3):
            at = channel * GROUP
            total = sums[at : at + GROUP] + sums[at + 3 * GROUP : at + 4 * GROUP]
            for part in range(2):
                image_ref[
                    channel, row + part * SUBS : row + (part + 1) * SUBS, col : col + LANES
                ] = block_transpose(total[:, part * LANES : (part + 1) * LANES])

    blocks = rows // SUBS
    lane_block = iota((SUBS, LANES), 1) // TILE
    even = place_ref[1] % 2 == 0
    for vector in range(6 * blocks // SUBS):
        at_left = jnp.zeros((SUBS, LANES), F32)
        at_right = jnp.zeros((SUBS, LANES), F32)
        for place in range(SUBS):
            number = vector * SUBS + place
            source = image_ref if number // blocks < 3 else target_ref
            channel = (number // blocks) % 3
            top = (number % blocks) * SUBS
            first = source[channel, top : top + SUBS, 0:LANES]
            final = source[channel, top : top + SUBS, (across - 1) * LANES :]
            if place:
                first = pltpu.roll(first, TILE * place, 1)
            if place != SUBS - 1:
                final = pltpu.roll(final, TILE * (place + 1), 1)
            at_left = jnp.where(lane_block == place, first, at_left)
            at_right = jnp.where(lane_block == place, final, at_right)
        send_a_ref[vector * SUBS : (vector + 1) * SUBS, :] = jnp.where(even, at_right, at_left)
        send_b_ref[vector * SUBS : (vector + 1) * SUBS, :] = jnp.where(even, at_left, at_right)


def lane_shift(block, shift, axis=1):
    shift %= block.shape[axis]
    return pltpu.roll(block, shift, axis) if shift else block


def strip_kernel(
    place_ref, got_a_in, got_b_in, image_ref, target_ref, side_ref, send_a_ref, send_b_ref,
    got_a_ref, got_b_ref, sems,
):
    copies = [
        pltpu.make_async_copy(got_a_in, got_a_ref, sems.at[0]),
        pltpu.make_async_copy(got_b_in, got_b_ref, sems.at[1]),
    ]
    for copy in copies:
        copy.start()
    for copy in copies:
        copy.wait()
    rows = image_ref.shape[1]
    cols = image_ref.shape[2]
    blocks = rows // SUBS
    lane_block = iota((SUBS, LANES), 1) // TILE
    even = place_ref[1] % 2 == 0
    for vector in range(6 * blocks // SUBS):
        got_a = got_a_ref[vector * SUBS : (vector + 1) * SUBS, :]
        got_b = got_b_ref[vector * SUBS : (vector + 1) * SUBS, :]
        from_right = jnp.where(even, got_a, got_b)
        from_left = jnp.where(even, got_b, got_a)
        for place in range(SUBS):
            number = vector * SUBS + place
            right = lane_shift(from_right, -TILE * place)
            left = lane_shift(from_left, -TILE * (place + 1))
            top = (number % blocks) * SUBS
            side_ref[number // blocks, top : top + SUBS, :] = jnp.where(
                lane_block == 0, right, jnp.where(lane_block == SUBS - 1, left, 0.0)
            )

    def packed(main, rest, shift):
        wide_sub = iota((SUBS, cols), 0) // 2
        side_sub = iota((SUBS, LANES), 0) // 2
        wides = []
        sides = []
        for number in range(6):
            source = image_ref if number < 3 else target_ref
            wides.append(source[number % 3, main : main + SUBS, :])
            sides.append(side_ref[number, main : main + SUBS, :])
        for first in (0, 4):
            wide = jnp.zeros((SUBS, cols), F32)
            side = jnp.zeros((SUBS, LANES), F32)
            for number in range(first, min(first + 4, 6)):
                source = image_ref if number < 3 else target_ref
                turn = 2 * (number - first) - shift
                block = lane_shift(source[number % 3, rest : rest + SUBS, :], turn, 0)
                wide = jnp.where(wide_sub == number - first, block, wide)
                block = lane_shift(side_ref[number, rest : rest + SUBS, :], turn, 0)
                side = jnp.where(side_sub == number - first, block, side)
            wides.append(wide)
            sides.append(side)
        lane_part = iota((SUBS, LANES), 1) // (2 * TILE)
        last = []
        for first in (0, 4):
            total = jnp.zeros((SUBS, LANES), F32)
            for part in range(4):
                moved = lane_shift(sides[first + part], TILE + 2 * TILE * part)
                total = jnp.where(lane_part == part, moved, total)
            last.append(total)
        return wides, last

    even_row = place_ref[0] % 2 == 0
    top, top_last = packed(0, SUBS, 0)
    bottom, bottom_last = packed(rows - SUBS, rows - 2 * SUBS, 6)
    for number in range(SUBS):
        here = slice(number * SUBS, (number + 1) * SUBS)
        send_a_ref[here, :] = jnp.where(even_row, bottom[number], top[number])
        send_b_ref[here, :] = jnp.where(even_row, top[number], bottom[number])
    for number in range(2):
        here = slice(number * LANES, (number + 1) * LANES)
        send_a_ref[SUBS * SUBS :, here] = jnp.where(even_row, bottom_last[number], top_last[number])
        send_b_ref[SUBS * SUBS :, here] = jnp.where(even_row, top_last[number], bottom_last[number])


def back_kernel(
    place_ref, got_a_in, got_b_in, image_ref, target_ref, side_ref, entry_ref, feat_ref,
    alpha_ref, weight_ref, down_ref, down_back_ref, across_ref, across_back_ref, mono_ref,
    out_ref,
    raw_ref, vert_ref, blur_ref, coef_ref, grad_ref, ahead_ref, pair_ref,
    right_ref, slope_ref, mask_ref, sum_ref, got_a_ref, got_b_ref, sems,
):
    rows = image_ref.shape[1]
    cols = image_ref.shape[2]
    wide = cols + LANES
    entries = entry_ref.shape[1]
    across = cols // LANES
    groups = (rows // TILE) * across
    length = entries // (groups * GROUP)
    tall = rows + 2 * HALO
    mid = rows + 2 * SUBS
    peers = out_ref.shape[0]
    half = LANES // 2

    got_copies = [
        pltpu.make_async_copy(got_a_in, got_a_ref, sems.at[0]),
        pltpu.make_async_copy(got_b_in, got_b_ref, sems.at[1]),
    ]
    for copy in got_copies:
        copy.start()
    for copy in got_copies:
        copy.wait()
    even_row = place_ref[0] % 2 == 0
    for number in range(6):
        source = image_ref if number < 3 else target_ref
        raw_ref[number, 0:rows, 0:cols] = source[number % 3]
        raw_ref[number, 0:rows, cols:] = side_ref[number]
    lane_block = iota((SUBS, LANES), 1) // TILE
    border = (lane_block == 0) | (lane_block == SUBS - 1)
    for below in (True, False):
        def got(rows_here, cols_here):
            got_a = got_a_ref[rows_here, cols_here]
            got_b = got_b_ref[rows_here, cols_here]
            return jnp.where(even_row, got_a, got_b) if below else jnp.where(even_row, got_b, got_a)

        main_at = rows if below else tall - SUBS
        rest_at = rows + SUBS if below else tall - 2 * SUBS
        goal = 0 if below else 3
        wide_keep = iota((SUBS, cols), 0) // 2 == goal
        side_keep = iota((SUBS, LANES), 0) // 2 == goal
        wides = [got(slice(number * SUBS, (number + 1) * SUBS), slice(0, cols)) for number in range(SUBS)]
        lasts = [
            got(slice(SUBS * SUBS, (SUBS + 1) * SUBS), slice(number * LANES, (number + 1) * LANES))
            for number in range(2)
        ]
        sides = [
            jnp.where(border, lane_shift(lasts[number // 4], -TILE - 2 * TILE * (number % 4)), 0.0)
            for number in range(SUBS)
        ]
        for number in range(6):
            raw_ref[number, main_at : main_at + SUBS, 0:cols] = wides[number]
            raw_ref[number, main_at : main_at + SUBS, cols:] = sides[number]
            turn = 2 * (goal - number % 4)
            block = lane_shift(wides[6 + number // 4], turn, 0)
            raw_ref[number, rest_at : rest_at + SUBS, 0:cols] = jnp.where(wide_keep, block, 0.0)
            block = lane_shift(sides[6 + number // 4], turn, 0)
            raw_ref[number, rest_at : rest_at + SUBS, cols:] = jnp.where(side_keep, block, 0.0)
    down = down_ref[...]
    for channel in range(3):
        shown = raw_ref[channel]
        wanted = raw_ref[3 + channel]
        for number, value in enumerate(
            [shown, wanted, shown * shown + wanted * wanted, shown * wanted]
        ):
            at = (channel * 4 + number) * mid
            vert_ref[at : at + mid, :] = dot_full(down, value)
    blur_ref[...] = dot_full(vert_ref[...], across_ref[...])
    line = iota((mid, wide), 0) - SUBS + place_ref[0] * rows
    spot = iota((mid, wide), 1)
    spot = jnp.where(spot < cols + half, spot, spot - wide) + place_ref[1] * cols
    inside = (
        (line >= 0) & (line < place_ref[2] * rows) & (spot >= 0) & (spot < place_ref[3] * cols)
    )
    down_back = down_back_ref[...]
    for channel in range(3):
        at = channel * 4 * mid
        mean_r, mean_t, squares, cross = [
            blur_ref[at + number * mid : at + (number + 1) * mid, :] for number in range(4)
        ]
        upper_one = 2.0 * mean_r * mean_t + STAB_ONE
        upper_two = 2.0 * (cross - mean_r * mean_t) + STAB_TWO
        lower_one = mean_r * mean_r + mean_t * mean_t + STAB_ONE
        lower_two = squares - mean_r * mean_r - mean_t * mean_t + STAB_TWO
        inv_one = 1.0 / lower_one
        inv_two = 1.0 / lower_two
        inverse = inv_one * inv_two
        value = upper_one * upper_two * inverse
        on_mean = (
            2.0 * mean_t * (upper_two - upper_one) * inverse
            + 2.0 * mean_r * value * (inv_two - inv_one)
        )
        on_square = -value * inv_two
        on_cross = 2.0 * upper_one * inverse
        for number, part in enumerate([on_mean, on_square, on_cross]):
            part = jnp.where(inside, -WEIGHT_SSIM * part, 0.0)
            spot_at = (channel * 3 + number) * rows
            high, rest = two_pieces(part)
            coef_ref[spot_at : spot_at + rows, :] = dot(
                down_back, jnp.concatenate([high, rest, high], axis=0)
            )
    high, rest = two_pieces(coef_ref[...])
    backs = dot(jnp.concatenate([high, rest, high], axis=1), across_back_ref[...])
    for channel in range(3):
        back = backs[channel * 3 * rows : (channel + 1) * 3 * rows]
        shown = image_ref[channel]
        wanted = target_ref[channel]
        gap = shown - wanted
        grad_ref[channel] = (
            (1.0 - WEIGHT_SSIM) * gap * lax.rsqrt(gap * gap + SMOOTHING * SMOOTHING)
            + back[0:rows]
            + 2.0 * shown * back[rows : 2 * rows]
            + wanted * back[2 * rows :]
        )

    pixels = TILE * TILE
    step_rows = length * GROUP
    mono = mono_ref[0 : 2 * SUBS, :]
    mono = jnp.concatenate([mono, mono], axis=1)
    same = iota((SUBS, step_rows), 0) == (iota((SUBS, step_rows), 1) & (GROUP - 1))
    slope_ref[...] = jnp.zeros(slope_ref.shape, F32)

    for group in range(groups):
        row = (group // across) * TILE
        col = (group % across) * LANES
        start = group * step_rows
        slopes = []
        for channel in range(3):
            for part in range(2):
                slopes.append(
                    block_transpose(
                        grad_ref[channel, row + part * SUBS : row + (part + 1) * SUBS, col : col + LANES]
                    )
                )
        slopes = jnp.concatenate(
            [jnp.concatenate(slopes[2 * channel : 2 * channel + 2], axis=1) for channel in range(3)],
            axis=0,
        )
        high, rest = [piece.astype(F32) for piece in two_pieces(slopes)]
        at = group * 6 * GROUP
        both = jnp.concatenate([high, rest], axis=0)
        right_ref[at : at + 6 * GROUP, 0:pixels] = both
        right_ref[at : at + 6 * GROUP, pixels:] = both
        top, low = [
            piece.astype(F32)
            for piece in two_pieces(spread_colours(feat_ref, start, step_rows))
        ]
        left = jnp.transpose(jnp.concatenate([top, low, top], axis=0)).astype(BF16)
        ahead_ref[start : start + step_rows, :] = dot(
            left, jnp.concatenate([high, high, rest], axis=0).astype(BF16)
        )

    def step(number, behinds):
        new_behinds = []
        at = (length // 2 - 1 - number) * 2 * GROUP
        for group in range(groups):
            source = pl.ds(pl.multiple_of(group * step_rows + at, 2 * GROUP), 2 * GROUP)
            alpha = alpha_ref[source, :]
            ahead = ahead_ref[source, :]
            weight = weight_ref[source, 0:pixels].astype(F32) + weight_ref[source, pixels:].astype(F32)
            behind = behinds[group]
            second = ahead[GROUP:] - behind
            behind = behind + alpha[GROUP:] * second
            first = ahead[0:GROUP] - behind
            new_behinds.append(behind + alpha[0:GROUP] * first)
            high, rest = two_pieces(weight * jnp.concatenate([first, second], axis=0))
            pair_ref[source, 0:pixels] = high
            pair_ref[source, pixels:] = rest
        return tuple(new_behinds)

    zero = jnp.zeros((GROUP, pixels), F32)
    lax.fori_loop(0, length // 2, step, tuple(zero for _ in range(groups)), unroll=4)

    for group in range(groups):
        here = slice(group * step_rows, (group + 1) * step_rows)
        at = group * 6 * GROUP
        moments = dot_nt(mono, pair_ref[here, :])
        tints = dot_nt(right_ref[at : at + 6 * GROUP, :].astype(BF16), weight_ref[here, :])
        on_xx = moments[0:1]
        on_xy = moments[1:2]
        on_yy = moments[2:3]
        on_x = moments[3:4]
        on_y = moments[4:5]
        on_one = moments[5:6]
        center_x = feat_ref[0:1, here]
        center_y = feat_ref[1:2, here]
        conic_xx = feat_ref[2:3, here]
        conic_xy = feat_ref[3:4, here]
        conic_yy = feat_ref[4:5, here]
        near_x = on_x - center_x * on_one
        near_y = on_y - center_y * on_one
        slope_ref[0:1, here] = conic_xx * near_x + conic_xy * near_y
        slope_ref[1:2, here] = conic_xy * near_x + conic_yy * near_y
        slope_ref[2:3, here] = -0.5 * (on_xx - center_x * (on_x + near_x))
        slope_ref[3:4, here] = -(on_xy - center_y * on_x - center_x * near_y)
        slope_ref[4:5, here] = -0.5 * (on_yy - center_y * (on_y + near_y))
        slope_ref[5:6, here] = on_one
        for channel in range(3):
            at = SUBS * channel
            both = tints[at : at + SUBS] + tints[at + 24 : at + 24 + SUBS]
            slope_ref[6 + channel : 7 + channel, here] = jnp.sum(
                jnp.where(same, both, 0.0), axis=0, keepdims=True
            )

    chunk = 512
    tops = peers * SUBS
    sum_ref[...] = jnp.zeros(sum_ref.shape, F32)
    pair_step = iota((2 * SUBS, chunk), 0) // SUBS

    def collect(index, part):
        start = pl.multiple_of(index * chunk, chunk)
        slot = entry_ref[:, pl.ds(start, chunk)]
        within = slot & (half - 1)
        owner = slot >> 6
        hot = jnp.where((iota((LANES, chunk), 0) & (half - 1)) == within, 1.0, 0.0).astype(BF16)
        values = [
            piece.astype(F32) for piece in two_pieces(slope_ref[0:SUBS, pl.ds(start, chunk)])
        ]
        values = [jnp.concatenate([value, value], axis=0) for value in values]
        offset = jnp.broadcast_to(owner, (2 * SUBS, chunk)) - pair_step
        for place in range(peers // 2):
            hit = offset == 2 * place
            for number in range(2):
                at = number * (tops + peers) + place * 2 * SUBS
                mask_ref[part, at : at + 2 * SUBS, :] = jnp.where(hit, values[number], 0.0).astype(BF16)
        hit = iota((peers, chunk), 0) == owner
        for number, piece in enumerate(
            two_pieces(slope_ref[SUBS : SUBS + 1, pl.ds(start, chunk)])
        ):
            at = number * (tops + peers) + tops
            mask_ref[part, at : at + peers, :] = jnp.where(hit, piece.astype(F32), 0.0).astype(BF16)
        return dot_nt(mask_ref[part], hot)

    def collect_some(index, carry):
        sum_ref[...] += sum(collect(UNROLL * index + part, part) for part in range(UNROLL))
        return carry

    lax.fori_loop(0, entries // (UNROLL * chunk), collect_some, 0)
    lane_low = iota((SUBS, LANES), 1) < half
    for place in range(peers):
        at = place * SUBS
        eight = sum_ref[at : at + SUBS, :] + sum_ref[tops + peers + at : tops + peers + at + SUBS, :]
        at = tops + place
        ninth = sum_ref[at : at + 1, :] + sum_ref[tops + peers + at : tops + peers + at + 1, :]
        out_ref[place] = jnp.where(lane_low, eight, jnp.broadcast_to(ninth, (SUBS, LANES)))


def return_kernel(
    place_ref, returned_ref, got_ref, jac_in, cam_ref, grad_out,
    row_ref, mask_ref, sum_ref, pack_ref, jac_ref, grad_ref, sems, jac_sems,
):
    jac_copy = pltpu.make_async_copy(jac_in, jac_ref, jac_sems.at[0])
    jac_copy.start()
    devices = got_ref.shape[0]
    count, own = grad_ref.shape
    high = own // LANES
    half = LANES // 2
    tops = high * SUBS
    part_rows = tops + high
    chunk = 4 * LANES
    cam = [[cam_ref[row, col] for col in range(3)] for row in range(3)]
    fill_numbers(place_ref, got_ref, row_ref)
    sum_ref[...] = jnp.zeros(sum_ref.shape, F32)
    lane_low = iota((SUBS, LANES), 1) < half
    pair_step = iota((2 * SUBS, chunk), 0) // SUBS

    def collect(index, part):
        numbers = row_ref[:, pl.ds(pl.multiple_of(index * chunk, chunk), chunk)]
        low = numbers & (LANES - 1)
        top = numbers >> 7
        hot = jnp.where(iota((LANES, chunk), 0) == low, 1.0, 0.0).astype(BF16)
        eights = []
        ninths = []
        for pair in range(chunk // LANES):
            first = returned_ref[index * 8 + 2 * pair]
            second = returned_ref[index * 8 + 2 * pair + 1]
            eights.append(jnp.where(lane_low, first, pltpu.roll(second, half, 1)))
            ninths.append(jnp.where(lane_low, pltpu.roll(first, half, 1), second)[0:1])
        values = [piece.astype(F32) for piece in two_pieces(jnp.concatenate(eights, axis=1))]
        values = [jnp.concatenate([value, value], axis=0) for value in values]
        offset = jnp.broadcast_to(top, (2 * SUBS, chunk)) - pair_step
        for place in range(high // 2):
            hit = offset == 2 * place
            for number in range(2):
                at = number * part_rows + place * 2 * SUBS
                mask_ref[part, at : at + 2 * SUBS, :] = jnp.where(hit, values[number], 0.0).astype(BF16)
        hit = iota((high, chunk), 0) == top
        for number, piece in enumerate(two_pieces(jnp.concatenate(ninths, axis=1))):
            at = number * part_rows + tops
            mask_ref[part, at : at + high, :] = jnp.where(hit, piece.astype(F32), 0.0).astype(BF16)
        return dot_nt(mask_ref[part], hot)

    def collect_some(index, carry):
        sum_ref[...] += sum(collect(UNROLL * index + part, part) for part in range(UNROLL))
        return carry

    lax.fori_loop(0, devices * half // (UNROLL * chunk), collect_some, 0)
    jac_copy.wait()

    def grad_copy(index):
        at = pl.ds(pl.multiple_of(index * SUBS * LANES, SUBS * LANES), SUBS * LANES)
        return pltpu.make_async_copy(grad_ref.at[:, at], grad_out.at[:, at], sems.at[index])

    def block(index, carry):
        start = pl.multiple_of(index * SUBS, SUBS)

        def jac(number):
            return jac_ref[pl.ds(number * high + start, SUBS), :]

        slopes = []
        for number in range(SUBS):
            at = start * SUBS + number
            slopes.append(
                sum_ref[pl.ds(at, SUBS, stride=SUBS), :]
                + sum_ref[pl.ds(part_rows + at, SUBS, stride=SUBS), :]
            )
        at = tops + start
        slopes.append(sum_ref[pl.ds(at, SUBS), :] + sum_ref[pl.ds(part_rows + at, SUBS), :])
        on_center = [slopes[0] * jac(30), slopes[1] * jac(31)]
        conic_xx = jac(48)
        conic_xy = jac(49)
        conic_yy = jac(50)
        on_xx, on_xy, on_yy = slopes[2:5]
        first_x = conic_xx * on_xx + conic_xy * on_xy
        first_y = conic_xy * on_xy + conic_yy * on_yy
        on_first = -(conic_xx * first_x + conic_xy * conic_xy * on_yy)
        on_second = -(conic_xy * conic_xy * on_xx + conic_yy * first_y)
        on_mixed = -(
            2.0 * conic_xx * conic_xy * on_xx
            + (conic_xx * conic_yy + conic_xy * conic_xy) * on_xy
            + 2.0 * conic_xy * conic_yy * on_yy
        )
        out = []
        for axis in range(3):
            out.append(
                cam[0][axis] * on_center[0]
                + cam[1][axis] * on_center[1]
                + slopes[6] * jac(21 + axis)
                + slopes[7] * jac(24 + axis)
                + slopes[8] * jac(27 + axis)
            )
        for number in range(7):
            out.append(
                on_first * jac(number) + on_mixed * jac(7 + number) + on_second * jac(14 + number)
            )
        out.append(slopes[5] * jac(32))
        for channel in range(3):
            out.append(SH_ZERO * slopes[6 + channel])
            for term in range(1, 16):
                out.append(slopes[6 + channel] * jac(32 + term))
        for number, value in enumerate(out):
            pack_ref[number * SUBS : (number + 1) * SUBS, :] = value
        for first in range(0, count, SUBS):
            number = min(SUBS, count - first)
            for place in range(SUBS):
                at = pl.ds(pl.multiple_of((start + place) * LANES, LANES), LANES)
                grad_ref[first : first + number, at] = pack_ref[
                    pl.ds(first * SUBS + place, number, stride=SUBS), :
                ]
        grad_copy(index).start()
        return carry

    lax.fori_loop(0, high // SUBS, block, 0)
    for index in range(high // SUBS):
        grad_copy(index).wait()


def band(outs, ins):
    taps = np.exp(-((np.arange(11) - 5.0) ** 2) / (2.0 * BLUR_SIGMA * BLUR_SIGMA))
    offset = np.asarray(ins)[None, :] - np.asarray(outs)[:, None]
    values = np.exp(-(offset**2) / (2.0 * BLUR_SIGMA * BLUR_SIGMA)) / taps.sum()
    return np.where(np.abs(offset) <= RIM, values, 0.0).astype(np.float32)


def band_pieces(values):
    high = values.astype(ml_dtypes.bfloat16)
    rest = (values - high.astype(np.float32)).astype(ml_dtypes.bfloat16)
    return [high, high, rest]


def monomials():
    pixel = np.arange(TILE * TILE)
    x = (pixel % TILE) - 7.5
    y = (pixel // TILE) - 7.5
    eight = np.stack([x * x, x * y, y * y, x, y, x * 0 + 1, x * 0, x * 0])
    return np.concatenate([eight, eight, eight, eight * 0]).astype(np.float32)


def call(body, out_shape, scratch, scalar_at, args, flops, vmem, outside=(), outs_outside=()):
    in_specs = [
        pl.BlockSpec(
            memory_space=pltpu.SMEM
            if number in scalar_at
            else pl.ANY
            if number in outside
            else pltpu.VMEM
        )
        for number in range(len(args))
    ]
    if isinstance(out_shape, tuple):
        out_specs = tuple(
            pl.BlockSpec(memory_space=pl.ANY if number in outs_outside else pltpu.VMEM)
            for number in range(len(out_shape))
        )
    else:
        out_specs = pl.BlockSpec(memory_space=pl.ANY if outs_outside else pltpu.VMEM)
    return pl.pallas_call(
        body,
        out_shape=out_shape,
        in_specs=in_specs,
        out_specs=out_specs,
        scratch_shapes=scratch,
        compiler_params=pltpu.CompilerParams(vmem_limit_bytes=vmem * MIB),
        cost_estimate=pl.CostEstimate(flops=flops, bytes_accessed=1 << 20, transcendentals=0),
    )(*args)


def swap_pairs(count, first):
    pairs = []
    for low in range(first, count - 1, 2):
        pairs += [(low, low + 1), (low + 1, low)]
    return pairs


def swap(value_a, value_b, axis):
    count = lax.axis_size(axis)
    got_b = lax.ppermute(value_b, axis, swap_pairs(count, 1))
    got_a = lax.ppermute(value_a, axis, swap_pairs(count, 0))
    return got_a, got_b


def exchange(payload):
    return lax.all_to_all(payload, ("img", "cell"), split_axis=0, concat_axis=0, tiled=True)


def shards(attributes, camera, target, visible_index, tile_lists, tile_len):
    img_count = lax.axis_size("img")
    cell_count = lax.axis_size("cell")
    devices = img_count * cell_count
    slots = visible_index.shape[1]
    count, own = attributes.shape
    high = own // LANES
    _, rows, cols = target.shape
    tiles_down, tiles_across, length = tile_lists.shape
    entries = tiles_down * tiles_across * length
    wide = cols + LANES
    mid = rows + 2 * SUBS
    tall = rows + 2 * HALO
    place = jnp.stack(
        [
            lax.axis_index("img"),
            lax.axis_index("cell"),
            jnp.int32(img_count),
            jnp.int32(cell_count),
        ]
    ).astype(jnp.int32)

    assert 2 * (slots // devices) == LANES
    asked = call(
        ask_kernel,
        jax.ShapeDtypeStruct((devices, LANES), jnp.int32),
        [],
        (),
        (visible_index,),
        1 << 14,
        2,
    )
    got = exchange(asked)

    table, jac = call(
        owner_kernel,
        (
            jax.ShapeDtypeStruct((high * (SUBS + 1), 2 * LANES), BF16),
            jax.ShapeDtypeStruct((JAC_ROWS * high, LANES), F32),
        ),
        [pltpu.VMEM((count * high, LANES), F32), pltpu.VMEM((high * (SUBS + 1), LANES), F32)],
        (1,),
        (attributes, camera),
        1 << 24,
        12,
    )
    reply = call(
        reply_kernel,
        jax.ShapeDtypeStruct((devices, SUBS, LANES), F32),
        [
            pltpu.VMEM((1, slots), jnp.int32),
            pltpu.VMEM((UNROLL, high * (SUBS + 1), 2 * LANES), F32),
            pltpu.VMEM((devices, LANES), jnp.int32),
            pltpu.SemaphoreType.DMA((1,)),
        ],
        (0,),
        (place, table, got),
        1 << 24,
        4 + slots // 128,
        outside=(2,),
    )
    arrived = exchange(reply)

    order = (tiles_down, tiles_across // GROUP, GROUP, length)
    entry = tile_lists.reshape(order).transpose(0, 1, 3, 2).reshape(1, entries)
    live = jnp.arange(length, dtype=jnp.int32)[None, None, :, None] < tile_len.reshape(
        tiles_down, tiles_across // GROUP, 1, GROUP
    )
    bias = jnp.where(live, 0.0, -1e30).astype(F32).reshape(1, entries)
    mono = jnp.asarray(monomials()).astype(BF16)
    packed = 6 * rows // SUBS
    pixels = TILE * TILE
    group_rows = length * GROUP
    groups = entries // group_rows
    strip = jax.ShapeDtypeStruct((packed, LANES), F32)
    image, feat, alpha, weight, send_a, send_b = call(
        render_kernel,
        (
            jax.ShapeDtypeStruct((3, rows, cols), F32),
            jax.ShapeDtypeStruct((2 * SUBS, entries), F32),
            jax.ShapeDtypeStruct((entries, pixels), F32),
            jax.ShapeDtypeStruct((entries, 2 * pixels), BF16),
            strip,
            strip,
        ),
        [
            pltpu.VMEM((UNROLL, devices * (SUBS + 1), 512), F32),
            pltpu.VMEM((UNROLL, 32, 512), F32),
            pltpu.VMEM((devices, SUBS, LANES), F32),
            pltpu.SemaphoreType.DMA((1,)),
        ],
        (0,),
        (place, arrived, entry, bias, target, mono),
        1 << 26,
        18 + devices // 6,
        outside=(1,),
    )
    got_a, got_b = swap(send_a, send_b, "cell")
    edge = jax.ShapeDtypeStruct(((SUBS + 1) * SUBS, cols), F32)
    side, send_a, send_b = call(
        strip_kernel,
        (jax.ShapeDtypeStruct((6, rows, LANES), F32), edge, edge),
        [
            pltpu.VMEM((packed, LANES), F32),
            pltpu.VMEM((packed, LANES), F32),
            pltpu.SemaphoreType.DMA((2,)),
        ],
        (0,),
        (place, got_a, got_b, image, target),
        1 << 20,
        4,
        outside=(1, 2),
    )
    got_a, got_b = swap(send_a, send_b, "img")

    tall_at = np.arange(tall)
    tall_at = np.where(tall_at < rows + HALO, tall_at, tall_at - tall)
    mid_at = np.arange(mid) - SUBS
    wide_at = np.arange(wide)
    wide_at = np.where(wide_at < cols + LANES // 2, wide_at, wide_at - wide)
    down = jnp.asarray(band(mid_at, tall_at))
    down_back = jnp.asarray(np.concatenate(band_pieces(band(np.arange(rows), mid_at)), axis=1))
    across = jnp.asarray(band(wide_at, wide_at))
    across_back = jnp.asarray(np.concatenate(band_pieces(band(wide_at, np.arange(cols))), axis=0))
    slot_grads = call(
        back_kernel,
        jax.ShapeDtypeStruct((devices, SUBS, LANES), F32),
        [
            pltpu.VMEM((6, tall, wide), F32),
            pltpu.VMEM((12 * mid, wide), F32),
            pltpu.VMEM((12 * mid, wide), F32),
            pltpu.VMEM((9 * rows, wide), F32),
            pltpu.VMEM((3, rows, cols), F32),
            pltpu.VMEM((entries, pixels), F32),
            pltpu.VMEM((entries, 2 * pixels), BF16),
            pltpu.VMEM((groups * 6 * GROUP, 2 * pixels), F32),
            pltpu.VMEM((2 * SUBS, entries), F32),
            pltpu.VMEM((UNROLL, 2 * devices * (SUBS + 1), 512), BF16),
            pltpu.VMEM((2 * devices * (SUBS + 1), LANES), F32),
            pltpu.VMEM(((SUBS + 1) * SUBS, cols), F32),
            pltpu.VMEM(((SUBS + 1) * SUBS, cols), F32),
            pltpu.SemaphoreType.DMA((2,)),
        ],
        (0,),
        (
            place, got_a, got_b, image, target, side, entry, feat, alpha, weight,
            down, down_back, across, across_back, mono,
        ),
        1 << 27,
        32 + devices // 8,
        outside=(1, 2),
    )
    returned = exchange(slot_grads)
    return call(
        return_kernel,
        jax.ShapeDtypeStruct((count, own), F32),
        [
            pltpu.VMEM((1, slots), jnp.int32),
            pltpu.VMEM((UNROLL, 2 * high * (SUBS + 1), 4 * LANES), BF16),
            pltpu.VMEM((2 * high * (SUBS + 1), LANES), F32),
            pltpu.VMEM((count * SUBS, LANES), F32),
            pltpu.VMEM((JAC_ROWS * high, LANES), F32),
            pltpu.VMEM((count, own), F32),
            pltpu.SemaphoreType.DMA((high // SUBS,)),
            pltpu.SemaphoreType.DMA((1,)),
        ],
        (0, 4),
        (place, returned, got, jac, camera),
        1 << 26,
        15,
        outside=(3,),
        outs_outside=(0,),
    )


def solution(mesh):
    return jax.shard_map(
        shards,
        mesh=mesh,
        in_specs=(
            P(None, ("img", "cell")),
            P(),
            P(None, "img", "cell"),
            P(("img", "cell"), None),
            P("img", "cell", None),
            P("img", "cell"),
        ),
        out_specs=P(None, ("img", "cell")),
        check_vma=False,
    )
```

```python
import jax
import jax.numpy as jnp
import ml_dtypes
import numpy as np
from jax import lax
from jax.experimental import pallas as pl
from jax.experimental.pallas import tpu as pltpu
from jax.sharding import PartitionSpec as P

TILE = 16
LANES = 128
SUBS = 8
GROUP = 8
RIM = 5
HALO = 16
WEIGHT_SSIM = 0.2
SMOOTHING = 0.01
STAB_ONE = 0.0001
STAB_TWO = 0.0009
BLUR_SIGMA = 1.5
LOG2E = 1.4426950408889634
SH_ZERO = 0.28209479177387814
SH_ONE = 0.4886025119029199
SH_TWO = (
    1.0925484305920792,
    -1.0925484305920792,
    0.31539156525252005,
    -1.0925484305920792,
    0.5462742152960396,
)
SH_THREE = (
    -0.5900435899266435,
    2.890611442640554,
    -0.4570457994644658,
    0.3731763325901154,
    -0.4570457994644658,
    1.445305721320277,
    -0.5900435899266435,
)
UNROLL = 4
F32 = jnp.float32
BF16 = jnp.bfloat16
JAC_ROWS = 51
MIB = 1024 * 1024


def harmonic_basis(unit_x, unit_y, unit_z):
    unit_xx = unit_x * unit_x
    unit_yy = unit_y * unit_y
    unit_zz = unit_z * unit_z
    return [
        -SH_ONE * unit_y,
        SH_ONE * unit_z,
        -SH_ONE * unit_x,
        SH_TWO[0] * unit_x * unit_y,
        SH_TWO[1] * unit_y * unit_z,
        SH_TWO[2] * (2.0 * unit_zz - unit_xx - unit_yy),
        SH_TWO[3] * unit_x * unit_z,
        SH_TWO[4] * (unit_xx - unit_yy),
        SH_THREE[0] * unit_y * (3.0 * unit_xx - unit_yy),
        SH_THREE[1] * unit_x * unit_y * unit_z,
        SH_THREE[2] * unit_y * (4.0 * unit_zz - unit_xx - unit_yy),
        SH_THREE[3] * unit_z * (2.0 * unit_zz - 3.0 * unit_xx - 3.0 * unit_yy),
        SH_THREE[4] * unit_x * (4.0 * unit_zz - unit_xx - unit_yy),
        SH_THREE[5] * unit_z * (unit_xx - unit_yy),
        SH_THREE[6] * unit_x * (unit_xx - 3.0 * unit_yy),
    ]


def three_pieces(value):
    first = value.astype(BF16)
    rest = value - first.astype(F32)
    second = rest.astype(BF16)
    third = (rest - second.astype(F32)).astype(BF16)
    return first, second, third


def two_pieces(value):
    first = value.astype(BF16)
    return first, (value - first.astype(F32)).astype(BF16)


def dot(left, right):
    return jnp.dot(left, right, preferred_element_type=F32)


def dot_nt(left, right):
    return lax.dot_general(left, right, (((1,), (1,)), ((), ())), preferred_element_type=F32)


def dot_full(left, right):
    return jnp.dot(left, right, preferred_element_type=F32, precision=lax.Precision.HIGHEST)


def iota(shape, dim):
    return lax.broadcasted_iota(jnp.int32, shape, dim)


def block_transpose(block):
    turn = (iota(block.shape, 0) - iota(block.shape, 1) // TILE) & (SUBS - 1)
    out = block
    for step in range(1, SUBS):
        moved = pltpu.roll(block, LANES - TILE * step, 1)
        moved = pltpu.roll(moved, step, 0)
        out = jnp.where(turn == step, moved, out)
    return out


def covariance(scale_rows, quat_rows, cam):
    scales = [jnp.exp(row) for row in scale_rows]
    quat_w = 1.5 + jnp.tanh(quat_rows[0])
    quat_x, quat_y, quat_z = quat_rows[1:]
    inverse = lax.rsqrt(quat_w * quat_w + quat_x * quat_x + quat_y * quat_y + quat_z * quat_z)
    quat_w, quat_x, quat_y, quat_z = (
        quat_w * inverse,
        quat_x * inverse,
        quat_y * inverse,
        quat_z * inverse,
    )
    rotation = [
        [
            1.0 - 2.0 * (quat_y * quat_y + quat_z * quat_z),
            2.0 * (quat_x * quat_y - quat_w * quat_z),
            2.0 * (quat_x * quat_z + quat_w * quat_y),
        ],
        [
            2.0 * (quat_x * quat_y + quat_w * quat_z),
            1.0 - 2.0 * (quat_x * quat_x + quat_z * quat_z),
            2.0 * (quat_y * quat_z - quat_w * quat_x),
        ],
        [
            2.0 * (quat_x * quat_z - quat_w * quat_y),
            2.0 * (quat_y * quat_z + quat_w * quat_x),
            1.0 - 2.0 * (quat_x * quat_x + quat_y * quat_y),
        ],
    ]
    axes = [
        [
            (
                cam[screen][0] * rotation[0][axis]
                + cam[screen][1] * rotation[1][axis]
                + cam[screen][2] * rotation[2][axis]
            )
            * scales[axis]
            for axis in range(3)
        ]
        for screen in range(2)
    ]
    first = axes[0][0] * axes[0][0] + axes[0][1] * axes[0][1] + axes[0][2] * axes[0][2] + 0.3
    mixed = axes[0][0] * axes[1][0] + axes[0][1] * axes[1][1] + axes[0][2] * axes[1][2]
    second = axes[1][0] * axes[1][0] + axes[1][1] * axes[1][1] + axes[1][2] * axes[1][2] + 0.3
    return first, mixed, second


def owner_kernel(attr_ref, cam_ref, table_ref, jac_ref, pack_ref, feat_ref):
    count, own = attr_ref.shape
    high = own // LANES
    cam = [[cam_ref[row, col] for col in range(3)] for row in range(3)]
    for first in range(0, count, SUBS):
        number = min(SUBS, count - first)
        for place in range(high):
            pack_ref[pl.ds(first * high + place, number, stride=high), :] = attr_ref[
                first : first + number, place * LANES : (place + 1) * LANES
            ]

    def block(index, carry):
        start = pl.multiple_of(index * SUBS, SUBS)

        def row(number):
            return pack_ref[pl.ds(number * high + start, SUBS), :]

        positions = [row(number) for number in range(3)]
        shape_rows = [row(3 + number) for number in range(7)]
        jac = []
        (cov_first, cov_mixed, cov_second), pull = jax.vjp(
            lambda *rows: covariance(rows[:3], rows[3:], cam), *shape_rows
        )
        one = jnp.ones_like(cov_first)
        zero = jnp.zeros_like(cov_first)
        jac += pull((one, zero, zero))
        jac += pull((zero, one, zero))
        jac += pull((zero, zero, one))
        inverse = 1.0 / (cov_first * cov_second - cov_mixed * cov_mixed)
        conic = [cov_second * inverse, -cov_mixed * inverse, cov_first * inverse]
        centers = []
        slopes = []
        for screen in range(2):
            angle = (
                cam[screen][0] * positions[0]
                + cam[screen][1] * positions[1]
                + cam[screen][2] * positions[2]
            ) / 3.0
            centers.append(7.0 * jnp.sin(angle))
            slopes.append((7.0 / 3.0) * jnp.cos(angle))
        raw = row(10)
        decay = jnp.exp(-raw)
        log_opacity = -jnp.log(1.0 + decay)
        harmonics = [[row(11 + 16 * channel + term) for term in range(16)] for channel in range(3)]

        def colours_of(pos_x, pos_y, pos_z):
            off_x = pos_x - cam[2][0]
            off_y = pos_y - cam[2][1]
            off_z = pos_z - cam[2][2]
            scale = lax.rsqrt(off_x * off_x + off_y * off_y + off_z * off_z)
            basis = harmonic_basis(off_x * scale, off_y * scale, off_z * scale)
            colours = []
            for channel in range(3):
                total = 0.5 + SH_ZERO * harmonics[channel][0]
                for term in range(1, 16):
                    total = total + basis[term - 1] * harmonics[channel][term]
                colours.append(total)
            return tuple(colours), basis

        colours, pull_colours, basis = jax.vjp(colours_of, *positions, has_aux=True)
        jac += pull_colours((one, zero, zero))
        jac += pull_colours((zero, one, zero))
        jac += pull_colours((zero, zero, one))
        jac += slopes
        jac.append(decay / (1.0 + decay))
        jac += basis
        jac += conic
        for number, value in enumerate(jac):
            jac_ref[pl.ds(number * high + start, SUBS), :] = value
        features = centers + conic + [log_opacity] + list(colours)
        for number in range(SUBS):
            feat_ref[pl.ds(start * SUBS + number, SUBS, stride=SUBS), :] = features[number]
        feat_ref[pl.ds(high * SUBS + start, SUBS), :] = features[SUBS]
        return carry

    lax.fori_loop(0, high // SUBS, block, 0)
    for number, piece in enumerate(two_pieces(feat_ref[...])):
        table_ref[:, number * LANES : (number + 1) * LANES] = piece


def ask_kernel(index_ref, out_ref):
    for pair in range(out_ref.shape[0] // 2):
        numbers = index_ref[:, pair * LANES : (pair + 1) * LANES]
        out_ref[2 * pair : 2 * pair + 2, :] = jnp.broadcast_to(numbers, (2, LANES))


def fill_numbers(place_ref, got_ref, row_ref):
    lane_low = iota((1, LANES), 1) < LANES // 2
    odd = (place_ref[0] * place_ref[3] + place_ref[1]) % 2 == 1
    for pair in range(got_ref.shape[0] // 2):
        first = got_ref[2 * pair : 2 * pair + 1, :]
        second = got_ref[2 * pair + 1 : 2 * pair + 2, :]
        row_ref[:, pair * LANES : (pair + 1) * LANES] = jnp.where(
            odd,
            jnp.where(lane_low, pltpu.roll(first, LANES // 2, 1), second),
            jnp.where(lane_low, first, pltpu.roll(second, LANES // 2, 1)),
        )


def reply_kernel(place_ref, table_ref, got_in, out_ref, row_ref, wide_ref, got_ref, sems):
    got_copy = pltpu.make_async_copy(got_in, got_ref, sems.at[0])
    got_copy.start()
    got_copy.wait()
    devices = got_ref.shape[0]
    high = table_ref.shape[0] // (SUBS + 1)
    chunk = 2 * LANES
    half = LANES // 2
    fill_numbers(place_ref, got_ref, row_ref)

    def look(index, slot):
        numbers = row_ref[:, pl.ds(pl.multiple_of(index * chunk, chunk), chunk)]
        low = numbers & (LANES - 1)
        top = numbers >> 7
        hot = jnp.where(iota((LANES, chunk), 0) == low, 1.0, 0.0).astype(BF16)
        wide_ref[slot] = dot(table_ref[...], jnp.concatenate([hot, hot], axis=0))
        return top

    def pick(index, slot, top):
        spread = jnp.broadcast_to(top, (SUBS, chunk))
        picked = jnp.zeros((SUBS, chunk), F32)
        for place in range(high):
            picked = jnp.where(
                spread == place, wide_ref[slot, place * SUBS : (place + 1) * SUBS, :], picked
            )
        last = jnp.sum(
            jnp.where(iota((high, chunk), 0) == top, wide_ref[slot, high * SUBS :, :], 0.0),
            axis=0,
            keepdims=True,
        )
        lane_low = iota((SUBS, LANES), 1) < half
        for part in range(chunk // LANES):
            eight = picked[:, part * LANES : (part + 1) * LANES]
            ninth = jnp.broadcast_to(last[:, part * LANES : (part + 1) * LANES], (SUBS, LANES))
            peer = index * 4 + part * 2
            out_ref[peer] = jnp.where(lane_low, eight, pltpu.roll(ninth, half, 1))
            out_ref[peer + 1] = jnp.where(lane_low, pltpu.roll(eight, half, 1), ninth)

    def step(index, carry):
        tops = [look(UNROLL * index + slot, slot) for slot in range(UNROLL)]
        for slot in range(UNROLL):
            pick(UNROLL * index + slot, slot, tops[slot])
        return carry

    lax.fori_loop(0, devices // (4 * UNROLL), step, 0)


def spread_colours(feat_ref, start, size):
    same = iota((GROUP, size), 0) == (iota((GROUP, size), 1) & (GROUP - 1))
    return jnp.concatenate(
        [
            jnp.where(same, feat_ref[6 + channel : 7 + channel, start : start + size], 0.0)
            for channel in range(3)
        ],
        axis=0,
    )


def render_kernel(
    place_ref, arrived_in, entry_ref, bias_ref, target_ref, mono_ref,
    image_ref, feat_ref, alpha_ref, weight_ref, send_a_ref, send_b_ref,
    wide_ref, coef_ref, arrived_ref, sems,
):
    arrived_copy = pltpu.make_async_copy(arrived_in, arrived_ref, sems.at[0])
    arrived_copy.start()
    arrived_copy.wait()
    peers = arrived_ref.shape[0]
    entries = entry_ref.shape[1]
    rows = image_ref.shape[1]
    across = image_ref.shape[2] // LANES
    groups = (rows // TILE) * across
    length = entries // (groups * GROUP)
    half = LANES // 2
    chunk = 512

    table = arrived_ref[...].reshape(peers * SUBS, LANES)
    ninth = arrived_ref[:, 0, :]
    low = iota((peers * SUBS, LANES), 1) < half
    low9 = iota((peers, LANES), 1) < half
    one, two, three = [piece.astype(F32) for piece in three_pieces(table)]
    one9, two9, three9 = [piece.astype(F32) for piece in three_pieces(ninth)]
    left = jnp.concatenate(
        [
            jnp.where(low, one, pltpu.roll(two, half, 1)),
            jnp.where(low9, pltpu.roll(two9, half, 1), one9),
        ],
        axis=0,
    ).astype(BF16)
    left_rest = jnp.concatenate(
        [jnp.where(low, three, 0.0), jnp.where(low9, 0.0, three9)], axis=0
    ).astype(BF16)
    left = jnp.concatenate([left, left_rest], axis=1)
    feat_ref[...] = jnp.zeros(feat_ref.shape, F32)
    coef_ref[...] = jnp.zeros(coef_ref.shape, F32)

    def look(index, slot_number):
        start = pl.multiple_of(index * chunk, chunk)
        slot = entry_ref[:, pl.ds(start, chunk)]
        within = slot & (half - 1)
        owner = slot >> 6
        hot = jnp.where((iota((LANES, chunk), 0) & (half - 1)) == within, 1.0, 0.0).astype(BF16)
        wide_ref[slot_number] = dot(left, jnp.concatenate([hot, hot], axis=0))
        return owner

    def gather(index, slot_number, owner):
        start = pl.multiple_of(index * chunk, chunk)
        spread = jnp.broadcast_to(owner, (SUBS, chunk))
        picked = jnp.zeros((SUBS, chunk), F32)
        for place in range(peers):
            picked = jnp.where(spread == place, wide_ref[slot_number, place * SUBS : (place + 1) * SUBS, :], picked)
        last = jnp.sum(
            jnp.where(iota((peers, chunk), 0) == owner, wide_ref[slot_number, peers * SUBS :, :], 0.0),
            axis=0,
            keepdims=True,
        )
        feat_ref[0:SUBS, pl.ds(start, chunk)] = picked
        feat_ref[SUBS : SUBS + 1, pl.ds(start, chunk)] = last
        center_x = picked[0:1]
        center_y = picked[1:2]
        conic_xx = picked[2:3]
        conic_xy = picked[3:4]
        conic_yy = picked[4:5]
        lin_x = conic_xx * center_x + conic_xy * center_y
        lin_y = conic_xy * center_x + conic_yy * center_y
        constant = picked[5:6] - 0.5 * (center_x * lin_x + center_y * lin_y)
        coef_ref[slot_number, 0:1] = (-0.5 * LOG2E) * conic_xx
        coef_ref[slot_number, 1:2] = -LOG2E * conic_xy
        coef_ref[slot_number, 2:3] = (-0.5 * LOG2E) * conic_yy
        coef_ref[slot_number, 3:4] = LOG2E * lin_x
        coef_ref[slot_number, 4:5] = LOG2E * lin_y
        coef_ref[slot_number, 5:6] = LOG2E * constant + bias_ref[:, pl.ds(start, chunk)]
        for number, piece in enumerate(three_pieces(coef_ref[slot_number, 0:SUBS])):
            coef_ref[slot_number, number * SUBS : (number + 1) * SUBS] = piece.astype(F32)
        columns = jnp.transpose(coef_ref[slot_number]).astype(BF16)
        alpha_ref[pl.ds(start, chunk), :] = jnp.exp2(dot(columns, mono_ref[...]))

    def gather_some(index, carry):
        owners = [look(UNROLL * index + number, number) for number in range(UNROLL)]
        for number in range(UNROLL):
            gather(UNROLL * index + number, number, owners[number])
        return carry

    lax.fori_loop(0, entries // (UNROLL * chunk), gather_some, 0)

    pixels = TILE * TILE
    step_rows = length * GROUP

    def scan(number, keeps):
        new_keeps = []
        for group in range(groups):
            at = pl.ds(
                pl.multiple_of(group * step_rows + number * 2 * GROUP, 2 * GROUP), 2 * GROUP
            )
            alpha = alpha_ref[at, :]
            first = keeps[group] * alpha[0:GROUP]
            keep = keeps[group] - first
            second = keep * alpha[GROUP:]
            new_keeps.append(keep - second)
            high, rest = two_pieces(jnp.concatenate([first, second], axis=0))
            weight_ref[at, 0:pixels] = high
            weight_ref[at, pixels:] = rest
        return tuple(new_keeps)

    keeps = tuple(jnp.ones((GROUP, pixels), F32) for _ in range(groups))
    lax.fori_loop(0, length // 2, scan, keeps, unroll=4)
    for group in range(groups):
        here = slice(group * step_rows, (group + 1) * step_rows)
        left = jnp.concatenate(
            two_pieces(spread_colours(feat_ref, group * step_rows, step_rows)), axis=0
        )
        sums = dot(left, weight_ref[here, 0:pixels]) + dot(left, weight_ref[here, pixels:])
        row = (group // across) * TILE
        col = (group % across) * LANES
        for channel in range(3):
            at = channel * GROUP
            total = sums[at : at + GROUP] + sums[at + 3 * GROUP : at + 4 * GROUP]
            for part in range(2):
                image_ref[
                    channel, row + part * SUBS : row + (part + 1) * SUBS, col : col + LANES
                ] = block_transpose(total[:, part * LANES : (part + 1) * LANES])

    blocks = rows // SUBS
    lane_block = iota((SUBS, LANES), 1) // TILE
    even = place_ref[1] % 2 == 0
    for vector in range(6 * blocks // SUBS):
        at_left = jnp.zeros((SUBS, LANES), F32)
        at_right = jnp.zeros((SUBS, LANES), F32)
        for place in range(SUBS):
            number = vector * SUBS + place
            source = image_ref if number // blocks < 3 else target_ref
            channel = (number // blocks) % 3
            top = (number % blocks) * SUBS
            first = source[channel, top : top + SUBS, 0:LANES]
            final = source[channel, top : top + SUBS, (across - 1) * LANES :]
            if place:
                first = pltpu.roll(first, TILE * place, 1)
            if place != SUBS - 1:
                final = pltpu.roll(final, TILE * (place + 1), 1)
            at_left = jnp.where(lane_block == place, first, at_left)
            at_right = jnp.where(lane_block == place, final, at_right)
        send_a_ref[vector * SUBS : (vector + 1) * SUBS, :] = jnp.where(even, at_right, at_left)
        send_b_ref[vector * SUBS : (vector + 1) * SUBS, :] = jnp.where(even, at_left, at_right)


def lane_shift(block, shift, axis=1):
    shift %= block.shape[axis]
    return pltpu.roll(block, shift, axis) if shift else block


def strip_kernel(
    place_ref, got_a_in, got_b_in, image_ref, target_ref, side_ref, send_a_ref, send_b_ref,
    got_a_ref, got_b_ref, sems,
):
    copies = [
        pltpu.make_async_copy(got_a_in, got_a_ref, sems.at[0]),
        pltpu.make_async_copy(got_b_in, got_b_ref, sems.at[1]),
    ]
    for copy in copies:
        copy.start()
    for copy in copies:
        copy.wait()
    rows = image_ref.shape[1]
    cols = image_ref.shape[2]
    blocks = rows // SUBS
    lane_block = iota((SUBS, LANES), 1) // TILE
    even = place_ref[1] % 2 == 0
    for vector in range(6 * blocks // SUBS):
        got_a = got_a_ref[vector * SUBS : (vector + 1) * SUBS, :]
        got_b = got_b_ref[vector * SUBS : (vector + 1) * SUBS, :]
        from_right = jnp.where(even, got_a, got_b)
        from_left = jnp.where(even, got_b, got_a)
        for place in range(SUBS):
            number = vector * SUBS + place
            right = lane_shift(from_right, -TILE * place)
            left = lane_shift(from_left, -TILE * (place + 1))
            top = (number % blocks) * SUBS
            side_ref[number // blocks, top : top + SUBS, :] = jnp.where(
                lane_block == 0, right, jnp.where(lane_block == SUBS - 1, left, 0.0)
            )

    def packed(main, rest, shift):
        wide_sub = iota((SUBS, cols), 0) // 2
        side_sub = iota((SUBS, LANES), 0) // 2
        wides = []
        sides = []
        for number in range(6):
            source = image_ref if number < 3 else target_ref
            wides.append(source[number % 3, main : main + SUBS, :])
            sides.append(side_ref[number, main : main + SUBS, :])
        for first in (0, 4):
            wide = jnp.zeros((SUBS, cols), F32)
            side = jnp.zeros((SUBS, LANES), F32)
            for number in range(first, min(first + 4, 6)):
                source = image_ref if number < 3 else target_ref
                turn = 2 * (number - first) - shift
                block = lane_shift(source[number % 3, rest : rest + SUBS, :], turn, 0)
                wide = jnp.where(wide_sub == number - first, block, wide)
                block = lane_shift(side_ref[number, rest : rest + SUBS, :], turn, 0)
                side = jnp.where(side_sub == number - first, block, side)
            wides.append(wide)
            sides.append(side)
        lane_part = iota((SUBS, LANES), 1) // (2 * TILE)
        last = []
        for first in (0, 4):
            total = jnp.zeros((SUBS, LANES), F32)
            for part in range(4):
                moved = lane_shift(sides[first + part], TILE + 2 * TILE * part)
                total = jnp.where(lane_part == part, moved, total)
            last.append(total)
        return wides, last

    even_row = place_ref[0] % 2 == 0
    top, top_last = packed(0, SUBS, 0)
    bottom, bottom_last = packed(rows - SUBS, rows - 2 * SUBS, 6)
    for number in range(SUBS):
        here = slice(number * SUBS, (number + 1) * SUBS)
        send_a_ref[here, :] = jnp.where(even_row, bottom[number], top[number])
        send_b_ref[here, :] = jnp.where(even_row, top[number], bottom[number])
    for number in range(2):
        here = slice(number * LANES, (number + 1) * LANES)
        send_a_ref[SUBS * SUBS :, here] = jnp.where(even_row, bottom_last[number], top_last[number])
        send_b_ref[SUBS * SUBS :, here] = jnp.where(even_row, top_last[number], bottom_last[number])


def back_kernel(
    place_ref, got_a_in, got_b_in, image_ref, target_ref, side_ref, entry_ref, feat_ref,
    alpha_ref, weight_ref, down_ref, down_back_ref, across_ref, across_back_ref, mono_ref,
    out_ref,
    raw_ref, vert_ref, blur_ref, coef_ref, grad_ref, ahead_ref, pair_ref,
    right_ref, slope_ref, mask_ref, sum_ref, got_a_ref, got_b_ref, sems,
):
    rows = image_ref.shape[1]
    cols = image_ref.shape[2]
    wide = cols + LANES
    entries = entry_ref.shape[1]
    across = cols // LANES
    groups = (rows // TILE) * across
    length = entries // (groups * GROUP)
    tall = rows + 2 * HALO
    mid = rows + 2 * SUBS
    peers = out_ref.shape[0]
    half = LANES // 2

    got_copies = [
        pltpu.make_async_copy(got_a_in, got_a_ref, sems.at[0]),
        pltpu.make_async_copy(got_b_in, got_b_ref, sems.at[1]),
    ]
    for copy in got_copies:
        copy.start()
    for copy in got_copies:
        copy.wait()
    even_row = place_ref[0] % 2 == 0
    for number in range(6):
        source = image_ref if number < 3 else target_ref
        raw_ref[number, 0:rows, 0:cols] = source[number % 3]
        raw_ref[number, 0:rows, cols:] = side_ref[number]
    lane_block = iota((SUBS, LANES), 1) // TILE
    border = (lane_block == 0) | (lane_block == SUBS - 1)
    for below in (True, False):
        def got(rows_here, cols_here):
            got_a = got_a_ref[rows_here, cols_here]
            got_b = got_b_ref[rows_here, cols_here]
            return jnp.where(even_row, got_a, got_b) if below else jnp.where(even_row, got_b, got_a)

        main_at = rows if below else tall - SUBS
        rest_at = rows + SUBS if below else tall - 2 * SUBS
        goal = 0 if below else 3
        wide_keep = iota((SUBS, cols), 0) // 2 == goal
        side_keep = iota((SUBS, LANES), 0) // 2 == goal
        wides = [got(slice(number * SUBS, (number + 1) * SUBS), slice(0, cols)) for number in range(SUBS)]
        lasts = [
            got(slice(SUBS * SUBS, (SUBS + 1) * SUBS), slice(number * LANES, (number + 1) * LANES))
            for number in range(2)
        ]
        sides = [
            jnp.where(border, lane_shift(lasts[number // 4], -TILE - 2 * TILE * (number % 4)), 0.0)
            for number in range(SUBS)
        ]
        for number in range(6):
            raw_ref[number, main_at : main_at + SUBS, 0:cols] = wides[number]
            raw_ref[number, main_at : main_at + SUBS, cols:] = sides[number]
            turn = 2 * (goal - number % 4)
            block = lane_shift(wides[6 + number // 4], turn, 0)
            raw_ref[number, rest_at : rest_at + SUBS, 0:cols] = jnp.where(wide_keep, block, 0.0)
            block = lane_shift(sides[6 + number // 4], turn, 0)
            raw_ref[number, rest_at : rest_at + SUBS, cols:] = jnp.where(side_keep, block, 0.0)
    down = down_ref[...]
    for channel in range(3):
        shown = raw_ref[channel]
        wanted = raw_ref[3 + channel]
        for number, value in enumerate(
            [shown, wanted, shown * shown + wanted * wanted, shown * wanted]
        ):
            at = (channel * 4 + number) * mid
            one, two, three = three_pieces(value)
            vert_ref[at : at + mid, :] = dot(
                down, jnp.concatenate([one, two, three, one, two, one], axis=0)
            )
    blur_ref[...] = dot_full(vert_ref[...], across_ref[...])
    line = iota((mid, wide), 0) - SUBS + place_ref[0] * rows
    spot = iota((mid, wide), 1)
    spot = jnp.where(spot < cols + half, spot, spot - wide) + place_ref[1] * cols
    inside = (
        (line >= 0) & (line < place_ref[2] * rows) & (spot >= 0) & (spot < place_ref[3] * cols)
    )
    down_back = down_back_ref[...]
    for channel in range(3):
        at = channel * 4 * mid
        mean_r, mean_t, squares, cross = [
            blur_ref[at + number * mid : at + (number + 1) * mid, :] for number in range(4)
        ]
        upper_one = 2.0 * mean_r * mean_t + STAB_ONE
        upper_two = 2.0 * (cross - mean_r * mean_t) + STAB_TWO
        lower_one = mean_r * mean_r + mean_t * mean_t + STAB_ONE
        lower_two = squares - mean_r * mean_r - mean_t * mean_t + STAB_TWO
        inv_one = 1.0 / lower_one
        inv_two = 1.0 / lower_two
        inverse = inv_one * inv_two
        value = upper_one * upper_two * inverse
        on_mean = (
            2.0 * mean_t * (upper_two - upper_one) * inverse
            + 2.0 * mean_r * value * (inv_two - inv_one)
        )
        on_square = -value * inv_two
        on_cross = 2.0 * upper_one * inverse
        for number, part in enumerate([on_mean, on_square, on_cross]):
            part = jnp.where(inside, -WEIGHT_SSIM * part, 0.0)
            spot_at = (channel * 3 + number) * rows
            high, rest = two_pieces(part)
            coef_ref[spot_at : spot_at + rows, :] = dot(
                down_back, jnp.concatenate([high, rest, high], axis=0)
            )
    high, rest = two_pieces(coef_ref[...])
    backs = dot(jnp.concatenate([high, rest, high], axis=1), across_back_ref[...])
    for channel in range(3):
        back = backs[channel * 3 * rows : (channel + 1) * 3 * rows]
        shown = image_ref[channel]
        wanted = target_ref[channel]
        gap = shown - wanted
        grad_ref[channel] = (
            (1.0 - WEIGHT_SSIM) * gap * lax.rsqrt(gap * gap + SMOOTHING * SMOOTHING)
            + back[0:rows]
            + 2.0 * shown * back[rows : 2 * rows]
            + wanted * back[2 * rows :]
        )

    pixels = TILE * TILE
    step_rows = length * GROUP
    mono = mono_ref[0 : 2 * SUBS, :]
    mono = jnp.concatenate([mono, mono], axis=1)
    same = iota((SUBS, step_rows), 0) == (iota((SUBS, step_rows), 1) & (GROUP - 1))
    slope_ref[...] = jnp.zeros(slope_ref.shape, F32)

    for group in range(groups):
        row = (group // across) * TILE
        col = (group % across) * LANES
        start = group * step_rows
        slopes = []
        for channel in range(3):
            for part in range(2):
                slopes.append(
                    block_transpose(
                        grad_ref[channel, row + part * SUBS : row + (part + 1) * SUBS, col : col + LANES]
                    )
                )
        slopes = jnp.concatenate(
            [jnp.concatenate(slopes[2 * channel : 2 * channel + 2], axis=1) for channel in range(3)],
            axis=0,
        )
        high, rest = [piece.astype(F32) for piece in two_pieces(slopes)]
        at = group * 6 * GROUP
        both = jnp.concatenate([high, rest], axis=0)
        right_ref[at : at + 6 * GROUP, 0:pixels] = both
        right_ref[at : at + 6 * GROUP, pixels:] = both
        top, low = [
            piece.astype(F32)
            for piece in two_pieces(spread_colours(feat_ref, start, step_rows))
        ]
        left = jnp.transpose(jnp.concatenate([top, low, top], axis=0)).astype(BF16)
        ahead_ref[start : start + step_rows, :] = dot(
            left, jnp.concatenate([high, high, rest], axis=0).astype(BF16)
        )

    def step(number, behinds):
        new_behinds = []
        at = (length // 2 - 1 - number) * 2 * GROUP
        for group in range(groups):
            source = pl.ds(pl.multiple_of(group * step_rows + at, 2 * GROUP), 2 * GROUP)
            alpha = alpha_ref[source, :]
            ahead = ahead_ref[source, :]
            weight = weight_ref[source, 0:pixels].astype(F32) + weight_ref[source, pixels:].astype(F32)
            behind = behinds[group]
            second = ahead[GROUP:] - behind
            behind = behind + alpha[GROUP:] * second
            first = ahead[0:GROUP] - behind
            new_behinds.append(behind + alpha[0:GROUP] * first)
            high, rest = two_pieces(weight * jnp.concatenate([first, second], axis=0))
            pair_ref[source, 0:pixels] = high
            pair_ref[source, pixels:] = rest
        return tuple(new_behinds)

    zero = jnp.zeros((GROUP, pixels), F32)
    lax.fori_loop(0, length // 2, step, tuple(zero for _ in range(groups)), unroll=4)

    for group in range(groups):
        here = slice(group * step_rows, (group + 1) * step_rows)
        at = group * 6 * GROUP
        moments = dot_nt(mono, pair_ref[here, :])
        tints = dot_nt(right_ref[at : at + 6 * GROUP, :].astype(BF16), weight_ref[here, :])
        on_xx = moments[0:1]
        on_xy = moments[1:2]
        on_yy = moments[2:3]
        on_x = moments[3:4]
        on_y = moments[4:5]
        on_one = moments[5:6]
        center_x = feat_ref[0:1, here]
        center_y = feat_ref[1:2, here]
        conic_xx = feat_ref[2:3, here]
        conic_xy = feat_ref[3:4, here]
        conic_yy = feat_ref[4:5, here]
        near_x = on_x - center_x * on_one
        near_y = on_y - center_y * on_one
        slope_ref[0:1, here] = conic_xx * near_x + conic_xy * near_y
        slope_ref[1:2, here] = conic_xy * near_x + conic_yy * near_y
        slope_ref[2:3, here] = -0.5 * (on_xx - center_x * (on_x + near_x))
        slope_ref[3:4, here] = -(on_xy - center_y * on_x - center_x * near_y)
        slope_ref[4:5, here] = -0.5 * (on_yy - center_y * (on_y + near_y))
        slope_ref[5:6, here] = on_one
        for channel in range(3):
            at = SUBS * channel
            both = tints[at : at + SUBS] + tints[at + 24 : at + 24 + SUBS]
            slope_ref[6 + channel : 7 + channel, here] = jnp.sum(
                jnp.where(same, both, 0.0), axis=0, keepdims=True
            )

    chunk = 512
    tops = peers * SUBS
    sum_ref[...] = jnp.zeros(sum_ref.shape, F32)
    pair_step = iota((2 * SUBS, chunk), 0) // SUBS

    def collect(index, part):
        start = pl.multiple_of(index * chunk, chunk)
        slot = entry_ref[:, pl.ds(start, chunk)]
        within = slot & (half - 1)
        owner = slot >> 6
        hot = jnp.where((iota((LANES, chunk), 0) & (half - 1)) == within, 1.0, 0.0).astype(BF16)
        values = [
            piece.astype(F32) for piece in two_pieces(slope_ref[0:SUBS, pl.ds(start, chunk)])
        ]
        values = [jnp.concatenate([value, value], axis=0) for value in values]
        offset = jnp.broadcast_to(owner, (2 * SUBS, chunk)) - pair_step
        for place in range(peers // 2):
            hit = offset == 2 * place
            for number in range(2):
                at = number * (tops + peers) + place * 2 * SUBS
                mask_ref[part, at : at + 2 * SUBS, :] = jnp.where(hit, values[number], 0.0).astype(BF16)
        hit = iota((peers, chunk), 0) == owner
        for number, piece in enumerate(
            two_pieces(slope_ref[SUBS : SUBS + 1, pl.ds(start, chunk)])
        ):
            at = number * (tops + peers) + tops
            mask_ref[part, at : at + peers, :] = jnp.where(hit, piece.astype(F32), 0.0).astype(BF16)
        return dot_nt(mask_ref[part], hot)

    def collect_some(index, carry):
        sum_ref[...] += sum(collect(UNROLL * index + part, part) for part in range(UNROLL))
        return carry

    lax.fori_loop(0, entries // (UNROLL * chunk), collect_some, 0)
    lane_low = iota((SUBS, LANES), 1) < half
    for place in range(peers):
        at = place * SUBS
        eight = sum_ref[at : at + SUBS, :] + sum_ref[tops + peers + at : tops + peers + at + SUBS, :]
        at = tops + place
        ninth = sum_ref[at : at + 1, :] + sum_ref[tops + peers + at : tops + peers + at + 1, :]
        out_ref[place] = jnp.where(lane_low, eight, jnp.broadcast_to(ninth, (SUBS, LANES)))


def return_kernel(
    place_ref, returned_ref, got_ref, jac_in, cam_ref, grad_out,
    row_ref, mask_ref, sum_ref, pack_ref, jac_ref, grad_ref, sems, jac_sems,
):
    jac_copy = pltpu.make_async_copy(jac_in, jac_ref, jac_sems.at[0])
    jac_copy.start()
    devices = got_ref.shape[0]
    count, own = grad_ref.shape
    high = own // LANES
    half = LANES // 2
    tops = high * SUBS
    part_rows = tops + high
    chunk = 4 * LANES
    cam = [[cam_ref[row, col] for col in range(3)] for row in range(3)]
    fill_numbers(place_ref, got_ref, row_ref)
    sum_ref[...] = jnp.zeros(sum_ref.shape, F32)
    lane_low = iota((SUBS, LANES), 1) < half
    pair_step = iota((2 * SUBS, chunk), 0) // SUBS

    def collect(index, part):
        numbers = row_ref[:, pl.ds(pl.multiple_of(index * chunk, chunk), chunk)]
        low = numbers & (LANES - 1)
        top = numbers >> 7
        hot = jnp.where(iota((LANES, chunk), 0) == low, 1.0, 0.0).astype(BF16)
        eights = []
        ninths = []
        for pair in range(chunk // LANES):
            first = returned_ref[index * 8 + 2 * pair]
            second = returned_ref[index * 8 + 2 * pair + 1]
            eights.append(jnp.where(lane_low, first, pltpu.roll(second, half, 1)))
            ninths.append(jnp.where(lane_low, pltpu.roll(first, half, 1), second)[0:1])
        values = [piece.astype(F32) for piece in two_pieces(jnp.concatenate(eights, axis=1))]
        values = [jnp.concatenate([value, value], axis=0) for value in values]
        offset = jnp.broadcast_to(top, (2 * SUBS, chunk)) - pair_step
        for place in range(high // 2):
            hit = offset == 2 * place
            for number in range(2):
                at = number * part_rows + place * 2 * SUBS
                mask_ref[part, at : at + 2 * SUBS, :] = jnp.where(hit, values[number], 0.0).astype(BF16)
        hit = iota((high, chunk), 0) == top
        for number, piece in enumerate(two_pieces(jnp.concatenate(ninths, axis=1))):
            at = number * part_rows + tops
            mask_ref[part, at : at + high, :] = jnp.where(hit, piece.astype(F32), 0.0).astype(BF16)
        return dot_nt(mask_ref[part], hot)

    def collect_some(index, carry):
        sum_ref[...] += sum(collect(UNROLL * index + part, part) for part in range(UNROLL))
        return carry

    lax.fori_loop(0, devices * half // (UNROLL * chunk), collect_some, 0)
    jac_copy.wait()

    def grad_copy(index):
        at = pl.ds(pl.multiple_of(index * SUBS * LANES, SUBS * LANES), SUBS * LANES)
        return pltpu.make_async_copy(grad_ref.at[:, at], grad_out.at[:, at], sems.at[index])

    def block(index, carry):
        start = pl.multiple_of(index * SUBS, SUBS)

        def jac(number):
            return jac_ref[pl.ds(number * high + start, SUBS), :]

        slopes = []
        for number in range(SUBS):
            at = start * SUBS + number
            slopes.append(
                sum_ref[pl.ds(at, SUBS, stride=SUBS), :]
                + sum_ref[pl.ds(part_rows + at, SUBS, stride=SUBS), :]
            )
        at = tops + start
        slopes.append(sum_ref[pl.ds(at, SUBS), :] + sum_ref[pl.ds(part_rows + at, SUBS), :])
        on_center = [slopes[0] * jac(30), slopes[1] * jac(31)]
        conic_xx = jac(48)
        conic_xy = jac(49)
        conic_yy = jac(50)
        on_xx, on_xy, on_yy = slopes[2:5]
        first_x = conic_xx * on_xx + conic_xy * on_xy
        first_y = conic_xy * on_xy + conic_yy * on_yy
        on_first = -(conic_xx * first_x + conic_xy * conic_xy * on_yy)
        on_second = -(conic_xy * conic_xy * on_xx + conic_yy * first_y)
        on_mixed = -(
            2.0 * conic_xx * conic_xy * on_xx
            + (conic_xx * conic_yy + conic_xy * conic_xy) * on_xy
            + 2.0 * conic_xy * conic_yy * on_yy
        )
        out = []
        for axis in range(3):
            out.append(
                cam[0][axis] * on_center[0]
                + cam[1][axis] * on_center[1]
                + slopes[6] * jac(21 + axis)
                + slopes[7] * jac(24 + axis)
                + slopes[8] * jac(27 + axis)
            )
        for number in range(7):
            out.append(
                on_first * jac(number) + on_mixed * jac(7 + number) + on_second * jac(14 + number)
            )
        out.append(slopes[5] * jac(32))
        for channel in range(3):
            out.append(SH_ZERO * slopes[6 + channel])
            for term in range(1, 16):
                out.append(slopes[6 + channel] * jac(32 + term))
        for number, value in enumerate(out):
            pack_ref[number * SUBS : (number + 1) * SUBS, :] = value
        for first in range(0, count, SUBS):
            number = min(SUBS, count - first)
            for place in range(SUBS):
                at = pl.ds(pl.multiple_of((start + place) * LANES, LANES), LANES)
                grad_ref[first : first + number, at] = pack_ref[
                    pl.ds(first * SUBS + place, number, stride=SUBS), :
                ]
        grad_copy(index).start()
        return carry

    lax.fori_loop(0, high // SUBS, block, 0)
    for index in range(high // SUBS):
        grad_copy(index).wait()


def band(outs, ins):
    taps = np.exp(-((np.arange(11) - 5.0) ** 2) / (2.0 * BLUR_SIGMA * BLUR_SIGMA))
    offset = np.asarray(ins)[None, :] - np.asarray(outs)[:, None]
    values = np.exp(-(offset**2) / (2.0 * BLUR_SIGMA * BLUR_SIGMA)) / taps.sum()
    return np.where(np.abs(offset) <= RIM, values, 0.0).astype(np.float32)


def band_pieces(values):
    high = values.astype(ml_dtypes.bfloat16)
    rest = (values - high.astype(np.float32)).astype(ml_dtypes.bfloat16)
    return [high, high, rest]


def band_six(values):
    one = values.astype(ml_dtypes.bfloat16)
    rest = values - one.astype(np.float32)
    two = rest.astype(ml_dtypes.bfloat16)
    three = (rest - two.astype(np.float32)).astype(ml_dtypes.bfloat16)
    return np.concatenate([one, one, one, two, two, three], axis=1)


def monomials():
    pixel = np.arange(TILE * TILE)
    x = (pixel % TILE) - 7.5
    y = (pixel // TILE) - 7.5
    eight = np.stack([x * x, x * y, y * y, x, y, x * 0 + 1, x * 0, x * 0])
    return np.concatenate([eight, eight, eight, eight * 0]).astype(np.float32)


def call(body, out_shape, scratch, scalar_at, args, flops, vmem, outside=(), outs_outside=()):
    in_specs = [
        pl.BlockSpec(
            memory_space=pltpu.SMEM
            if number in scalar_at
            else pl.ANY
            if number in outside
            else pltpu.VMEM
        )
        for number in range(len(args))
    ]
    if isinstance(out_shape, tuple):
        out_specs = tuple(
            pl.BlockSpec(memory_space=pl.ANY if number in outs_outside else pltpu.VMEM)
            for number in range(len(out_shape))
        )
    else:
        out_specs = pl.BlockSpec(memory_space=pl.ANY if outs_outside else pltpu.VMEM)
    return pl.pallas_call(
        body,
        out_shape=out_shape,
        in_specs=in_specs,
        out_specs=out_specs,
        scratch_shapes=scratch,
        compiler_params=pltpu.CompilerParams(vmem_limit_bytes=vmem * MIB),
        cost_estimate=pl.CostEstimate(flops=flops, bytes_accessed=1 << 20, transcendentals=0),
    )(*args)


def swap_pairs(count, first):
    pairs = []
    for low in range(first, count - 1, 2):
        pairs += [(low, low + 1), (low + 1, low)]
    return pairs


def swap(value_a, value_b, axis):
    count = lax.axis_size(axis)
    got_b = lax.ppermute(value_b, axis, swap_pairs(count, 1))
    got_a = lax.ppermute(value_a, axis, swap_pairs(count, 0))
    return got_a, got_b


def exchange(payload):
    return lax.all_to_all(payload, ("img", "cell"), split_axis=0, concat_axis=0, tiled=True)


def shards(attributes, camera, target, visible_index, tile_lists, tile_len):
    img_count = lax.axis_size("img")
    cell_count = lax.axis_size("cell")
    devices = img_count * cell_count
    slots = visible_index.shape[1]
    count, own = attributes.shape
    high = own // LANES
    _, rows, cols = target.shape
    tiles_down, tiles_across, length = tile_lists.shape
    entries = tiles_down * tiles_across * length
    wide = cols + LANES
    mid = rows + 2 * SUBS
    tall = rows + 2 * HALO
    place = jnp.stack(
        [
            lax.axis_index("img"),
            lax.axis_index("cell"),
            jnp.int32(img_count),
            jnp.int32(cell_count),
        ]
    ).astype(jnp.int32)

    assert 2 * (slots // devices) == LANES
    asked = call(
        ask_kernel,
        jax.ShapeDtypeStruct((devices, LANES), jnp.int32),
        [],
        (),
        (visible_index,),
        1 << 14,
        2,
    )
    got = exchange(asked)

    table, jac = call(
        owner_kernel,
        (
            jax.ShapeDtypeStruct((high * (SUBS + 1), 2 * LANES), BF16),
            jax.ShapeDtypeStruct((JAC_ROWS * high, LANES), F32),
        ),
        [pltpu.VMEM((count * high, LANES), F32), pltpu.VMEM((high * (SUBS + 1), LANES), F32)],
        (1,),
        (attributes, camera),
        1 << 24,
        12,
    )
    reply = call(
        reply_kernel,
        jax.ShapeDtypeStruct((devices, SUBS, LANES), F32),
        [
            pltpu.VMEM((1, slots), jnp.int32),
            pltpu.VMEM((UNROLL, high * (SUBS + 1), 2 * LANES), F32),
            pltpu.VMEM((devices, LANES), jnp.int32),
            pltpu.SemaphoreType.DMA((1,)),
        ],
        (0,),
        (place, table, got),
        1 << 24,
        4 + slots // 128,
        outside=(2,),
    )
    arrived = exchange(reply)

    order = (tiles_down, tiles_across // GROUP, GROUP, length)
    entry = tile_lists.reshape(order).transpose(0, 1, 3, 2).reshape(1, entries)
    live = jnp.arange(length, dtype=jnp.int32)[None, None, :, None] < tile_len.reshape(
        tiles_down, tiles_across // GROUP, 1, GROUP
    )
    bias = jnp.where(live, 0.0, -1e30).astype(F32).reshape(1, entries)
    mono = jnp.asarray(monomials()).astype(BF16)
    packed = 6 * rows // SUBS
    pixels = TILE * TILE
    group_rows = length * GROUP
    groups = entries // group_rows
    strip = jax.ShapeDtypeStruct((packed, LANES), F32)
    image, feat, alpha, weight, send_a, send_b = call(
        render_kernel,
        (
            jax.ShapeDtypeStruct((3, rows, cols), F32),
            jax.ShapeDtypeStruct((2 * SUBS, entries), F32),
            jax.ShapeDtypeStruct((entries, pixels), F32),
            jax.ShapeDtypeStruct((entries, 2 * pixels), BF16),
            strip,
            strip,
        ),
        [
            pltpu.VMEM((UNROLL, devices * (SUBS + 1), 512), F32),
            pltpu.VMEM((UNROLL, 32, 512), F32),
            pltpu.VMEM((devices, SUBS, LANES), F32),
            pltpu.SemaphoreType.DMA((1,)),
        ],
        (0,),
        (place, arrived, entry, bias, target, mono),
        1 << 26,
        18 + devices // 6,
        outside=(1,),
    )
    got_a, got_b = swap(send_a, send_b, "cell")
    edge = jax.ShapeDtypeStruct(((SUBS + 1) * SUBS, cols), F32)
    side, send_a, send_b = call(
        strip_kernel,
        (jax.ShapeDtypeStruct((6, rows, LANES), F32), edge, edge),
        [
            pltpu.VMEM((packed, LANES), F32),
            pltpu.VMEM((packed, LANES), F32),
            pltpu.SemaphoreType.DMA((2,)),
        ],
        (0,),
        (place, got_a, got_b, image, target),
        1 << 20,
        4,
        outside=(1, 2),
    )
    got_a, got_b = swap(send_a, send_b, "img")

    tall_at = np.arange(tall)
    tall_at = np.where(tall_at < rows + HALO, tall_at, tall_at - tall)
    mid_at = np.arange(mid) - SUBS
    wide_at = np.arange(wide)
    wide_at = np.where(wide_at < cols + LANES // 2, wide_at, wide_at - wide)
    down = jnp.asarray(band_six(band(mid_at, tall_at)))
    down_back = jnp.asarray(np.concatenate(band_pieces(band(np.arange(rows), mid_at)), axis=1))
    across = jnp.asarray(band(wide_at, wide_at))
    across_back = jnp.asarray(np.concatenate(band_pieces(band(wide_at, np.arange(cols))), axis=0))
    slot_grads = call(
        back_kernel,
        jax.ShapeDtypeStruct((devices, SUBS, LANES), F32),
        [
            pltpu.VMEM((6, tall, wide), F32),
            pltpu.VMEM((12 * mid, wide), F32),
            pltpu.VMEM((12 * mid, wide), F32),
            pltpu.VMEM((9 * rows, wide), F32),
            pltpu.VMEM((3, rows, cols), F32),
            pltpu.VMEM((entries, pixels), F32),
            pltpu.VMEM((entries, 2 * pixels), BF16),
            pltpu.VMEM((groups * 6 * GROUP, 2 * pixels), F32),
            pltpu.VMEM((2 * SUBS, entries), F32),
            pltpu.VMEM((UNROLL, 2 * devices * (SUBS + 1), 512), BF16),
            pltpu.VMEM((2 * devices * (SUBS + 1), LANES), F32),
            pltpu.VMEM(((SUBS + 1) * SUBS, cols), F32),
            pltpu.VMEM(((SUBS + 1) * SUBS, cols), F32),
            pltpu.SemaphoreType.DMA((2,)),
        ],
        (0,),
        (
            place, got_a, got_b, image, target, side, entry, feat, alpha, weight,
            down, down_back, across, across_back, mono,
        ),
        1 << 27,
        32 + devices // 8,
        outside=(1, 2),
    )
    returned = exchange(slot_grads)
    return call(
        return_kernel,
        jax.ShapeDtypeStruct((count, own), F32),
        [
            pltpu.VMEM((1, slots), jnp.int32),
            pltpu.VMEM((UNROLL, 2 * high * (SUBS + 1), 4 * LANES), BF16),
            pltpu.VMEM((2 * high * (SUBS + 1), LANES), F32),
            pltpu.VMEM((count * SUBS, LANES), F32),
            pltpu.VMEM((JAC_ROWS * high, LANES), F32),
            pltpu.VMEM((count, own), F32),
            pltpu.SemaphoreType.DMA((high // SUBS,)),
            pltpu.SemaphoreType.DMA((1,)),
        ],
        (0, 4),
        (place, returned, got, jac, camera),
        1 << 26,
        15,
        outside=(3,),
        outs_outside=(0,),
    )


def solution(mesh):
    return jax.shard_map(
        shards,
        mesh=mesh,
        in_specs=(
            P(None, ("img", "cell")),
            P(),
            P(None, "img", "cell"),
            P(("img", "cell"), None),
            P("img", "cell", None),
            P("img", "cell"),
        ),
        out_specs=P(None, ("img", "cell")),
        check_vma=False,
    )
```
